128 devices in a mesh: dp: 16 (over x, y_hi, core), seq: 8 (over y_lo, z).
Axes of the slice: x: 4, y: 4 (y_hi: 2, y_lo: 2; y = y_hi * 2 + y_lo), z: 4, core: 2. Of those that a mesh axis runs over, the one named last changes fastest.
Arguments:
- latents: bfloat16 [16, 8, 256, 1152], P('dp', 'seq'), may hold values from -6 to 6
- cotangent: bfloat16 [16, 8, 256, 1152], P('dp', 'seq'), may hold values from -6 to 6
- modulation: float32 [16, 2, 3, 1152], P('dp'), may hold values from -3 to 3
- qk_gains: float32 [2, 2, 72], replicated, may hold values from 0.6 to 2
- spatial_qkv: bfloat16 [1152, 1728], replicated, may hold values from -0.1875 to 0.1875
- spatial_out: bfloat16 [576, 1152], replicated, may hold values from -0.25 to 0.25
- temporal_qkv: bfloat16 [1152, 1728], replicated, may hold values from -0.1875 to 0.1875
- temporal_out: bfloat16 [576, 1152], replicated, may hold values from -0.25 to 0.25
Outputs:
- block_output: bfloat16 [16, 8, 256, 1152], P('dp', 'seq')
- latents_grad: bfloat16 [16, 8, 256, 1152], P('dp', 'seq')
- spatial_qkv_grad: float32 [1152, 1728], P(('dp', 'seq'))
- spatial_out_grad: float32 [576, 1152], P(None, ('dp', 'seq'))
- temporal_qkv_grad: float32 [1152, 1728], P(('dp', 'seq'))
- temporal_out_grad: float32 [576, 1152], P(None, ('dp', 'seq'))
The draws below stay inside these ranges and needn't reach their ends.
All inputs are finite; a program needn't handle non-finite values.
Results may differ from the reference program's by a relative error of at most 0.035.
Values may be sent and summed in bfloat16 or wider, within the bound.
No kernel may reach another device: no remote copies, remote signals or barrier semaphores. Data moves between devices by JAX's collectives and lax.ppermute only.
A program may use at most 192 MiB of HBM per device.

```python
import math
import jax
import jax.numpy as jnp
from jax import lax

D = 1152
HEAD_DIM = 72
HEADS = 8
PATCHES = 256
FRAMES = 8
CLIPS = 16


def levels(stream_key, shape, split, smallest, top_value):
    factor_of = 1.0
    for dim, blocks in split:
        heights = jax.random.uniform(jax.random.fold_in(jax.random.fold_in(stream_key, 6), dim), (blocks,), jnp.float32, smallest / len(split), top_value / len(split))
        factor_of = factor_of * jnp.repeat(jnp.exp(heights), shape[dim] // blocks).reshape((-1,) + (1,) * (len(shape) - 1 - dim))
    return factor_of


def normal_values(own_key, extent, scale, most, shards=(), kind=jnp.bfloat16):
    array = scale * jax.random.normal(own_key, extent, jnp.float32)
    if shards:
        array = array * levels(own_key, extent, shards, -0.22, 0.18)
    return jnp.clip(array, -most, most).astype(kind)


def setup_inputs(seed: int = 0) -> dict:
    key_of = jax.random.split(jax.random.key(seed), 9)
    latents = normal_values(key_of[0], (CLIPS, FRAMES, PATCHES, D), 1.0, 6.0, ((0, 16), (1, 8)))
    cotangent = normal_values(key_of[1], (CLIPS, FRAMES, PATCHES, D), 1.0, 6.0, ((0, 16), (1, 8)))
    modulation = normal_values(key_of[2], (CLIPS, 2, 3, D), 0.5, 3.0, ((0, 16),), jnp.float32)
    qk_gains = jnp.clip(jnp.exp(jax.random.uniform(key_of[3], (2, 2, HEAD_DIM), jnp.float32, math.log(0.6), math.log(2.0))), 0.6, 2.0)
    spatial_qkv = normal_values(key_of[4], (D, 3 * HEADS * HEAD_DIM), D ** -0.5, 0.1875)
    spatial_out = normal_values(key_of[5], (HEADS * HEAD_DIM, D), (HEADS * HEAD_DIM) ** -0.5, 0.25)
    temporal_qkv = normal_values(key_of[6], (D, 3 * HEADS * HEAD_DIM), D ** -0.5, 0.1875)
    temporal_out = normal_values(key_of[7], (HEADS * HEAD_DIM, D), (HEADS * HEAD_DIM) ** -0.5, 0.25)
    return {"latents": latents, "cotangent": cotangent, "modulation": modulation, "qk_gains": qk_gains, "spatial_qkv": spatial_qkv, "spatial_out": spatial_out, "temporal_qkv": temporal_qkv, "temporal_out": temporal_out}


EPS = 1e-06

def modulate(x32, shift, scale):
    mean = lax.optimization_barrier(jnp.mean(x32, axis=-1, keepdims=True))
    centered = x32 - mean
    variance = lax.optimization_barrier(jnp.mean(centered * centered, axis=-1, keepdims=True))
    return (centered * lax.rsqrt(variance + EPS) * (1.0 + scale) + shift).astype(jnp.bfloat16)

def head_norm(part, gain):
    wide = part.astype(jnp.float32)
    square = lax.optimization_barrier(jnp.mean(wide * wide, axis=-1, keepdims=True))
    return (wide * lax.rsqrt(square + EPS) * gain).astype(jnp.bfloat16)

def attend(qkv, gains, frames_first):
    leading = qkv.shape[:-1]
    parts = qkv.reshape(leading + (3, HEADS, HEAD_DIM))
    query = head_norm(parts[..., 0, :, :], gains[0])
    keys = head_norm(parts[..., 1, :, :], gains[1])
    values = parts[..., 2, :, :]
    if frames_first:
        scores = jnp.einsum('lbhd,mbhd->bhlm', query, keys, preferred_element_type=jnp.float32)
    else:
        scores = jnp.einsum('blhd,bmhd->bhlm', query, keys, preferred_element_type=jnp.float32)
    scores = scores * HEAD_DIM ** (-0.5)
    highest = lax.optimization_barrier(jnp.max(scores, axis=-1, keepdims=True))
    expo = jnp.exp(scores - highest)
    probs = (expo / lax.optimization_barrier(jnp.sum(expo, axis=-1, keepdims=True))).astype(jnp.bfloat16)
    if frames_first:
        result = jnp.einsum('bhlm,mbhd->lbhd', probs, values, preferred_element_type=jnp.float32)
    else:
        result = jnp.einsum('bhlm,bmhd->blhd', probs, values, preferred_element_type=jnp.float32)
    return result.astype(jnp.bfloat16).reshape(leading + (HEADS * HEAD_DIM,))

def outer_sum(left, right):
    flat_left = left.reshape(-1, left.shape[-1])
    flat_right = right.reshape(-1, right.shape[-1])
    return lax.dot_general(flat_left, flat_right, (((0,), (0,)), ((), ())), preferred_element_type=jnp.float32)

def times_t(left, weight):
    return lax.dot_general(left, weight, (((left.ndim - 1,), (1,)), ((), ())), preferred_element_type=jnp.float32)

def clip_pass(latents, cotangent, modulation, qk_gains, spatial_qkv, spatial_out, temporal_qkv, temporal_out):
    x32 = latents.astype(jnp.float32)
    normed_s = modulate(x32, modulation[0, 0], modulation[0, 1])
    qkv_s = jnp.dot(normed_s, spatial_qkv, preferred_element_type=jnp.float32).astype(jnp.bfloat16)
    att_s, back_s = jax.vjp(lambda t: attend(t, qk_gains[0], False), qkv_s)
    middle = (x32 + modulation[0, 2] * jnp.dot(att_s, spatial_out, preferred_element_type=jnp.float32)).astype(jnp.bfloat16)
    mid32 = middle.astype(jnp.float32)
    normed_t = modulate(mid32, modulation[1, 0], modulation[1, 1])
    qkv_t = jnp.dot(normed_t, temporal_qkv, preferred_element_type=jnp.float32).astype(jnp.bfloat16)
    att_t, back_t = jax.vjp(lambda t: attend(t, qk_gains[1], True), qkv_t)
    output = (mid32 + modulation[1, 2] * jnp.dot(att_t, temporal_out, preferred_element_type=jnp.float32)).astype(jnp.bfloat16)
    cot32 = cotangent.astype(jnp.float32)
    scaled_t = (modulation[1, 2] * cot32).astype(jnp.bfloat16)
    grad_t_out = outer_sum(att_t, scaled_t)
    att_grad_t = times_t(scaled_t, temporal_out).astype(jnp.bfloat16)
    qkv_grad_t = back_t(att_grad_t)[0]
    grad_t_qkv = outer_sum(normed_t, qkv_grad_t)
    normed_grad_t = times_t(qkv_grad_t, temporal_qkv).astype(jnp.bfloat16)
    pre_back_t = jax.vjp(lambda v: modulate(v, modulation[1, 0], modulation[1, 1]), mid32)[1]
    middle_grad = (cot32 + pre_back_t(normed_grad_t)[0]).astype(jnp.bfloat16)
    mg32 = middle_grad.astype(jnp.float32)
    scaled_s = (modulation[0, 2] * mg32).astype(jnp.bfloat16)
    grad_s_out = outer_sum(att_s, scaled_s)
    att_grad_s = times_t(scaled_s, spatial_out).astype(jnp.bfloat16)
    qkv_grad_s = back_s(att_grad_s)[0]
    grad_s_qkv = outer_sum(normed_s, qkv_grad_s)
    normed_grad_s = times_t(qkv_grad_s, spatial_qkv).astype(jnp.bfloat16)
    pre_back_s = jax.vjp(lambda v: modulate(v, modulation[0, 0], modulation[0, 1]), x32)[1]
    latents_grad = (mg32 + pre_back_s(normed_grad_s)[0]).astype(jnp.bfloat16)
    return (output, latents_grad, grad_s_qkv, grad_s_out, grad_t_qkv, grad_t_out)

def reference(latents, cotangent, modulation, qk_gains, spatial_qkv, spatial_out, temporal_qkv, temporal_out):

    def one_clip(items):
        return clip_pass(items[0], items[1], items[2], qk_gains, spatial_qkv, spatial_out, temporal_qkv, temporal_out)
    output, latents_grad, gsq, gso, gtq, gto = lax.map(one_clip, (latents, cotangent, modulation))
    return (output, latents_grad, lax.optimization_barrier(jnp.sum(gsq, axis=0)), lax.optimization_barrier(jnp.sum(gso, axis=0)), lax.optimization_barrier(jnp.sum(gtq, axis=0)), lax.optimization_barrier(jnp.sum(gto, axis=0)))
```

```python
import jax
import jax.numpy as jnp
from jax import lax
from jax.experimental import pallas as pl
from jax.experimental.pallas import tpu as pltpu
from jax.sharding import PartitionSpec as P

T = 256
D = 1152
HEADS = 8
HEAD_DIM = 72
A = HEADS * HEAD_DIM
Q = 3 * A
A_PAD = 640
Q_PAD = 1792
LOCAL = 32
EPS = 1e-06
BF = jnp.bfloat16
F32 = jnp.float32
MESH = ("dp", "seq")
VMEM_LIMIT = 48 * 1024 * 1024


def dot(left, right, over_left, over_right):
    return lax.dot_general(
        left, right, (((over_left,), (over_right,)), ((), ())), preferred_element_type=F32
    )


def call(body, outs, args, flops, scratch=()):
    shapes = tuple(jax.ShapeDtypeStruct(shape, kind) for shape, kind in outs)
    size = sum(x.size * x.dtype.itemsize for x in args)
    size += sum(x.size * x.dtype.itemsize for x in shapes)
    return pl.pallas_call(
        body,
        out_shape=shapes,
        in_specs=[pl.BlockSpec(memory_space=pltpu.VMEM)] * len(args),
        out_specs=tuple(pl.BlockSpec(memory_space=pltpu.VMEM) for _ in shapes),
        scratch_shapes=list(scratch),
        cost_estimate=pl.CostEstimate(flops=flops, bytes_accessed=size, transcendentals=0),
        compiler_params=pltpu.CompilerParams(vmem_limit_bytes=VMEM_LIMIT),
    )(*args)


def normalized(x32):
    mean = jnp.mean(x32, axis=-1, keepdims=True)
    centered = x32 - mean
    spread = lax.rsqrt(jnp.mean(centered * centered, axis=-1, keepdims=True) + EPS)
    return centered * spread, spread


def normalized_back(unit, spread, scale, grad):
    grad = grad * (1.0 + scale)
    inner = jnp.mean(grad * unit, axis=-1, keepdims=True)
    return spread * (grad - jnp.mean(grad, axis=-1, keepdims=True) - unit * inner)


def flip(source, target, blocks):
    for b in range(blocks):
        target[128 * b : 128 * b + 128, :] = source[:, 128 * b : 128 * b + 128].T


def flip_back(source, target, blocks):
    for b in range(blocks):
        target[:, 128 * b : 128 * b + 128] = source[128 * b : 128 * b + 128, :].T


def head_rows(which, h):
    start = which * A + h * HEAD_DIM
    return slice(start, start + HEAD_DIM)


def head_norm(rows, gain):
    root = lax.rsqrt(jnp.mean(rows * rows, axis=0, keepdims=True) + EPS)
    return root, (rows * root * gain).astype(BF)


def head_norm_back(rows, root, gain, grad):
    grad = grad.astype(BF).astype(F32) * gain
    inner = jnp.mean(rows * grad, axis=0, keepdims=True)
    return (root * grad - rows * (root * root * root * inner)).astype(BF).astype(F32)


def same_patch():
    key = lax.broadcasted_iota(jnp.int32, (T, T), 0)
    query = lax.broadcasted_iota(jnp.int32, (T, T), 1)
    return ((key ^ query) & (LOCAL - 1)) == 0


def head_probs(queries, keys, mask):
    scores = dot(keys, queries, 0, 0) * HEAD_DIM ** (-0.5)
    if mask is not None:
        scores = jnp.where(mask, scores, -1e30)
    expo = jnp.exp(scores - jnp.max(scores, axis=0, keepdims=True))
    return expo * (1.0 / jnp.sum(expo, axis=0, keepdims=True))


def head_back(q_rows, k_rows, v_rows, gains, probs, grad):
    q_root, queries = head_norm(q_rows, gains[0])
    k_root, keys = head_norm(k_rows, gains[1])
    grad = grad.astype(BF)
    probs16 = probs.astype(BF)
    v_grad = dot(grad, probs16, 1, 1).astype(BF).astype(F32)
    p_grad = dot(v_rows.astype(BF), grad, 0, 0).astype(BF).astype(F32)
    inner = jnp.sum(p_grad * probs, axis=0, keepdims=True)
    s_grad = (probs * (p_grad - inner) * HEAD_DIM ** (-0.5)).astype(BF)
    q_grad = head_norm_back(q_rows, q_root, gains[0], dot(keys, s_grad, 1, 0))
    k_grad = head_norm_back(k_rows, k_root, gains[1], dot(queries, s_grad, 1, 1))
    return q_grad, k_grad, v_grad


def order(core, chip):
    row = lax.broadcasted_iota(jnp.int32, (1, A), 1)
    part = (row >= 192).astype(jnp.int32) + (row >= 384).astype(jnp.int32)
    rest = row - 192 * part
    first = (rest * 171) >> 12
    rest = rest - 24 * first
    second = (rest * 11) >> 5
    piece = 3 * part + rest - 3 * second
    place = []
    for axis in range(3):
        step = axis - part
        step = jnp.where(step < 0, step + 3, step)
        one = jnp.where(step == 0, first >> 2, jnp.where(step == 1, first >> 1, first)) & 1
        two = (second >> (2 - axis)) & 1
        near = jnp.where(core == 0, one, two) ^ ((chip[axis] ^ (chip[axis] >> 1)) & 1)
        far = jnp.where(core == 0, two, one) ^ (chip[axis] >> 1)
        place.append(2 * far + (near ^ far))
    x, y, z = place
    device = x * 32 + (y >> 1) * 16 + core * 8 + (y & 1) * 4 + z
    return 9 * device + piece


def position():
    dp, seq = lax.axis_index("dp"), lax.axis_index("seq")
    return dp & 1, (dp >> 2, ((dp >> 1) & 1) * 2 + (seq >> 2), seq & 3)


def picker(core, chip):
    feature = lax.broadcasted_iota(jnp.int32, (D, A), 0)
    return (feature == order(core, chip)).astype(F32).astype(BF)


def pickers():
    core, chip = position()
    return picker(core, chip), picker(1 - core, chip)


def forward_spatial(
    latents, cot, mod, gains, w_qkv, w_out, w_out_t,
    both, qkv_t, probs_t, normed, att, scaled_t, wide, flat, tall
):
    scaled = (mod[5:6, :] * cot[...].astype(F32)).astype(BF)
    scaled_t[...] = scaled
    both[:, D:] = dot(scaled, w_out_t[...], 1, 1).astype(BF)
    unit, _ = normalized(latents[...].astype(F32))
    norm = (unit * (1.0 + mod[1:2, :]) + mod[0:1, :]).astype(BF)
    normed[...] = norm
    wide[:, Q:] = jnp.zeros((T, Q_PAD - Q), F32)
    wide[:, :Q] = dot(norm, w_qkv[...], 1, 0).astype(BF).astype(F32)
    flip(wide, qkv_t, Q_PAD // 128)
    tall[A:, :] = jnp.zeros((A_PAD - A, T), F32)
    for h in range(HEADS):
        queries = head_norm(qkv_t[head_rows(0, h), :], gains[:, 0:1])[1]
        keys = head_norm(qkv_t[head_rows(1, h), :], gains[:, 1:2])[1]
        probs = head_probs(queries, keys, None)
        probs_t[h] = probs
        values = qkv_t[head_rows(2, h), :].astype(BF)
        tall[head_rows(0, h), :] = dot(values, probs.astype(BF), 1, 0)
    flip_back(tall, flat, A_PAD // 128)
    att16 = flat[:, :A].astype(BF)
    att[...] = att16
    result = dot(att16, w_out[...], 1, 0)
    both[:, :D] = (latents[...].astype(F32) + mod[2:3, :] * result).astype(BF)


def temporal(
    both, mod, gains, w_qkv, back, normed, qkv_grad, wide, tall_qkv, tall_grad, flat, tall, tall_att
):
    unit, _ = normalized(both[:, :D].astype(F32))
    norm = (unit * (1.0 + mod[4:5, :]) + mod[3:4, :]).astype(BF)
    normed[...] = norm
    wide[:, Q:] = jnp.zeros((T, Q_PAD - Q), F32)
    wide[:, :Q] = dot(norm, w_qkv[...], 1, 0).astype(BF).astype(F32)
    flip(wide, tall_qkv, Q_PAD // 128)
    flat[:, A:] = jnp.zeros((T, A_PAD - A), F32)
    flat[:, :A] = both[:, D:].astype(F32)
    flip(flat, tall, A_PAD // 128)
    tall_att[A:, :] = jnp.zeros((A_PAD - A, T), F32)
    tall_grad[Q:, :] = jnp.zeros((Q_PAD - Q, T), F32)
    mask = same_patch()
    pair = (gains[:, 0:1], gains[:, 1:2])
    for h in range(HEADS):
        q_rows = tall_qkv[head_rows(0, h), :]
        k_rows = tall_qkv[head_rows(1, h), :]
        v_rows = tall_qkv[head_rows(2, h), :]
        probs = head_probs(head_norm(q_rows, pair[0])[1], head_norm(k_rows, pair[1])[1], mask)
        tall_att[head_rows(0, h), :] = dot(v_rows.astype(BF), probs.astype(BF), 1, 0)
        grads = head_back(q_rows, k_rows, v_rows, pair, probs, tall[head_rows(0, h), :])
        for which in range(3):
            tall_grad[head_rows(which, h), :] = grads[which]
    flip_back(tall_att, flat, A_PAD // 128)
    back[:, D:] = flat[:, :A].astype(BF)
    flip_back(tall_grad, wide, Q_PAD // 128)
    grad = wide[:, :Q].astype(BF)
    qkv_grad[...] = grad
    back[:, :D] = dot(grad, w_qkv[...], 1, 1).astype(BF)


def pick_two(first, second, mine, theirs):
    own, other = pickers()
    for k, source in enumerate((first, second)):
        mine[:, k * A : k * A + A] = dot(source[...], own, 1, 0).astype(BF)
        theirs[:, k * A : k * A + A] = dot(source[...], other, 1, 0).astype(BF)


def pick_one(source, mine, theirs):
    own, other = pickers()
    mine[...] = dot(source[...], own, 1, 0).astype(BF)
    theirs[...] = dot(source[...], other, 1, 0).astype(BF)


def enter_spatial_back(back, both, cot, mod, w_out, mid_grad, att_grad, mine, theirs):
    unit, spread = normalized(both[:, :D].astype(F32))
    grad = normalized_back(unit, spread, mod[4:5, :], back[:, :D].astype(F32))
    total = (cot[...].astype(F32) + grad).astype(BF)
    mid_grad[...] = total
    scaled = (mod[2:3, :] * total.astype(F32)).astype(BF)
    att_grad[...] = dot(scaled, w_out[...], 1, 1).astype(BF)
    own, other = pickers()
    mine[...] = dot(scaled, own, 1, 0).astype(BF)
    theirs[:, :A] = dot(scaled, other, 1, 0).astype(BF)
    theirs[:, A:] = back[:, D:]


def spatial_attention_back(
    att_grad, qkv_t, probs_t, gains, qkv_grad, tall_grad, wide, flat, tall
):
    flat[:, A:] = jnp.zeros((T, A_PAD - A), F32)
    flat[:, :A] = att_grad[...].astype(F32)
    flip(flat, tall, A_PAD // 128)
    tall_grad[Q:, :] = jnp.zeros((Q_PAD - Q, T), F32)
    pair = (gains[:, 0:1], gains[:, 1:2])
    for h in range(HEADS):
        grads = head_back(
            qkv_t[head_rows(0, h), :], qkv_t[head_rows(1, h), :], qkv_t[head_rows(2, h), :],
            pair, probs_t[h], tall[head_rows(0, h), :]
        )
        for which in range(3):
            tall_grad[head_rows(which, h), :] = grads[which]
    flip_back(tall_grad, wide, Q_PAD // 128)
    qkv_grad[...] = wide[:, :Q].astype(BF)


def leave_spatial_back(mid_grad, qkv_grad, latents, mod, w_qkv, latents_grad):
    norm_grad = dot(qkv_grad[...], w_qkv[...], 1, 1).astype(BF).astype(F32)
    unit, spread = normalized(latents[...].astype(F32))
    grad = normalized_back(unit, spread, mod[1:2, :], norm_grad)
    latents_grad[...] = (mid_grad[...].astype(F32) + grad).astype(BF)


def project_output(both, back, mod, w_out, output):
    result = dot(back[:, D:], w_out[...], 1, 0)
    output[...] = (both[:, :D].astype(F32) + mod[5:6, :] * result).astype(BF)


def weight_rows(columns):
    def body(*refs):
        keep, sends = refs[-4], refs[-3:]
        ins = refs[:-4]
        start = 0
        for k, width in enumerate(columns):
            left, left_in, right, right_in = (ref[...] for ref in ins[4 * k : 4 * k + 4])
            total = dot(left, right, 0, 0) + dot(left_in, right_in, 0, 0)
            padded = -(-width // 128) * 128
            for p in range(3):
                rows = total[192 * p : 192 * p + 192]
                keep[p, :, start : start + width] = rows[:96]
                sends[p][:, start : start + width] = rows[96:].astype(BF)
                if padded > width:
                    keep[p, :, start + width : start + padded] = jnp.zeros((96, padded - width), F32)
                    sends[p][:, start + width : start + padded] = jnp.zeros((96, padded - width), BF)
            start += padded

    return body


def add_halve(keep, got, kept, send):
    half = kept.shape[0]
    total = keep[...] + got[...].astype(F32)
    kept[...] = total[:half]
    send[...] = total[half:].astype(BF)


def add_halve_first(keep, got, kept, send):
    half = kept.shape[0]
    total = keep[0] + got[...].astype(F32)
    kept[...] = total[:half]
    send[...] = total[half:].astype(BF)


def make_add_halve_first(p):
    def body(keep, got, kept, send):
        half = kept.shape[0]
        total = keep[p] + got[...].astype(F32)
        kept[...] = total[:half]
        send[...] = total[half:].astype(BF)

    return body


def join_halve(*refs):
    kept, send = refs[-2:]
    ins = refs[:-2]
    start = 0
    for g in range(0, len(ins), 6):
        width = ins[g].shape[1]
        for p in range(3):
            total = ins[g + p][...] + ins[g + 3 + p][...].astype(F32)
            half = total.shape[0] // 2
            kept[p, :, start : start + width] = total[:half]
            send[p, :, start : start + width] = total[half:].astype(BF)
        start += width


def tail_halve(keep, got, kept, send):
    half = kept.shape[1]
    for p in range(3):
        total = keep[p] + got[p].astype(F32)
        kept[p] = total[:half]
        send[p] = total[half:].astype(BF)


def last_add(keep, got, *outs):
    start = 0
    for out in outs:
        width = out.shape[1]
        for p in range(3):
            rows = keep[p, :, start : start + width] + got[p, :, start : start + width].astype(F32)
            out[3 * p : 3 * p + 3, :] = rows
        start += -(-width // 128) * 128


def pairs(change):
    found = []
    for device in range(128):
        dp, seq = divmod(device, 8)
        x, y, z, core = dp >> 2, ((dp >> 1) & 1) * 2 + (seq >> 2), seq & 3, dp & 1
        x, y, z, core = change(x, y, z, core)
        found.append((device, (x * 4 + (y >> 1) * 2 + core) * 8 + (y & 1) * 4 + z))
    return found


def to_other_core(value):
    return lax.ppermute(value, MESH, pairs(lambda x, y, z, c: (x, y, z, 1 - c)))


def along(value, axis, late):
    def change(x, y, z, core):
        place = [x, y, z]
        place[axis] ^= 1 if (core == 0) != late else 3
        return (*place, core)

    return lax.ppermute(value, MESH, pairs(change))


def early_rounds(keep, sends):
    columns = keep.shape[2]
    kept, out = [], []
    for p in range(3):
        got = along(sends[p], p, False)
        mine, send = call(
            make_add_halve_first(p),
            [((48, columns), F32), ((48, columns), BF)],
            (keep, got),
            96 * columns,
        )
        kept.append(mine)
        out.append(send)
    for p in range(3):
        got = along(out[p], (p + 1) % 3, False)
        kept[p], out[p] = call(
            add_halve, [((24, columns), F32), ((24, columns), BF)], (kept[p], got), 48 * columns
        )
    return kept, [along(out[p], (p + 2) % 3, False) for p in range(3)]


def weight_partials(groups, columns):
    width = sum(-(-w // 128) * 128 for w in columns)
    outs = [((3, 96, width), F32)] + [((96, width), BF)] * 3
    args = [x for group in groups for x in group]
    keep, *sends = call(weight_rows(columns), outs, args, 2 * 512 * A * width)
    return keep, sends


def shards(
    latents, cotangent, modulation, qk_gains, spatial_qkv, spatial_out, temporal_qkv, temporal_out
):
    x, cot = latents.reshape(T, D), cotangent.reshape(T, D)
    mod = modulation.reshape(6, D)
    gains_s, gains_t = qk_gains[0].T, qk_gains[1].T
    wide, tall_qkv = pltpu.VMEM((T, Q_PAD), F32), pltpu.VMEM((Q_PAD, T), F32)
    flat, tall = pltpu.VMEM((T, A_PAD), F32), pltpu.VMEM((A_PAD, T), F32)

    both, qkv_t, probs_t, normed_s, att_s, scaled_t = call(
        forward_spatial,
        [
            ((T, D + A), BF), ((Q_PAD, T), F32), ((HEADS, T, T), F32),
            ((T, D), BF), ((T, A), BF), ((T, D), BF),
        ],
        (x, cot, mod, gains_s, spatial_qkv, spatial_out, temporal_out),
        2 * T * D * (Q + 2 * A),
        (wide, flat, tall),
    )
    patch = lax.all_to_all(both.reshape(8, LOCAL, D + A), "seq", 0, 0, tiled=True)
    early_mine, early_theirs = call(
        pick_two, [((T, D), BF), ((T, D), BF)], (normed_s, scaled_t), 4 * T * D * D
    )
    early_in, att_s_in = to_other_core(early_theirs), to_other_core(att_s)

    back_patch, normed_t, qkv_grad_t = call(
        temporal,
        [((T, D + A), BF), ((T, D), BF), ((T, Q), BF)],
        (patch.reshape(T, D + A), mod, gains_t, temporal_qkv),
        4 * T * D * Q,
        (wide, tall_qkv, tall_qkv, flat, tall, tall),
    )
    back = lax.all_to_all(back_patch.reshape(8, LOCAL, D + A), "seq", 0, 0, tiled=True)
    back = back.reshape(T, D + A)
    t_mine, t_theirs = call(pick_one, [((T, A), BF), ((T, A), BF)], (normed_t,), 4 * T * D * A)
    t_in, qkv_grad_t_in = to_other_core(t_theirs), to_other_core(qkv_grad_t)
    keep_t, sends_t = weight_partials([(t_mine, t_in, qkv_grad_t, qkv_grad_t_in)], (Q,))
    kept_t, got_t = early_rounds(keep_t, sends_t)

    mid_grad, att_grad_s, late_mine, late_theirs = call(
        enter_spatial_back,
        [((T, D), BF), ((T, A), BF), ((T, A), BF), ((T, D), BF)],
        (back, both, cot, mod, spatial_out),
        6 * T * D * A,
    )
    late_in = to_other_core(late_theirs)
    (qkv_grad_s,) = call(
        spatial_attention_back,
        [((T, Q), BF)],
        (att_grad_s, qkv_t, probs_t, gains_s),
        2 * T * T * HEADS * 128 * 5,
        (tall_qkv, wide, flat, tall),
    )
    qkv_grad_s_in = to_other_core(qkv_grad_s)
    (latents_grad,) = call(
        leave_spatial_back,
        [((T, D), BF)],
        (mid_grad, qkv_grad_s, x, mod, spatial_qkv),
        2 * T * D * Q,
    )
    (output,) = call(
        project_output, [((T, D), BF)], (both, back, mod, temporal_out), 2 * T * D * A
    )
    keep_s, sends_s = weight_partials(
        [
            (early_mine[:, :A], early_in[:, :A], qkv_grad_s, qkv_grad_s_in),
            (late_mine, late_in[:, :A], att_s, att_s_in),
            (early_mine[:, A:], early_in[:, A:], back[:, D:], late_in[:, A:]),
        ],
        (Q, A, A),
    )
    kept_s, got_s = early_rounds(keep_s, sends_s)
    columns = Q_PAD * 2 + A_PAD * 2
    kept, send = call(
        join_halve,
        [((3, 12, columns), F32), ((3, 12, columns), BF)],
        (*kept_s, *got_s, *kept_t, *got_t),
        72 * columns,
    )
    got = along(send, 0, True)
    kept, send = call(
        tail_halve, [((3, 6, columns), F32), ((3, 6, columns), BF)], (kept, got), 36 * columns
    )
    got = along(send, 1, True)
    kept, send = call(
        tail_halve, [((3, 3, columns), F32), ((3, 3, columns), BF)], (kept, got), 18 * columns
    )
    got = along(send, 2, True)
    sq, so, to, tq = call(
        last_add,
        [((9, Q), F32), ((9, A), F32), ((9, A), F32), ((9, Q), F32)],
        (kept, got),
        9 * columns,
    )
    shape = (1, 1, T, D)
    return output.reshape(shape), latents_grad.reshape(shape), sq, so.T, tq, to.T


def solution(mesh):
    tokens = P("dp", "seq", None, None)
    rows, cols = P(("dp", "seq"), None), P(None, ("dp", "seq"))
    return jax.shard_map(
        shards,
        mesh=mesh,
        in_specs=(tokens, tokens, P("dp", None, None, None), P(), P(), P(), P(), P()),
        out_specs=(tokens, tokens, rows, cols, rows, cols),
        check_vma=False,
    )
```

```python
import jax
import jax.numpy as jnp
from jax import lax
from jax.experimental import pallas as pl
from jax.experimental.pallas import tpu as pltpu
from jax.sharding import PartitionSpec as P

T = 256
D = 1152
HEADS = 8
HEAD_DIM = 72
A = HEADS * HEAD_DIM
Q = 3 * A
A_PAD = 640
Q_PAD = 1792
LOCAL = 32
EPS = 1e-06
BF = jnp.bfloat16
F32 = jnp.float32
MESH = ("dp", "seq")
MIB = 1024 * 1024


def dot(left, right, over_left, over_right):
    return lax.dot_general(
        left, right, (((over_left,), (over_right,)), ((), ())), preferred_element_type=F32
    )


def call(body, outs, args, flops, scratch=(), limit=24, apart=()):
    shapes = tuple(jax.ShapeDtypeStruct(shape, kind) for shape, kind in outs)
    size = sum(x.size * x.dtype.itemsize for x in args)
    size += sum(x.size * x.dtype.itemsize for x in shapes)
    spaces = [pltpu.HBM if k in apart else pltpu.VMEM for k in range(len(args))]
    return pl.pallas_call(
        body,
        out_shape=shapes,
        in_specs=[pl.BlockSpec(memory_space=space) for space in spaces],
        out_specs=tuple(pl.BlockSpec(memory_space=pltpu.VMEM) for _ in shapes),
        scratch_shapes=list(scratch),
        cost_estimate=pl.CostEstimate(flops=flops, bytes_accessed=size, transcendentals=0),
        compiler_params=pltpu.CompilerParams(vmem_limit_bytes=limit * MIB),
    )(*args)


def in_order(*values):
    return lax.optimization_barrier(values)


def normalized(x32):
    mean = jnp.mean(x32, axis=-1, keepdims=True)
    centered = x32 - mean
    spread = lax.rsqrt(jnp.mean(centered * centered, axis=-1, keepdims=True) + EPS)
    return centered * spread, spread


def normalized_back(unit, spread, scale, grad):
    grad = grad * (1.0 + scale)
    inner = jnp.mean(grad * unit, axis=-1, keepdims=True)
    return spread * (grad - jnp.mean(grad, axis=-1, keepdims=True) - unit * inner)


def flip(source, target, blocks):
    for b in range(blocks):
        target[128 * b : 128 * b + 128, :] = source[:, 128 * b : 128 * b + 128].T


def flip_back(source, target, blocks):
    for b in range(blocks):
        target[:, 128 * b : 128 * b + 128] = source[128 * b : 128 * b + 128, :].T


def gain_columns(gains, block):
    row = lax.broadcasted_iota(jnp.int32, (HEAD_DIM, HEAD_DIM), 0)
    column = lax.broadcasted_iota(jnp.int32, (HEAD_DIM, HEAD_DIM), 1)
    return tuple(
        jnp.sum(jnp.where(row == column, gains[block, k : k + 1, :], 0.0), axis=1, keepdims=True)
        for k in range(2)
    )


def head_rows(which, h):
    start = which * A + h * HEAD_DIM
    return slice(start, start + HEAD_DIM)


def head_norm(rows, gain):
    root = lax.rsqrt(jnp.mean(rows * rows, axis=0, keepdims=True) + EPS)
    return root, (rows * root * gain).astype(BF)


def head_norm_back(rows, root, gain, grad):
    grad = grad.astype(BF).astype(F32) * gain
    inner = jnp.mean(rows * grad, axis=0, keepdims=True)
    return (root * grad - rows * (root * root * root * inner)).astype(BF).astype(F32)


def same_patch():
    key = lax.broadcasted_iota(jnp.int32, (T, T), 0)
    query = lax.broadcasted_iota(jnp.int32, (T, T), 1)
    return ((key ^ query) & (LOCAL - 1)) == 0


def head_probs(queries, keys, mask):
    scores = dot(keys, queries, 0, 0) * HEAD_DIM ** (-0.5)
    if mask is not None:
        scores = jnp.where(mask, scores, -1e30)
    expo = jnp.exp(scores - jnp.max(scores, axis=0, keepdims=True))
    return expo * (1.0 / jnp.sum(expo, axis=0, keepdims=True))


def head_back(q_rows, k_rows, v_rows, gains, probs, grad):
    q_root, queries = head_norm(q_rows, gains[0])
    k_root, keys = head_norm(k_rows, gains[1])
    grad = grad.astype(BF)
    probs16 = probs.astype(BF)
    v_grad = dot(grad, probs16, 1, 1).astype(BF).astype(F32)
    p_grad = dot(v_rows.astype(BF), grad, 0, 0).astype(BF).astype(F32)
    inner = jnp.sum(p_grad * probs, axis=0, keepdims=True)
    s_grad = (probs * (p_grad - inner) * HEAD_DIM ** (-0.5)).astype(BF)
    q_grad = head_norm_back(q_rows, q_root, gains[0], dot(keys, s_grad, 1, 0))
    k_grad = head_norm_back(k_rows, k_root, gains[1], dot(queries, s_grad, 1, 1))
    return q_grad, k_grad, v_grad


def order(core, chip):
    row = lax.broadcasted_iota(jnp.int32, (1, A_PAD), 1)
    part = (row >= 192).astype(jnp.int32) + (row >= 384).astype(jnp.int32)
    rest = row - 192 * part
    first = (rest * 171) >> 12
    rest = rest - 24 * first
    second = (rest * 11) >> 5
    piece = 3 * part + rest - 3 * second
    place = []
    for axis in range(3):
        step = axis - part
        step = jnp.where(step < 0, step + 3, step)
        one = jnp.where(step == 0, first >> 2, jnp.where(step == 1, first >> 1, first)) & 1
        two = (second >> (2 - axis)) & 1
        near = jnp.where(core == 0, one, two) ^ ((chip[axis] ^ (chip[axis] >> 1)) & 1)
        far = jnp.where(core == 0, two, one) ^ (chip[axis] >> 1)
        place.append(2 * far + (near ^ far))
    x, y, z = place
    device = x * 32 + (y >> 1) * 16 + core * 8 + (y & 1) * 4 + z
    return jnp.where(row < A, 9 * device + piece, -1)


def position():
    dp, seq = lax.axis_index("dp"), lax.axis_index("seq")
    return dp & 1, (dp >> 2, ((dp >> 1) & 1) * 2 + (seq >> 2), seq & 3)


def picker(core, chip):
    feature = lax.broadcasted_iota(jnp.int32, (D, A_PAD), 0)
    return (feature == order(core, chip)).astype(F32).astype(BF)


def pickers():
    core, chip = position()
    return picker(core, chip), picker(1 - core, chip)


def forward_spatial(
    latents, cot, mod, gains, w_qkv_any, w_out_any, w_out_t_any,
    both, qkv_t, probs_t, normed, att, scaled_t, flat, tall, w_qkv, w_out, w_out_t, sems
):
    loads = [
        pltpu.make_async_copy(source, target, sems.at[k])
        for k, (source, target) in enumerate(
            ((w_qkv_any, w_qkv), (w_out_t_any, w_out_t), (w_out_any, w_out))
        )
    ]
    for load in loads:
        load.start()
    unit, _ = normalized(latents[...].astype(F32))
    norm = (unit * (1.0 + mod[1, 0:1, :]) + mod[0, 0:1, :]).astype(BF)
    normed[...] = norm
    scaled = (mod[2, 1:2, :] * cot[...].astype(F32)).astype(BF)
    scaled_t[...] = scaled
    loads[0].wait()
    qkv_t[...] = dot(w_qkv[...], norm, 1, 1).astype(BF).astype(F32)
    tall[A:, :] = jnp.zeros((A_PAD - A, T), F32)
    pair = gain_columns(gains, 0)
    for h in range(HEADS):
        queries = head_norm(qkv_t[head_rows(0, h), :], pair[0])[1]
        keys = head_norm(qkv_t[head_rows(1, h), :], pair[1])[1]
        probs = head_probs(queries, keys, None)
        probs_t[h] = probs
        values = qkv_t[head_rows(2, h), :].astype(BF)
        tall[head_rows(0, h), :] = dot(values, probs.astype(BF), 1, 0)
    flip_back(tall, flat, A_PAD // 128)
    att[...] = flat[...].astype(BF)
    loads[1].wait()
    both[:, D:] = dot(scaled, w_out_t[...], 1, 1).astype(BF)
    loads[2].wait()
    result = dot(att[:, :A], w_out[...], 1, 0)
    both[:, :D] = (latents[...].astype(F32) + mod[2, 0:1, :] * result).astype(BF)


def temporal(
    both, mod, gains, w_qkv, back, normed, qkv_grad, tall_qkv, tall_grad, wide, flat, tall, tall_att
):
    unit, _ = normalized(both[:, :D].astype(F32))
    norm = (unit * (1.0 + mod[1, 1:2, :]) + mod[0, 1:2, :]).astype(BF)
    normed[...] = norm
    tall_qkv[...] = dot(w_qkv[...], norm, 1, 1).astype(BF).astype(F32)
    flat[:, A:] = jnp.zeros((T, A_PAD - A), F32)
    flat[:, :A] = both[:, D:].astype(F32)
    flip(flat, tall, A_PAD // 128)
    tall_att[A:, :] = jnp.zeros((A_PAD - A, T), F32)
    tall_grad[Q:, :] = jnp.zeros((Q_PAD - Q, T), F32)
    mask = same_patch()
    pair = gain_columns(gains, 1)
    for h in range(HEADS):
        q_rows = tall_qkv[head_rows(0, h), :]
        k_rows = tall_qkv[head_rows(1, h), :]
        v_rows = tall_qkv[head_rows(2, h), :]
        probs = head_probs(head_norm(q_rows, pair[0])[1], head_norm(k_rows, pair[1])[1], mask)
        tall_att[head_rows(0, h), :] = dot(v_rows.astype(BF), probs.astype(BF), 1, 0)
        grads = head_back(q_rows, k_rows, v_rows, pair, probs, tall[head_rows(0, h), :])
        for which in range(3):
            tall_grad[head_rows(which, h), :] = grads[which]
    flip_back(tall_att, flat, A_PAD // 128)
    back[:, D:] = flat[:, :A].astype(BF)
    flip_back(tall_grad, wide, Q_PAD // 128)
    qkv_grad[...] = wide[...].astype(BF)
    back[:, :D] = dot(qkv_grad[:, :Q], w_qkv[...], 1, 0).astype(BF)


def pick_early(normed, scaled, att, mine, theirs):
    own, other = pickers()
    for k, source in enumerate((normed, scaled)):
        columns = slice(k * A_PAD, k * A_PAD + A_PAD)
        theirs[:, columns] = dot(source[...], other, 1, 0).astype(BF)
        mine[:, columns] = dot(source[...], own, 1, 0).astype(BF)
    theirs[:, 2 * A_PAD :] = att[...]


def pick_temporal(source, mine, theirs):
    own, other = pickers()
    mine[...] = dot(source[...], own, 1, 0).astype(BF)
    theirs[...] = dot(source[...], other, 1, 0).astype(BF)


def enter_spatial_back(back, both, cot, mod, w_out, mid_grad, att_grad, mine, theirs):
    unit, spread = normalized(both[:, :D].astype(F32))
    grad = normalized_back(unit, spread, mod[1, 1:2, :], back[:, :D].astype(F32))
    total = (cot[...].astype(F32) + grad).astype(BF)
    mid_grad[...] = total
    scaled = (mod[2, 0:1, :] * total.astype(F32)).astype(BF)
    att_grad[:, A:] = jnp.zeros((T, A_PAD - A), F32)
    att_grad[:, :A] = dot(scaled, w_out[...], 1, 1).astype(BF).astype(F32)
    own, other = pickers()
    mine[...] = dot(scaled, own, 1, 0).astype(BF)
    theirs[:, :A_PAD] = dot(scaled, other, 1, 0).astype(BF)
    theirs[:, A_PAD + A :] = jnp.zeros((T, A_PAD - A), BF)
    theirs[:, A_PAD : A_PAD + A] = back[:, D:]


def spatial_attention_back(att_grad, qkv_t, probs_t, gains, qkv_grad, tall_grad, wide, tall):
    flip(att_grad, tall, A_PAD // 128)
    tall_grad[Q:, :] = jnp.zeros((Q_PAD - Q, T), F32)
    pair = gain_columns(gains, 0)
    for h in range(HEADS):
        grads = head_back(
            qkv_t[head_rows(0, h), :], qkv_t[head_rows(1, h), :], qkv_t[head_rows(2, h), :],
            pair, probs_t[h], tall[head_rows(0, h), :]
        )
        for which in range(3):
            tall_grad[head_rows(which, h), :] = grads[which]
    flip_back(tall_grad, wide, Q_PAD // 128)
    qkv_grad[...] = wide[...].astype(BF)


def leave_spatial_back(mid_grad, qkv_grad, latents, mod, w_qkv, latents_grad):
    norm_grad = dot(qkv_grad[:, :Q], w_qkv[...], 1, 0).astype(BF).astype(F32)
    unit, spread = normalized(latents[...].astype(F32))
    grad = normalized_back(unit, spread, mod[1, 0:1, :], norm_grad)
    latents_grad[...] = (mid_grad[...].astype(F32) + grad).astype(BF)


def project_output(both, back, mod, w_out, output):
    result = dot(back[:, D:], w_out[...], 1, 0)
    output[...] = (both[:, :D].astype(F32) + mod[2, 1:2, :] * result).astype(BF)


def weight_rows(groups):
    def body(*refs):
        keep, sends = refs[-4], refs[-3:]
        start = 0
        for left, left_in, right, right_in, width in groups:
            total = None
            for (l_ref, l_at), (r_ref, r_at) in ((left, right), (left_in, right_in)):
                more = dot(
                    refs[l_ref][:, l_at : l_at + A], refs[r_ref][:, r_at : r_at + width], 0, 0
                )
                total = more if total is None else total + more
            padded = -(-width // 128) * 128
            for p in range(3):
                rows = total[192 * p : 192 * p + 192]
                keep[p, :, start : start + width] = rows[:96]
                sends[p][:, start : start + width] = rows[96:].astype(BF)
                if padded > width:
                    gap = slice(start + width, start + padded)
                    keep[p, :, gap] = jnp.zeros((96, padded - width), F32)
                    sends[p][:, gap] = jnp.zeros((96, padded - width), BF)
            start += padded

    return body


def first_halve(p):
    def body(*refs):
        kept, send = refs[-2:]
        half = kept.shape[0]
        start = 0
        for keep, got in ((refs[0], refs[1]), (refs[2], refs[3])):
            width = got.shape[1]
            total = keep[p] + got[...].astype(F32)
            kept[:, start : start + width] = total[:half]
            send[:, start : start + width] = total[half:].astype(BF)
            start += width

    return body


def add_halve(keep, got, kept, send):
    half = kept.shape[0]
    total = keep[...] + got[...].astype(F32)
    kept[...] = total[:half]
    send[...] = total[half:].astype(BF)


def join_halve(*refs):
    kept, send = refs[-2:]
    for p in range(3):
        total = refs[p][...] + refs[3 + p][...].astype(F32)
        half = total.shape[0] // 2
        kept[p] = total[:half]
        send[p] = total[half:].astype(BF)


def tail_halve(keep, got, kept, send):
    half = kept.shape[1]
    for p in range(3):
        total = keep[p] + got[p].astype(F32)
        kept[p] = total[:half]
        send[p] = total[half:].astype(BF)


def last_add(keep, got, *outs):
    start = 0
    for out in outs:
        width = out.shape[1]
        for p in range(3):
            rows = keep[p, :, start : start + width] + got[p, :, start : start + width].astype(F32)
            out[3 * p : 3 * p + 3, :] = rows
        start += -(-width // 128) * 128


def pairs(change):
    found = []
    for device in range(128):
        dp, seq = divmod(device, 8)
        x, y, z, core = dp >> 2, ((dp >> 1) & 1) * 2 + (seq >> 2), seq & 3, dp & 1
        x, y, z, core = change(x, y, z, core)
        found.append((device, (x * 4 + (y >> 1) * 2 + core) * 8 + (y & 1) * 4 + z))
    return found


def to_other_core(value):
    return lax.ppermute(value, MESH, pairs(lambda x, y, z, c: (x, y, z, 1 - c)))


def along(value, axis, late):
    def change(x, y, z, core):
        place = [x, y, z]
        place[axis] ^= 1 if (core == 0) != late else 3
        return (*place, core)

    return lax.ppermute(value, MESH, pairs(change))


def weight_partials(groups, args):
    width = sum(-(-group[-1] // 128) * 128 for group in groups)
    outs = [((3, 96, width), F32)] + [((96, width), BF)] * 3
    keep, *sends = call(weight_rows(groups), outs, args, 2 * 512 * A * width)
    return keep, sends


def shards(
    latents, cotangent, modulation, qk_gains, spatial_qkv, spatial_out, temporal_qkv, temporal_out
):
    x, cot = latents.reshape(T, D), cotangent.reshape(T, D)
    mod = modulation[0].transpose(1, 0, 2)
    w_qkv_s, w_qkv_t = spatial_qkv.T, temporal_qkv.T
    wide, tall_grad = pltpu.VMEM((T, Q_PAD), F32), pltpu.VMEM((Q_PAD, T), F32)
    flat, tall = pltpu.VMEM((T, A_PAD), F32), pltpu.VMEM((A_PAD, T), F32)

    both, qkv_t, probs_t, normed_s, att_s, scaled_t = call(
        forward_spatial,
        [
            ((T, D + A), BF), ((Q, T), F32), ((HEADS, T, T), F32),
            ((T, D), BF), ((T, A_PAD), BF), ((T, D), BF),
        ],
        (x, cot, mod, qk_gains, w_qkv_s, spatial_out, temporal_out),
        2 * T * D * (Q + 2 * A),
        (
            flat, tall, pltpu.VMEM((Q, D), BF), pltpu.VMEM((A, D), BF), pltpu.VMEM((A, D), BF),
            pltpu.SemaphoreType.DMA((3,)),
        ),
        apart=(4, 5, 6),
    )
    patch = lax.all_to_all(both.reshape(8, LOCAL, D + A), "seq", 0, 0, tiled=True)
    early_mine, early_theirs = call(
        pick_early,
        [((T, 2 * A_PAD), BF), ((T, 3 * A_PAD), BF)],
        (normed_s, scaled_t, att_s),
        4 * T * D * D,
    )
    patch, early_mine, early_theirs = in_order(patch, early_mine, early_theirs)
    early_in = to_other_core(early_theirs)

    back_patch, normed_t, qkv_grad_t = call(
        temporal,
        [((T, D + A), BF), ((T, D), BF), ((T, Q_PAD), BF)],
        (patch.reshape(T, D + A), mod, qk_gains, w_qkv_t),
        4 * T * D * Q,
        (pltpu.VMEM((Q, T), F32), tall_grad, wide, flat, tall, tall),
    )
    back = lax.all_to_all(back_patch.reshape(8, LOCAL, D + A), "seq", 0, 0, tiled=True)
    back = back.reshape(T, D + A)
    qkv_grad_t_in = to_other_core(qkv_grad_t)
    t_mine, t_theirs = call(
        pick_temporal, [((T, A_PAD), BF), ((T, A_PAD), BF)], (normed_t,), 4 * T * D * A
    )
    t_in = to_other_core(t_theirs)
    back, t_in, qkv_grad_t_in = in_order(back, t_in, qkv_grad_t_in)

    mid_grad, att_grad_s, late_mine, late_theirs = call(
        enter_spatial_back,
        [((T, D), BF), ((T, A_PAD), F32), ((T, A_PAD), BF), ((T, 2 * A_PAD), BF)],
        (back, both, cot, mod, spatial_out),
        6 * T * D * A,
    )
    late_in = to_other_core(late_theirs)
    (qkv_grad_s,) = call(
        spatial_attention_back,
        [((T, Q_PAD), BF)],
        (att_grad_s, qkv_t, probs_t, qk_gains),
        2 * T * T * HEADS * 128 * 5,
        (tall_grad, wide, tall),
    )
    qkv_grad_s_in = to_other_core(qkv_grad_s)
    keep_a, sends_a = weight_partials(
        (
            ((0, 0), (1, 0), (2, 0), (3, 0), Q),
            ((4, A_PAD), (5, A_PAD), (6, D), (7, A_PAD), A),
            ((8, 0), (7, 0), (9, 0), (5, 2 * A_PAD), A),
        ),
        (
            t_mine, t_in, qkv_grad_t, qkv_grad_t_in, early_mine, early_in, back, late_in, late_mine,
            att_s,
        ),
    )
    got_a = [along(sends_a[p], p, False) for p in range(3)]
    keep_b, sends_b = weight_partials(
        (((0, 0), (1, 0), (2, 0), (3, 0), Q),),
        (early_mine, early_in, qkv_grad_s, qkv_grad_s_in),
    )
    keep_b, *sends_b, mid_grad, back = in_order(keep_b, *sends_b, mid_grad, back)
    got_b = [along(sends_b[p], p, False) for p in range(3)]
    (latents_grad,) = call(
        leave_spatial_back,
        [((T, D), BF)],
        (mid_grad, qkv_grad_s, x, mod, w_qkv_s),
        2 * T * D * Q,
    )
    (output,) = call(
        project_output, [((T, D), BF)], (both, back, mod, temporal_out), 2 * T * D * A
    )
    keep_b, latents_grad, output = in_order(keep_b, latents_grad, output)

    columns = 2 * Q_PAD + 2 * A_PAD
    kept, got = [], []
    for p in range(3):
        mine, send = call(
            first_halve(p),
            [((48, columns), F32), ((48, columns), BF)],
            (keep_a, got_a[p], keep_b, got_b[p]),
            96 * columns,
        )
        kept.append(mine)
        got.append(along(send, (p + 1) % 3, False))
    for p in range(3):
        kept[p], send = call(
            add_halve, [((24, columns), F32), ((24, columns), BF)], (kept[p], got[p]), 48 * columns
        )
        got[p] = along(send, (p + 2) % 3, False)
    kept, send = call(
        join_halve,
        [((3, 12, columns), F32), ((3, 12, columns), BF)],
        (*kept, *got),
        72 * columns,
    )
    got = along(send, 0, True)
    kept, send = call(
        tail_halve, [((3, 6, columns), F32), ((3, 6, columns), BF)], (kept, got), 36 * columns
    )
    got = along(send, 1, True)
    kept, send = call(
        tail_halve, [((3, 3, columns), F32), ((3, 3, columns), BF)], (kept, got), 18 * columns
    )
    got = along(send, 2, True)
    tq, to, so, sq = call(
        last_add,
        [((9, Q), F32), ((9, A), F32), ((9, A), F32), ((9, Q), F32)],
        (kept, got),
        9 * columns,
    )
    shape = (1, 1, T, D)
    return output.reshape(shape), latents_grad.reshape(shape), sq, so.T, tq, to.T


def solution(mesh):
    tokens = P("dp", "seq", None, None)
    rows, cols = P(("dp", "seq"), None), P(None, ("dp", "seq"))
    return jax.shard_map(
        shards,
        mesh=mesh,
        in_specs=(tokens, tokens, P("dp", None, None, None), P(), P(), P(), P(), P()),
        out_specs=(tokens, tokens, rows, cols, rows, cols),
        check_vma=False,
    )
```

```python
import math

import jax
import jax.numpy as jnp
from jax import lax
from jax.experimental import pallas as pl
from jax.experimental.pallas import tpu as pltpu
from jax.sharding import PartitionSpec as P

T = 256
D = 1152
HEADS = 8
HEAD_DIM = 72
A = HEADS * HEAD_DIM
Q = 3 * A
A_PAD = 640
Q_PAD = 1792
LOCAL = 32
EPS = 1e-06
BF = jnp.bfloat16
F32 = jnp.float32
MESH = ("dp", "seq")
MIB = 1024 * 1024


def dot(left, right, over_left, over_right):
    return lax.dot_general(
        left, right, (((over_left,), (over_right,)), ((), ())), preferred_element_type=F32
    )


def call(body, outs, args, flops, scratch=(), limit=16, apart=()):
    shapes, specs = [], []
    for k, (shape, kind, *place) in enumerate(outs):
        if not place:
            shapes.append(pltpu.VMEM(shape, kind))
        elif place[0] == "hbm":
            shapes.append(pltpu.HBM(shape, kind))
        else:
            shapes.append(jax.ShapeDtypeStruct(shape, kind))
        specs.append(pl.BlockSpec(memory_space=pltpu.HBM if place == ["hbm"] else pltpu.VMEM))
    size = sum(x.size * x.dtype.itemsize for x in args)
    size += sum(math.prod(out[0]) * jnp.dtype(out[1]).itemsize for out in outs)
    args = [
        pltpu.with_memory_space_constraint(x, pltpu.HBM) if k in apart else x
        for k, x in enumerate(args)
    ]
    spaces = [pltpu.HBM if k in apart else pltpu.VMEM for k in range(len(args))]
    return pl.pallas_call(
        body,
        out_shape=tuple(shapes),
        in_specs=[pl.BlockSpec(memory_space=space) for space in spaces],
        out_specs=tuple(specs),
        scratch_shapes=list(scratch),
        cost_estimate=pl.CostEstimate(flops=flops, bytes_accessed=size, transcendentals=0),
        compiler_params=pltpu.CompilerParams(vmem_limit_bytes=limit * MIB),
    )(*args)


def in_order(*values):
    return lax.optimization_barrier(values)


def normalized(x32):
    mean = jnp.mean(x32, axis=-1, keepdims=True)
    centered = x32 - mean
    spread = lax.rsqrt(jnp.mean(centered * centered, axis=-1, keepdims=True) + EPS)
    return centered * spread, spread


def normalized_back(unit, spread, scale, grad):
    grad = grad * (1.0 + scale)
    inner = jnp.mean(grad * unit, axis=-1, keepdims=True)
    return spread * (grad - jnp.mean(grad, axis=-1, keepdims=True) - unit * inner)


def flip(source, target, blocks):
    for b in range(blocks):
        target[128 * b : 128 * b + 128, :] = source[:, 128 * b : 128 * b + 128].T


def flip_back(source, target, blocks):
    for b in range(blocks):
        target[:, 128 * b : 128 * b + 128] = source[128 * b : 128 * b + 128, :].T


def gain_columns(gains, block):
    row = lax.broadcasted_iota(jnp.int32, (HEAD_DIM, HEAD_DIM), 0)
    column = lax.broadcasted_iota(jnp.int32, (HEAD_DIM, HEAD_DIM), 1)
    return tuple(
        jnp.sum(jnp.where(row == column, gains[block, k : k + 1, :], 0.0), axis=1, keepdims=True)
        for k in range(2)
    )


def head_rows(which, h):
    start = which * A + h * HEAD_DIM
    return slice(start, start + HEAD_DIM)


def head_norm(rows, gain):
    root = lax.rsqrt(jnp.mean(rows * rows, axis=0, keepdims=True) + EPS)
    return root, (rows * root * gain).astype(BF)


def head_norm_back(rows, root, gain, grad):
    grad = grad.astype(BF).astype(F32) * gain
    inner = jnp.mean(rows * grad, axis=0, keepdims=True)
    return (root * grad - rows * (root * root * root * inner)).astype(BF).astype(F32)


def same_patch():
    key = lax.broadcasted_iota(jnp.int32, (T, T), 0)
    query = lax.broadcasted_iota(jnp.int32, (T, T), 1)
    return ((key ^ query) & (LOCAL - 1)) == 0


def head_probs(queries, keys, mask):
    scores = dot(keys, queries, 0, 0) * HEAD_DIM ** (-0.5)
    if mask is not None:
        scores = jnp.where(mask, scores, -1e30)
    expo = jnp.exp(scores - jnp.max(scores, axis=0, keepdims=True))
    return expo * (1.0 / jnp.sum(expo, axis=0, keepdims=True))


def head_back(q_rows, k_rows, v_rows, gains, probs, grad):
    q_root, queries = head_norm(q_rows, gains[0])
    k_root, keys = head_norm(k_rows, gains[1])
    grad = grad.astype(BF)
    probs16 = probs.astype(BF)
    v_grad = dot(grad, probs16, 1, 1).astype(BF).astype(F32)
    p_grad = dot(v_rows.astype(BF), grad, 0, 0).astype(BF).astype(F32)
    inner = jnp.sum(p_grad * probs, axis=0, keepdims=True)
    s_grad = (probs * (p_grad - inner) * HEAD_DIM ** (-0.5)).astype(BF)
    q_grad = head_norm_back(q_rows, q_root, gains[0], dot(keys, s_grad, 1, 0))
    k_grad = head_norm_back(k_rows, k_root, gains[1], dot(queries, s_grad, 1, 1))
    return q_grad, k_grad, v_grad


def order(core, chip):
    row = lax.broadcasted_iota(jnp.int32, (A, 1), 0)
    part = (row >= 192).astype(jnp.int32) + (row >= 384).astype(jnp.int32)
    rest = row - 192 * part
    first = (rest * 171) >> 12
    rest = rest - 24 * first
    second = (rest * 11) >> 5
    piece = 3 * part + rest - 3 * second
    place = []
    for axis in range(3):
        step = axis - part
        step = jnp.where(step < 0, step + 3, step)
        one = jnp.where(step == 0, first >> 2, jnp.where(step == 1, first >> 1, first)) & 1
        two = (second >> (2 - axis)) & 1
        near = jnp.where(core == 0, one, two) ^ ((chip[axis] ^ (chip[axis] >> 1)) & 1)
        far = jnp.where(core == 0, two, one) ^ (chip[axis] >> 1)
        place.append(2 * far + (near ^ far))
    x, y, z = place
    device = x * 32 + (y >> 1) * 16 + core * 8 + (y & 1) * 4 + z
    return 9 * device + piece


def position():
    dp, seq = lax.axis_index("dp"), lax.axis_index("seq")
    return dp & 1, (dp >> 2, ((dp >> 1) & 1) * 2 + (seq >> 2), seq & 3)


def picker(core, chip):
    feature = lax.broadcasted_iota(jnp.int32, (A, D), 1)
    return (feature == order(core, chip)).astype(F32).astype(BF)


def pick(hot, source):
    return dot(hot, source, 1, 1).astype(BF)


def forward_spatial(*refs):
    sources, refs = refs[:7], refs[7:]
    latents, cot, mod, gains, w_qkv, w_out_t, w_out = refs[:7]
    both_far, both_mid, qkv_t, probs_t, normed, att, scaled_t, flat, tall, both, sems, out_sem = refs[7:]
    loads = [
        pltpu.make_async_copy(source, target, sems.at[k])
        for k, (source, target) in enumerate(zip(sources, refs[:7]))
    ]
    for load in loads:
        load.start()
    for load in loads[:4]:
        load.wait()
    unit, _ = normalized(latents[...].astype(F32))
    norm = (unit * (1.0 + mod[1, 0:1, :]) + mod[0, 0:1, :]).astype(BF)
    normed[...] = norm
    scaled = (mod[2, 1:2, :] * cot[...].astype(F32)).astype(BF)
    scaled_t[...] = scaled
    loads[4].wait()
    qkv_t[...] = dot(w_qkv[...], norm, 1, 1).astype(BF).astype(F32)
    tall[A:, :] = jnp.zeros((A_PAD - A, T), F32)
    pair = gain_columns(gains, 0)
    for h in range(HEADS):
        queries = head_norm(qkv_t[head_rows(0, h), :], pair[0])[1]
        keys = head_norm(qkv_t[head_rows(1, h), :], pair[1])[1]
        probs = head_probs(queries, keys, None)
        probs_t[h] = probs
        values = qkv_t[head_rows(2, h), :].astype(BF)
        tall[head_rows(0, h), :] = dot(values, probs.astype(BF), 1, 0)
    flip_back(tall, flat, A_PAD // 128)
    att[...] = flat[...].astype(BF)
    loads[5].wait()
    both[:, D:] = dot(scaled, w_out_t[...], 1, 1).astype(BF)
    loads[6].wait()
    result = dot(att[:, :A], w_out[...], 1, 0)
    mid = (latents[...].astype(F32) + mod[2, 0:1, :] * result).astype(BF)
    both_mid[...] = mid
    both[:, :D] = mid
    send = pltpu.make_async_copy(both, both_far, out_sem)
    send.start()
    send.wait()


def temporal(
    both, mod, gains, w_qkv, back_far, normed, qkv_grad,
    tall_qkv, tall_grad, wide, flat, tall, tall_att, back, out_sem
):
    unit, _ = normalized(both[:, :D].astype(F32))
    norm = (unit * (1.0 + mod[1, 1:2, :]) + mod[0, 1:2, :]).astype(BF)
    normed[...] = norm
    tall_qkv[...] = dot(w_qkv[...], norm, 1, 1).astype(BF).astype(F32)
    flat[:, A:] = jnp.zeros((T, A_PAD - A), F32)
    flat[:, :A] = both[:, D:].astype(F32)
    flip(flat, tall, A_PAD // 128)
    tall_att[A:, :] = jnp.zeros((A_PAD - A, T), F32)
    tall_grad[Q:, :] = jnp.zeros((Q_PAD - Q, T), F32)
    mask = same_patch()
    pair = gain_columns(gains, 1)
    for h in range(HEADS):
        q_rows = tall_qkv[head_rows(0, h), :]
        k_rows = tall_qkv[head_rows(1, h), :]
        v_rows = tall_qkv[head_rows(2, h), :]
        probs = head_probs(head_norm(q_rows, pair[0])[1], head_norm(k_rows, pair[1])[1], mask)
        tall_att[head_rows(0, h), :] = dot(v_rows.astype(BF), probs.astype(BF), 1, 0)
        grads = head_back(q_rows, k_rows, v_rows, pair, probs, tall[head_rows(0, h), :])
        for which in range(3):
            tall_grad[head_rows(which, h), :] = grads[which]
    flip_back(tall_att, flat, A_PAD // 128)
    back[:, D:] = flat[:, :A].astype(BF)
    flip_back(tall_grad, wide, Q_PAD // 128)
    qkv_grad[...] = wide[...].astype(BF)
    back[:, :D] = dot(qkv_grad[:, :Q], w_qkv[...], 1, 0).astype(BF)
    send = pltpu.make_async_copy(back, back_far, out_sem)
    send.start()
    send.wait()


def pick_early(normed, scaled, w_far, own, other, mine, theirs, w_qkv, sem):
    load = pltpu.make_async_copy(w_far, w_qkv, sem)
    load.start()
    core, chip = position()
    own[...] = picker(core, chip)
    other[...] = picker(1 - core, chip)
    for k, source in enumerate((normed, scaled)):
        rows = slice(k * A, k * A + A)
        theirs[rows, :] = pick(other[...], source[...])
        mine[rows, :] = pick(own[...], source[...])
    load.wait()


def pick_later(source, own, other, mine, theirs):
    theirs[...] = pick(other[...], source[...])
    mine[...] = pick(own[...], source[...])


def enter_spatial_back(back, mid, cot, mod, w_out, mid_grad, scaled_s, att_grad, att_t):
    unit, spread = normalized(mid[...].astype(F32))
    grad = normalized_back(unit, spread, mod[1, 1:2, :], back[:, :D].astype(F32))
    total = (cot[...].astype(F32) + grad).astype(BF)
    mid_grad[...] = total
    scaled = (mod[2, 0:1, :] * total.astype(F32)).astype(BF)
    scaled_s[...] = scaled
    att_grad[:, A:] = jnp.zeros((T, A_PAD - A), F32)
    att_grad[:, :A] = dot(scaled, w_out[...], 1, 1).astype(BF).astype(F32)
    att_t[:, A:] = jnp.zeros((T, A_PAD - A), BF)
    att_t[:, :A] = back[:, D:]


def spatial_attention_back(att_grad, qkv_t, probs_t, gains, qkv_grad, tall_grad, wide, tall):
    flip(att_grad, tall, A_PAD // 128)
    tall_grad[Q:, :] = jnp.zeros((Q_PAD - Q, T), F32)
    pair = gain_columns(gains, 0)
    for h in range(HEADS):
        grads = head_back(
            qkv_t[head_rows(0, h), :], qkv_t[head_rows(1, h), :], qkv_t[head_rows(2, h), :],
            pair, probs_t[h], tall[head_rows(0, h), :]
        )
        for which in range(3):
            tall_grad[head_rows(which, h), :] = grads[which]
    flip_back(tall_grad, wide, Q_PAD // 128)
    qkv_grad[...] = wide[...].astype(BF)


def leave_spatial_back(mid_grad, qkv_grad, latents, mod, w_qkv, latents_grad):
    norm_grad = dot(qkv_grad[:, :Q], w_qkv[...], 1, 0).astype(BF).astype(F32)
    unit, spread = normalized(latents[...].astype(F32))
    grad = normalized_back(unit, spread, mod[1, 0:1, :], norm_grad)
    latents_grad[...] = (mid_grad[...].astype(F32) + grad).astype(BF)


def project_output(mid, att_t, mod, w_out, output):
    result = dot(att_t[:, :A], w_out[...], 1, 0)
    output[...] = (mid[...].astype(F32) + mod[2, 1:2, :] * result).astype(BF)


def weight_rows(groups):
    def body(*refs):
        keep, sends = refs[-4], refs[-3:]
        start = 0
        for (left, left_in, row), (right, right_in, column), width in groups:
            lefts = [refs[k][row : row + A, :] for k in (left, left_in)]
            rights = [refs[k][:, column : column + width] for k in (right, right_in)]
            tall_left = jnp.concatenate(lefts, axis=1)
            tall_right = jnp.concatenate(rights, axis=0)
            padded = -(-width // 128) * 128
            for at in range(0, width, 576):
                size = min(576, width - at)
                total = dot(tall_left, tall_right[:, at : at + size], 1, 0)
                for p in range(3):
                    rows = total[192 * p : 192 * p + 192]
                    columns = slice(start + at, start + at + size)
                    keep[p, :, columns] = rows[:96]
                    sends[p][:, columns] = rows[96:].astype(BF)
            if padded > width:
                gap = slice(start + width, start + padded)
                for p in range(3):
                    keep[p, :, gap] = jnp.zeros((96, padded - width), F32)
                    sends[p][:, gap] = jnp.zeros((96, padded - width), BF)
            start += padded

    return body


def first_halve(p):
    def body(*refs):
        kept, send = refs[-2:]
        half = kept.shape[0]
        start = 0
        for keep, got in zip(refs[0:6:2], refs[1:6:2]):
            width = got.shape[1]
            total = keep[p] + got[...].astype(F32)
            kept[:, start : start + width] = total[:half]
            send[:, start : start + width] = total[half:].astype(BF)
            start += width

    return body


def add_halve(keep, got, kept, send):
    half = kept.shape[0]
    total = keep[...] + got[...].astype(F32)
    kept[...] = total[:half]
    send[...] = total[half:].astype(BF)


def join_halve(*refs):
    kept, send = refs[-2:]
    for p in range(3):
        total = refs[p][...] + refs[3 + p][...].astype(F32)
        half = total.shape[0] // 2
        kept[p] = total[:half]
        send[p] = total[half:].astype(BF)


def tail_halve(keep, got, kept, send):
    half = kept.shape[1]
    for p in range(3):
        total = keep[p] + got[p].astype(F32)
        kept[p] = total[:half]
        send[p] = total[half:].astype(BF)


def last_add(keep, got, *outs):
    start = 0
    for out in outs:
        width = out.shape[1]
        for p in range(3):
            rows = keep[p, :, start : start + width] + got[p, :, start : start + width].astype(F32)
            out[3 * p : 3 * p + 3, :] = rows
        start += -(-width // 128) * 128


def pairs(change):
    found = []
    for device in range(128):
        dp, seq = divmod(device, 8)
        x, y, z, core = dp >> 2, ((dp >> 1) & 1) * 2 + (seq >> 2), seq & 3, dp & 1
        x, y, z, core = change(x, y, z, core)
        found.append((device, (x * 4 + (y >> 1) * 2 + core) * 8 + (y & 1) * 4 + z))
    return found


def to_other_core(value):
    return lax.ppermute(value, MESH, pairs(lambda x, y, z, c: (x, y, z, 1 - c)))


def along(value, axis, late):
    def change(x, y, z, core):
        place = [x, y, z]
        place[axis] ^= 1 if (core == 0) != late else 3
        return (*place, core)

    return lax.ppermute(value, MESH, pairs(change))


def weight_partials(groups, args):
    width = sum(-(-group[-1] // 128) * 128 for group in groups)
    outs = [((3, 96, width), F32)] + [((96, width), BF)] * 3
    keep, *sends = call(weight_rows(groups), outs, args, 2 * 512 * A * width)
    return keep, sends


def shards(
    latents, cotangent, modulation, qk_gains, spatial_qkv, spatial_out, temporal_qkv, temporal_out
):
    wide, tall_grad = pltpu.VMEM((T, Q_PAD), F32), pltpu.VMEM((Q_PAD, T), F32)
    flat, tall = pltpu.VMEM((T, A_PAD), F32), pltpu.VMEM((A_PAD, T), F32)
    stage, signal = pltpu.VMEM((T, D + A), BF), pltpu.SemaphoreType.DMA(())
    one_block, pick_flops = ((A, T), BF), 2 * T * D * A

    x, cot, mod, gains, w_qkv_s, w_out_t, w_out_s, both, mid, qkv_t, probs_t, normed_s, att_s, scaled_t = call(
        forward_spatial,
        [
            ((T, D), BF), ((T, D), BF), ((3, 2, D), F32), ((2, 2, HEAD_DIM), F32),
            ((Q, D), BF), ((A, D), BF), ((A, D), BF),
            ((T, D + A), BF, "hbm"), ((T, D), BF), ((Q, T), F32), ((HEADS, T, T), F32),
            ((T, D), BF), ((T, A_PAD), BF), ((T, D), BF),
        ],
        (
            latents.reshape(T, D), cotangent.reshape(T, D), modulation[0].transpose(1, 0, 2), qk_gains,
            spatial_qkv.T, temporal_out, spatial_out,
        ),
        2 * T * D * (Q + 2 * A),
        (flat, tall, stage, pltpu.SemaphoreType.DMA((7,)), signal),
        limit=18,
        apart=range(7),
    )
    patch = lax.all_to_all(both.reshape(8, LOCAL, D + A), "seq", 0, 0, tiled=True)
    att_s_in = to_other_core(att_s)
    own, other, early_mine, early_theirs, w_qkv_t = call(
        pick_early,
        [((A, D), BF), ((A, D), BF), ((2 * A, T), BF), ((2 * A, T), BF), ((Q, D), BF)],
        (normed_s, scaled_t, temporal_qkv.T),
        4 * pick_flops,
        (signal,),
        apart=(2,),
    )
    patch, early_mine, early_theirs = in_order(patch, early_mine, early_theirs)
    early_in = to_other_core(early_theirs)

    back_patch, normed_t, qkv_grad_t = call(
        temporal,
        [((T, D + A), BF, "hbm"), ((T, D), BF), ((T, Q_PAD), BF)],
        (patch.reshape(T, D + A), mod, gains, w_qkv_t),
        4 * T * D * Q,
        (pltpu.VMEM((Q, T), F32), tall_grad, wide, flat, tall, tall, stage, signal),
        limit=20,
    )
    back = lax.all_to_all(back_patch.reshape(8, LOCAL, D + A), "seq", 0, 0, tiled=True)
    back = back.reshape(T, D + A)
    qkv_grad_t_in = to_other_core(qkv_grad_t)
    t_mine, t_theirs = call(pick_later, [one_block] * 2, (normed_t, own, other), 2 * pick_flops)
    t_in = to_other_core(t_theirs)
    keep_t, sends_t = weight_partials(
        (((0, 1, 0), (2, 3, 0), Q),), (t_mine, t_in, qkv_grad_t, qkv_grad_t_in)
    )
    back, *sends_t = in_order(back, *sends_t)
    got_t = [along(sends_t[p], p, False) for p in range(3)]

    mid_grad, scaled_s, att_grad_s, att_t = call(
        enter_spatial_back,
        [((T, D), BF), ((T, D), BF), ((T, A_PAD), F32), ((T, A_PAD), BF)],
        (back, mid, cot, mod, w_out_s),
        2 * T * D * A,
    )
    att_t_in = to_other_core(att_t)
    (qkv_grad_s,) = call(
        spatial_attention_back,
        [((T, Q_PAD), BF)],
        (att_grad_s, qkv_t, probs_t, gains),
        2 * T * T * HEADS * 128 * 5,
        (tall_grad, wide, tall),
    )
    qkv_grad_s_in = to_other_core(qkv_grad_s)
    qkv_grad_s, scaled_s = in_order(qkv_grad_s, scaled_s)
    late_mine, late_theirs = call(
        pick_later, [one_block] * 2, (scaled_s, own, other), 2 * pick_flops
    )
    late_in = to_other_core(late_theirs)
    keep_b, sends_b = weight_partials(
        (((0, 1, 0), (2, 3, 0), Q),), (early_mine, early_in, qkv_grad_s, qkv_grad_s_in)
    )
    keep_b, late_in, att_t, *sends_b = in_order(keep_b, late_in, att_t, *sends_b)
    got_b = [along(sends_b[p], p, False) for p in range(3)]
    keep_o, sends_o = weight_partials(
        (((0, 1, A), (2, 3, 0), A), ((4, 5, 0), (6, 7, 0), A)),
        (early_mine, early_in, att_t, att_t_in, late_mine, late_in, att_s, att_s_in),
    )
    keep_o, att_t, *sends_o = in_order(keep_o, att_t, *sends_o)
    got_o = [along(sends_o[p], p, False) for p in range(3)]
    (output,) = call(
        project_output, [((T, D), BF, "any")], (mid, att_t, mod, w_out_t), 2 * T * D * A
    )
    keep_b, output = in_order(keep_b, output)

    columns = 2 * Q_PAD + 2 * A_PAD
    kept, got = [], []
    for p in range(3):
        mine, send = call(
            first_halve(p),
            [((48, columns), F32), ((48, columns), BF)],
            (keep_t, got_t[p], keep_o, got_o[p], keep_b, got_b[p]),
            96 * columns,
        )
        kept.append(mine)
        got.append(along(send, (p + 1) % 3, False))
    mid_grad, kept[2] = in_order(mid_grad, kept[2])
    (latents_grad,) = call(
        leave_spatial_back,
        [((T, D), BF, "any")],
        (mid_grad, qkv_grad_s, x, mod, w_qkv_s),
        2 * T * D * Q,
    )
    kept[0], latents_grad = in_order(kept[0], latents_grad)
    for p in range(3):
        kept[p], send = call(
            add_halve, [((24, columns), F32), ((24, columns), BF)], (kept[p], got[p]), 48 * columns
        )
        got[p] = along(send, (p + 2) % 3, False)
    kept, send = call(
        join_halve,
        [((3, 12, columns), F32), ((3, 12, columns), BF)],
        (*kept, *got),
        72 * columns,
    )
    got = along(send, 0, True)
    kept, send = call(
        tail_halve, [((3, 6, columns), F32), ((3, 6, columns), BF)], (kept, got), 36 * columns
    )
    got = along(send, 1, True)
    kept, send = call(
        tail_halve, [((3, 3, columns), F32), ((3, 3, columns), BF)], (kept, got), 18 * columns
    )
    got = along(send, 2, True)
    tq, to, so, sq = call(
        last_add,
        [((9, Q), F32, "any"), ((9, A), F32, "any"), ((9, A), F32, "any"), ((9, Q), F32, "any")],
        (kept, got),
        9 * columns,
    )
    shape = (1, 1, T, D)
    return output.reshape(shape), latents_grad.reshape(shape), sq, so.T, tq, to.T


def solution(mesh):
    tokens = P("dp", "seq", None, None)
    rows, cols = P(("dp", "seq"), None), P(None, ("dp", "seq"))
    return jax.shard_map(
        shards,
        mesh=mesh,
        in_specs=(tokens, tokens, P("dp", None, None, None), P(), P(), P(), P(), P()),
        out_specs=(tokens, tokens, rows, cols, rows, cols),
        check_vma=False,
    )
```

```python
import math

import jax
import jax.numpy as jnp
from jax import lax
from jax.experimental import pallas as pl
from jax.experimental.pallas import tpu as pltpu
from jax.sharding import PartitionSpec as P

T = 256
D = 1152
HEADS = 8
HEAD_DIM = 72
A = HEADS * HEAD_DIM
Q = 3 * A
A_PAD = 640
Q_PAD = 1792
LOCAL = 32
EPS = 1e-06
BF = jnp.bfloat16
F32 = jnp.float32
MESH = ("dp", "seq")
MIB = 1024 * 1024


def dot(left, right, over_left, over_right):
    return lax.dot_general(
        left, right, (((over_left,), (over_right,)), ((), ())), preferred_element_type=F32
    )


def call(body, outs, args, cost, scratch=(), limit=16, apart=()):
    shapes, specs = [], []
    for k, (shape, kind, *place) in enumerate(outs):
        if not place:
            shapes.append(pltpu.VMEM(shape, kind))
        elif place[0] == "hbm":
            shapes.append(pltpu.HBM(shape, kind))
        else:
            shapes.append(jax.ShapeDtypeStruct(shape, kind))
        specs.append(pl.BlockSpec(memory_space=pltpu.HBM if place == ["hbm"] else pltpu.VMEM))
    size = sum(x.size * x.dtype.itemsize for x in args)
    size += sum(math.prod(out[0]) * jnp.dtype(out[1]).itemsize for out in outs)
    args = [
        pltpu.with_memory_space_constraint(x, pltpu.HBM) if k in apart else x
        for k, x in enumerate(args)
    ]
    spaces = [pltpu.HBM if k in apart else pltpu.VMEM for k in range(len(args))]
    return pl.pallas_call(
        body,
        out_shape=tuple(shapes),
        in_specs=[pl.BlockSpec(memory_space=space) for space in spaces],
        out_specs=tuple(specs),
        scratch_shapes=list(scratch),
        cost_estimate=pl.CostEstimate(
            flops=int(cost * 1.1e9), bytes_accessed=size, transcendentals=0
        ),
        compiler_params=pltpu.CompilerParams(vmem_limit_bytes=limit * MIB),
    )(*args)


def in_order(*values):
    return lax.optimization_barrier(values)


def normalized(x32):
    mean = jnp.mean(x32, axis=-1, keepdims=True)
    centered = x32 - mean
    spread = lax.rsqrt(jnp.mean(centered * centered, axis=-1, keepdims=True) + EPS)
    return centered * spread, spread


def normalized_back(unit, spread, scale, grad):
    grad = grad * (1.0 + scale)
    inner = jnp.mean(grad * unit, axis=-1, keepdims=True)
    return spread * (grad - jnp.mean(grad, axis=-1, keepdims=True) - unit * inner)


def flip(source, target, blocks):
    for b in range(blocks):
        target[128 * b : 128 * b + 128, :] = source[:, 128 * b : 128 * b + 128].T


def flip_back(source, target, blocks):
    for b in range(blocks):
        target[:, 128 * b : 128 * b + 128] = source[128 * b : 128 * b + 128, :].T


def gain_columns(gains, block):
    row = lax.broadcasted_iota(jnp.int32, (HEAD_DIM, HEAD_DIM), 0)
    column = lax.broadcasted_iota(jnp.int32, (HEAD_DIM, HEAD_DIM), 1)
    return tuple(
        jnp.sum(jnp.where(row == column, gains[block, k : k + 1, :], 0.0), axis=1, keepdims=True)
        for k in range(2)
    )


def head_rows(which, h):
    start = which * A + h * HEAD_DIM
    return slice(start, start + HEAD_DIM)


def head_norm(rows, gain):
    root = lax.rsqrt(jnp.mean(rows * rows, axis=0, keepdims=True) + EPS)
    return root, (rows * root * gain).astype(BF)


def head_norm_back(rows, root, gain, grad):
    grad = grad.astype(BF).astype(F32) * gain
    inner = jnp.mean(rows * grad, axis=0, keepdims=True)
    return (root * grad - rows * (root * root * root * inner)).astype(BF).astype(F32)


def same_patch():
    key = lax.broadcasted_iota(jnp.int32, (T, T), 0)
    query = lax.broadcasted_iota(jnp.int32, (T, T), 1)
    return ((key ^ query) & (LOCAL - 1)) == 0


def head_probs(queries, keys, mask):
    scores = dot(keys, queries, 0, 0) * HEAD_DIM ** (-0.5)
    if mask is not None:
        scores = jnp.where(mask, scores, -1e30)
    expo = jnp.exp(scores - jnp.max(scores, axis=0, keepdims=True))
    return expo * (1.0 / jnp.sum(expo, axis=0, keepdims=True))


def head_back(q_rows, k_rows, v_rows, gains, probs, grad):
    q_root, queries = head_norm(q_rows, gains[0])
    k_root, keys = head_norm(k_rows, gains[1])
    grad = grad.astype(BF)
    probs16 = probs.astype(BF)
    v_grad = dot(grad, probs16, 1, 1).astype(BF).astype(F32)
    p_grad = dot(v_rows.astype(BF), grad, 0, 0).astype(BF).astype(F32)
    inner = jnp.sum(p_grad * probs, axis=0, keepdims=True)
    s_grad = (probs * (p_grad - inner) * HEAD_DIM ** (-0.5)).astype(BF)
    q_grad = head_norm_back(q_rows, q_root, gains[0], dot(keys, s_grad, 1, 0))
    k_grad = head_norm_back(k_rows, k_root, gains[1], dot(queries, s_grad, 1, 1))
    return q_grad, k_grad, v_grad


def order(core, chip):
    row = lax.broadcasted_iota(jnp.int32, (A, 1), 0)
    part = (row >= 192).astype(jnp.int32) + (row >= 384).astype(jnp.int32)
    rest = row - 192 * part
    first = (rest * 171) >> 12
    rest = rest - 24 * first
    second = (rest * 11) >> 5
    piece = 3 * part + rest - 3 * second
    place = []
    for axis in range(3):
        step = axis - part
        step = jnp.where(step < 0, step + 3, step)
        one = jnp.where(step == 0, first >> 2, jnp.where(step == 1, first >> 1, first)) & 1
        two = jnp.where(step == 0, second >> 2, jnp.where(step == 1, second >> 1, second)) & 1
        near = jnp.where(core == 0, one, two) ^ ((chip[axis] ^ (chip[axis] >> 1)) & 1)
        far = jnp.where(core == 0, two, one) ^ (chip[axis] >> 1)
        place.append(2 * far + (near ^ far))
    x, y, z = place
    device = x * 32 + (y >> 1) * 16 + core * 8 + (y & 1) * 4 + z
    return 9 * device + piece


def position():
    dp, seq = lax.axis_index("dp"), lax.axis_index("seq")
    return dp & 1, (dp >> 2, ((dp >> 1) & 1) * 2 + (seq >> 2), seq & 3)


def picker(core, chip):
    feature = lax.broadcasted_iota(jnp.int32, (A, D), 1)
    return (feature == order(core, chip)).astype(F32).astype(BF)


def pick(hot, source):
    return dot(hot, source, 1, 1).astype(BF)


def local_rows(k):
    return pl.ds(pl.multiple_of((lax.axis_index("seq") ^ k) * LOCAL, LOCAL), LOCAL)


def forward_spatial(*refs):
    sources, refs = refs[:7], refs[7:]
    latents, cot, mod, gains, w_qkv, w_out_t, w_out = refs[:7]
    chunks, (both_mid, qkv_t, probs_t, normed, att, scaled_t, flat, tall, both, sems) = refs[7:15], refs[15:]
    loads = [
        pltpu.make_async_copy(source, target, sems.at[k])
        for k, (source, target) in enumerate(zip(sources, refs[:7]))
    ]
    for load in loads:
        load.start()
    for load in loads[:4]:
        load.wait()
    unit, _ = normalized(latents[...].astype(F32))
    norm = (unit * (1.0 + mod[1, 0:1, :]) + mod[0, 0:1, :]).astype(BF)
    normed[...] = norm
    scaled = (mod[2, 1:2, :] * cot[...].astype(F32)).astype(BF)
    scaled_t[...] = scaled
    loads[4].wait()
    qkv_t[...] = dot(w_qkv[...], norm, 1, 1).astype(BF).astype(F32)
    tall[A:, :] = jnp.zeros((A_PAD - A, T), F32)
    pair = gain_columns(gains, 0)
    for h in range(HEADS):
        queries = head_norm(qkv_t[head_rows(0, h), :], pair[0])[1]
        keys = head_norm(qkv_t[head_rows(1, h), :], pair[1])[1]
        probs = head_probs(queries, keys, None)
        probs_t[h] = probs
        values = qkv_t[head_rows(2, h), :].astype(BF)
        tall[head_rows(0, h), :] = dot(values, probs.astype(BF), 1, 0)
    flip_back(tall, flat, A_PAD // 128)
    att[...] = flat[...].astype(BF)
    loads[5].wait()
    both[:, D:] = dot(scaled, w_out_t[...], 1, 1).astype(BF)
    loads[6].wait()
    result = dot(att[:, :A], w_out[...], 1, 0)
    mid = (latents[...].astype(F32) + mod[2, 0:1, :] * result).astype(BF)
    both_mid[...] = mid
    both[:, :D] = mid
    for k in range(8):
        chunks[k][...] = both[local_rows(k), :]


def temporal(*refs):
    mod, gains, w_qkv = refs[8:11]
    normed, qkv_grad, tall_qkv, tall_grad, wide, flat, tall, tall_att, both = refs[19:]
    for k in range(8):
        both[LOCAL * k : LOCAL * k + LOCAL, :] = refs[k][...]
    unit, _ = normalized(both[:, :D].astype(F32))
    norm = (unit * (1.0 + mod[1, 1:2, :]) + mod[0, 1:2, :]).astype(BF)
    normed[...] = norm
    tall_qkv[...] = dot(w_qkv[...], norm, 1, 1).astype(BF).astype(F32)
    flat[:, A:] = jnp.zeros((T, A_PAD - A), F32)
    flat[:, :A] = both[:, D:].astype(F32)
    flip(flat, tall, A_PAD // 128)
    tall_att[A:, :] = jnp.zeros((A_PAD - A, T), F32)
    tall_grad[Q:, :] = jnp.zeros((Q_PAD - Q, T), F32)
    mask = same_patch()
    pair = gain_columns(gains, 1)
    for h in range(HEADS):
        q_rows = tall_qkv[head_rows(0, h), :]
        k_rows = tall_qkv[head_rows(1, h), :]
        v_rows = tall_qkv[head_rows(2, h), :]
        probs = head_probs(head_norm(q_rows, pair[0])[1], head_norm(k_rows, pair[1])[1], mask)
        tall_att[head_rows(0, h), :] = dot(v_rows.astype(BF), probs.astype(BF), 1, 0)
        grads = head_back(q_rows, k_rows, v_rows, pair, probs, tall[head_rows(0, h), :])
        for which in range(3):
            tall_grad[head_rows(which, h), :] = grads[which]
    flip_back(tall_att, flat, A_PAD // 128)
    both[:, D:] = flat[:, :A].astype(BF)
    flip_back(tall_grad, wide, Q_PAD // 128)
    qkv_grad[...] = wide[...].astype(BF)
    both[:, :D] = dot(qkv_grad[:, :Q], w_qkv[...], 1, 0).astype(BF)
    for k in range(8):
        refs[11 + k][...] = both[LOCAL * k : LOCAL * k + LOCAL, :]


def pick_early(normed, scaled, w_far, own, other, mine, theirs, w_qkv, sem):
    load = pltpu.make_async_copy(w_far, w_qkv, sem)
    load.start()
    core, chip = position()
    own[...] = picker(core, chip)
    other[...] = picker(1 - core, chip)
    for k, source in enumerate((normed, scaled)):
        rows = slice(k * A, k * A + A)
        theirs[rows, :] = pick(other[...], source[...])
        mine[rows, :] = pick(own[...], source[...])
    load.wait()


def pick_later(source, own, other, mine, theirs):
    theirs[...] = pick(other[...], source[...])
    mine[...] = pick(own[...], source[...])


def enter_spatial_back(*refs):
    mid, cot, mod, w_out, mid_grad, scaled_s, att_grad, att_t, back = refs[8:]
    for k in range(8):
        back[local_rows(k), :] = refs[k][...]
    unit, spread = normalized(mid[...].astype(F32))
    grad = normalized_back(unit, spread, mod[1, 1:2, :], back[:, :D].astype(F32))
    total = (cot[...].astype(F32) + grad).astype(BF)
    mid_grad[...] = total
    scaled = (mod[2, 0:1, :] * total.astype(F32)).astype(BF)
    scaled_s[...] = scaled
    att_grad[:, A:] = jnp.zeros((T, A_PAD - A), F32)
    att_grad[:, :A] = dot(scaled, w_out[...], 1, 1).astype(BF).astype(F32)
    att_t[:, A:] = jnp.zeros((T, A_PAD - A), BF)
    att_t[:, :A] = back[:, D:]


def spatial_attention_back(att_grad, qkv_t, probs_t, gains, qkv_grad, tall_grad, wide, tall):
    flip(att_grad, tall, A_PAD // 128)
    tall_grad[Q:, :] = jnp.zeros((Q_PAD - Q, T), F32)
    pair = gain_columns(gains, 0)
    for h in range(HEADS):
        grads = head_back(
            qkv_t[head_rows(0, h), :], qkv_t[head_rows(1, h), :], qkv_t[head_rows(2, h), :],
            pair, probs_t[h], tall[head_rows(0, h), :]
        )
        for which in range(3):
            tall_grad[head_rows(which, h), :] = grads[which]
    flip_back(tall_grad, wide, Q_PAD // 128)
    qkv_grad[...] = wide[...].astype(BF)


def leave_spatial_back(mid_grad, qkv_grad, latents, mod, w_qkv, latents_grad):
    norm_grad = dot(qkv_grad[:, :Q], w_qkv[...], 1, 0).astype(BF).astype(F32)
    unit, spread = normalized(latents[...].astype(F32))
    grad = normalized_back(unit, spread, mod[1, 0:1, :], norm_grad)
    latents_grad[...] = (mid_grad[...].astype(F32) + grad).astype(BF)


def project_output(mid, att_t, mod, w_out, output):
    result = dot(att_t[:, :A], w_out[...], 1, 0)
    output[...] = (mid[...].astype(F32) + mod[2, 1:2, :] * result).astype(BF)


def weight_rows(groups):
    def body(*refs):
        keep, sends = refs[-4], refs[-3:]
        start = 0
        for (left, left_in, row), (right, right_in, column), width in groups:
            lefts = [refs[k][row : row + A, :] for k in (left, left_in)]
            rights = [refs[k][:, column : column + width] for k in (right, right_in)]
            tall_left = jnp.concatenate(lefts, axis=1)
            tall_right = jnp.concatenate(rights, axis=0)
            padded = -(-width // 128) * 128
            for at in range(0, width, 576):
                size = min(576, width - at)
                total = dot(tall_left, tall_right[:, at : at + size], 1, 0)
                for p in range(3):
                    rows = total[192 * p : 192 * p + 192]
                    columns = slice(start + at, start + at + size)
                    keep[p, :, columns] = rows[:96]
                    sends[p][:, columns] = rows[96:].astype(BF)
            if padded > width:
                gap = slice(start + width, start + padded)
                for p in range(3):
                    keep[p, :, gap] = jnp.zeros((96, padded - width), F32)
                    sends[p][:, gap] = jnp.zeros((96, padded - width), BF)
            start += padded

    return body


def first_halve(p):
    def body(*refs):
        kept, send = refs[-2:]
        half = kept.shape[0]
        start = 0
        for keep, got in zip(refs[0:6:2], refs[1:6:2]):
            width = got.shape[1]
            total = keep[p] + got[...].astype(F32)
            kept[:, start : start + width] = total[:half]
            send[:, start : start + width] = total[half:].astype(BF)
            start += width

    return body


def add_halve(keep, got, kept, send):
    half = kept.shape[0]
    total = keep[...] + got[...].astype(F32)
    kept[...] = total[:half]
    send[...] = total[half:].astype(BF)


def last_add(*refs):
    start = 0
    for out in refs[6:]:
        width = out.shape[1]
        columns = slice(start, start + width)
        for p in range(3):
            rows = refs[p][:, columns] + refs[3 + p][:, columns].astype(F32)
            out[3 * p : 3 * p + 3, :] = rows
        start += -(-width // 128) * 128


def pairs(change):
    found = []
    for device in range(128):
        dp, seq = divmod(device, 8)
        x, y, z, core = dp >> 2, ((dp >> 1) & 1) * 2 + (seq >> 2), seq & 3, dp & 1
        x, y, z, core = change(x, y, z, core)
        found.append((device, (x * 4 + (y >> 1) * 2 + core) * 8 + (y & 1) * 4 + z))
    return found


def to_other_core(value):
    return lax.ppermute(value, MESH, pairs(lambda x, y, z, c: (x, y, z, 1 - c)))


def along(value, axis, late):
    def change(x, y, z, core):
        place = [x, y, z]
        place[axis] ^= 1 if (core == 0) != late else 3
        return (*place, core)

    return lax.ppermute(value, MESH, pairs(change))


def to_frame_holders(chunks):
    def step(k):
        return lax.ppermute(chunks[k], MESH, [(d, d ^ k) for d in range(128)])

    return [chunks[0]] + [step(k) for k in range(1, 8)]


def weight_partials(groups, args):
    width = sum(-(-group[-1] // 128) * 128 for group in groups)
    outs = [((3, 96, width), F32)] + [((96, width), BF)] * 3
    keep, *sends = call(weight_rows(groups), outs, args, width / 1000)
    return keep, sends


def shards(
    latents, cotangent, modulation, qk_gains, spatial_qkv, spatial_out, temporal_qkv, temporal_out
):
    wide, tall_grad = pltpu.VMEM((T, Q_PAD), F32), pltpu.VMEM((Q_PAD, T), F32)
    flat, tall = pltpu.VMEM((T, A_PAD), F32), pltpu.VMEM((A_PAD, T), F32)
    stage = pltpu.VMEM((T, D + A), BF)
    one_block, chunk = ((A, T), BF), ((LOCAL, D + A), BF)

    x, cot, mod, gains, w_qkv_s, w_out_t, w_out_s, *rest = call(
        forward_spatial,
        [
            ((T, D), BF), ((T, D), BF), ((3, 2, D), F32), ((2, 2, HEAD_DIM), F32),
            ((Q, D), BF), ((A, D), BF), ((A, D), BF), *[chunk] * 8,
            ((T, D), BF), ((Q, T), F32), ((HEADS, T, T), F32),
            ((T, D), BF), ((T, A_PAD), BF), ((T, D), BF),
        ],
        (
            latents.reshape(T, D), cotangent.reshape(T, D), modulation[0].transpose(1, 0, 2), qk_gains,
            spatial_qkv.T, temporal_out, spatial_out,
        ),
        10,
        (flat, tall, stage, pltpu.SemaphoreType.DMA((7,))),
        limit=18,
        apart=range(7),
    )
    mid, qkv_t, probs_t, normed_s, att_s, scaled_t = rest[8:]
    patch = to_frame_holders(rest[:8])
    att_s_in = to_other_core(att_s)
    own, other, early_mine, early_theirs, w_qkv_t = call(
        pick_early,
        [((A, D), BF), ((A, D), BF), ((2 * A, T), BF), ((2 * A, T), BF), ((Q, D), BF)],
        (normed_s, scaled_t, temporal_qkv.T),
        2.8,
        (pltpu.SemaphoreType.DMA(()),),
        apart=(2,),
    )
    *patch, early_mine, early_theirs, att_s_in = in_order(
        *patch, early_mine, early_theirs, att_s_in
    )
    early_in = to_other_core(early_theirs)

    *back, normed_t, qkv_grad_t = call(
        temporal,
        [*[chunk] * 8, ((T, D), BF), ((T, Q_PAD), BF)],
        (*patch, mod, gains, w_qkv_t),
        10,
        (pltpu.VMEM((Q, T), F32), tall_grad, wide, flat, tall, tall, stage),
        limit=20,
    )
    back = to_frame_holders(back)
    qkv_grad_t_in = to_other_core(qkv_grad_t)
    t_mine, t_theirs = call(pick_later, [one_block] * 2, (normed_t, own, other), 1)
    t_in = to_other_core(t_theirs)
    keep_t, sends_t = weight_partials(
        (((0, 1, 0), (2, 3, 0), Q),), (t_mine, t_in, qkv_grad_t, qkv_grad_t_in)
    )
    *back, keep_t, early_in = in_order(*back, keep_t, early_in)
    got_t = [along(sends_t[p], p, False) for p in range(3)]

    mid_grad, scaled_s, att_grad_s, att_t = call(
        enter_spatial_back,
        [((T, D), BF), ((T, D), BF), ((T, A_PAD), F32), ((T, A_PAD), BF)],
        (*back, mid, cot, mod, w_out_s),
        2.8,
        (stage,),
    )
    att_t_in = to_other_core(att_t)
    (qkv_grad_s,) = call(
        spatial_attention_back,
        [((T, Q_PAD), BF)],
        (att_grad_s, qkv_t, probs_t, gains),
        2.9,
        (tall_grad, wide, tall),
    )
    qkv_grad_s, scaled_s, *got_t = in_order(qkv_grad_s, scaled_s, *got_t)
    qkv_grad_s_in = to_other_core(qkv_grad_s)
    late_mine, late_theirs = call(pick_later, [one_block] * 2, (scaled_s, own, other), 1)
    late_in = to_other_core(late_theirs)
    keep_b, sends_b = weight_partials(
        (((0, 1, 0), (2, 3, 0), Q),), (early_mine, early_in, qkv_grad_s, qkv_grad_s_in)
    )
    keep_b, late_in, att_t, *sends_b = in_order(keep_b, late_in, att_t, *sends_b)
    got_b = [along(sends_b[p], p, False) for p in range(3)]
    keep_o, sends_o = weight_partials(
        (((0, 1, A), (2, 3, 0), A), ((4, 5, 0), (6, 7, 0), A)),
        (early_mine, early_in, att_t, att_t_in, late_mine, late_in, att_s, att_s_in),
    )
    keep_o, att_t, *sends_o = in_order(keep_o, att_t, *sends_o)
    got_o = [along(sends_o[p], p, False) for p in range(3)]
    (output,) = call(project_output, [((T, D), BF, "any")], (mid, att_t, mod, w_out_t), 1.5)
    keep_b, output = in_order(keep_b, output)

    columns = 2 * Q_PAD + 2 * A_PAD
    kept, got = [], []
    for p in range(3):
        mine, send = call(
            first_halve(p),
            [((48, columns), F32), ((48, columns), BF)],
            (keep_t, got_t[p], keep_o, got_o[p], keep_b, got_b[p]),
            0.2,
        )
        kept.append(mine)
        got.append(along(send, (p + 1) % 3, False))
    mid_grad, kept[2] = in_order(mid_grad, kept[2])
    (latents_grad,) = call(
        leave_spatial_back, [((T, D), BF, "any")], (mid_grad, qkv_grad_s, x, mod, w_qkv_s), 2.7
    )
    kept[0], latents_grad = in_order(kept[0], latents_grad)
    for rows, turn, late in ((24, 2, False), (12, 0, True), (6, 1, True), (3, 2, True)):
        for p in range(3):
            kept[p], send = call(
                add_halve,
                [((rows, columns), F32), ((rows, columns), BF)],
                (kept[p], got[p]),
                0.2,
            )
            got[p] = along(send, (p + turn) % 3, late)
    tq, to, so, sq = call(
        last_add,
        [((9, Q), F32, "any"), ((9, A), F32, "any"), ((9, A), F32, "any"), ((9, Q), F32, "any")],
        (*kept, *got),
        0.8,
    )
    shape = (1, 1, T, D)
    return output.reshape(shape), latents_grad.reshape(shape), sq, so.T, tq, to.T


def solution(mesh):
    tokens = P("dp", "seq", None, None)
    rows, cols = P(("dp", "seq"), None), P(None, ("dp", "seq"))
    return jax.shard_map(
        shards,
        mesh=mesh,
        in_specs=(tokens, tokens, P("dp", None, None, None), P(), P(), P(), P(), P()),
        out_specs=(tokens, tokens, rows, cols, rows, cols),
        check_vma=False,
    )
```

```python
import math

import jax
import jax.numpy as jnp
from jax import lax
from jax.experimental import pallas as pl
from jax.experimental.pallas import tpu as pltpu
from jax.sharding import PartitionSpec as P

T = 256
D = 1152
HEADS = 8
HEAD_DIM = 72
A = HEADS * HEAD_DIM
Q = 3 * A
A_PAD = 640
Q_PAD = 1792
COLUMNS = 2 * Q_PAD + 2 * A_PAD
LOCAL = 32
STRIP = 288
EPS = 1e-06
BF = jnp.bfloat16
F32 = jnp.float32
MESH = ("dp", "seq")
MIB = 1024 * 1024
PEERS = (0, 6, 5, 7, 4, 2, 1, 3)


def dot(left, right, over_left, over_right):
    return lax.dot_general(
        left, right, (((over_left,), (over_right,)), ((), ())), preferred_element_type=F32
    )


def call(body, outs, args, cost, scratch=(), limit=16, apart=(), aliases={}):
    shapes, specs = [], []
    for k, (shape, kind, *place) in enumerate(outs):
        if not place:
            shapes.append(pltpu.VMEM(shape, kind))
        elif place[0] == "hbm":
            shapes.append(pltpu.HBM(shape, kind))
        else:
            shapes.append(jax.ShapeDtypeStruct(shape, kind))
        specs.append(pl.BlockSpec(memory_space=pltpu.HBM if place == ["hbm"] else pltpu.VMEM))
    size = sum(x.size * x.dtype.itemsize for x in args)
    size += sum(math.prod(out[0]) * jnp.dtype(out[1]).itemsize for out in outs)
    args = [
        pltpu.with_memory_space_constraint(x, pltpu.HBM) if k in apart else x
        for k, x in enumerate(args)
    ]
    spaces = [pltpu.HBM if k in apart else pltpu.VMEM for k in range(len(args))]
    return pl.pallas_call(
        body,
        out_shape=tuple(shapes),
        in_specs=[pl.BlockSpec(memory_space=space) for space in spaces],
        out_specs=tuple(specs),
        scratch_shapes=list(scratch),
        input_output_aliases=aliases,
        cost_estimate=pl.CostEstimate(
            flops=int(cost * 1.1e9), bytes_accessed=size, transcendentals=0
        ),
        compiler_params=pltpu.CompilerParams(vmem_limit_bytes=limit * MIB),
    )(*args)


def in_order(*values):
    return lax.optimization_barrier(values)


def normalized(x32):
    mean = jnp.mean(x32, axis=-1, keepdims=True)
    centered = x32 - mean
    spread = lax.rsqrt(jnp.mean(centered * centered, axis=-1, keepdims=True) + EPS)
    return centered * spread, spread


def normalized_back(unit, spread, scale, grad):
    grad = grad * (1.0 + scale)
    inner = jnp.mean(grad * unit, axis=-1, keepdims=True)
    return spread * (grad - jnp.mean(grad, axis=-1, keepdims=True) - unit * inner)


def flip(source, target, blocks):
    for b in range(blocks):
        target[128 * b : 128 * b + 128, :] = source[:, 128 * b : 128 * b + 128].T


def flip_back(source, target, blocks):
    for b in range(blocks):
        target[:, 128 * b : 128 * b + 128] = source[128 * b : 128 * b + 128, :].T


def gain_columns(gains, block):
    row = lax.broadcasted_iota(jnp.int32, (HEAD_DIM, HEAD_DIM), 0)
    column = lax.broadcasted_iota(jnp.int32, (HEAD_DIM, HEAD_DIM), 1)
    return tuple(
        jnp.sum(jnp.where(row == column, gains[block, k : k + 1, :], 0.0), axis=1, keepdims=True)
        for k in range(2)
    )


def head_rows(which, h):
    start = which * A + h * HEAD_DIM
    return slice(start, start + HEAD_DIM)


def head_norm(rows, gain):
    root = lax.rsqrt(jnp.mean(rows * rows, axis=0, keepdims=True) + EPS)
    return root, (rows * root * gain).astype(BF)


def head_norm_back(rows, root, gain, grad):
    grad = grad.astype(BF).astype(F32) * gain
    inner = jnp.mean(rows * grad, axis=0, keepdims=True)
    return (root * grad - rows * (root * root * root * inner)).astype(BF).astype(F32)


def same_patch():
    key = lax.broadcasted_iota(jnp.int32, (T, T), 0)
    query = lax.broadcasted_iota(jnp.int32, (T, T), 1)
    return ((key ^ query) & (LOCAL - 1)) == 0


def heads_forward(qkv, pair, mask, probs, result):
    for h in range(HEADS):
        queries = head_norm(qkv[head_rows(0, h), :], pair[0])[1]
        keys = head_norm(qkv[head_rows(1, h), :], pair[1])[1]
        probs[h] = dot(keys, queries, 0, 0)
    for h in range(HEADS):
        scores = probs[h] * HEAD_DIM ** (-0.5)
        if mask is not None:
            scores = jnp.where(mask, scores, -1e30)
        expo = jnp.exp(scores - jnp.max(scores, axis=0, keepdims=True))
        probs[h] = expo * (1.0 / jnp.sum(expo, axis=0, keepdims=True))
    for h in range(HEADS):
        values = qkv[head_rows(2, h), :].astype(BF)
        result[head_rows(0, h), :] = dot(values, probs[h].astype(BF), 1, 0)


def heads_back(qkv, pair, probs, grads, out, work):
    for h in range(HEADS):
        grad = grads[head_rows(0, h), :].astype(BF)
        work[h] = dot(qkv[head_rows(2, h), :].astype(BF), grad, 0, 0).astype(BF)
        out[head_rows(2, h), :] = dot(grad, probs[h].astype(BF), 1, 1).astype(BF).astype(F32)
    for h in range(HEADS):
        prob, p_grad = probs[h], work[h].astype(F32)
        inner = jnp.sum(p_grad * prob, axis=0, keepdims=True)
        work[h] = (prob * (p_grad - inner) * HEAD_DIM ** (-0.5)).astype(BF)
    for h in range(HEADS):
        queries = head_norm(qkv[head_rows(0, h), :], pair[0])[1]
        keys = head_norm(qkv[head_rows(1, h), :], pair[1])[1]
        out[head_rows(0, h), :] = dot(keys, work[h], 1, 0)
        out[head_rows(1, h), :] = dot(queries, work[h], 1, 1)
    for h in range(HEADS):
        for which in range(2):
            rows = head_rows(which, h)
            root = head_norm(qkv[rows, :], pair[which])[0]
            out[rows, :] = head_norm_back(qkv[rows, :], root, pair[which], out[rows, :])


def order(core, chip):
    row = lax.broadcasted_iota(jnp.int32, (A, 1), 0)
    part = (row >= 192).astype(jnp.int32) + (row >= 384).astype(jnp.int32)
    rest = row - 192 * part
    first = (rest * 171) >> 12
    rest = rest - 24 * first
    second = (rest * 11) >> 5
    piece = 3 * part + rest - 3 * second
    place = []
    for axis in range(3):
        step = axis - part
        step = jnp.where(step < 0, step + 3, step)
        one = jnp.where(step == 0, first >> 2, jnp.where(step == 1, first >> 1, first)) & 1
        two = (second >> (2 - axis)) & 1
        near = jnp.where(core == 1, one, two) ^ ((chip[axis] ^ (chip[axis] >> 1)) & 1)
        far = jnp.where(core == 1, two, one) ^ (chip[axis] >> 1)
        place.append(2 * far + (near ^ far))
    x, y, z = place
    device = x * 32 + (y >> 1) * 16 + core * 8 + (y & 1) * 4 + z
    return 9 * device + piece


def position():
    dp, seq = lax.axis_index("dp"), lax.axis_index("seq")
    return dp & 1, (dp >> 2, ((dp >> 1) & 1) * 2 + (seq >> 2), seq & 3)


def picker(core, chip):
    feature = lax.broadcasted_iota(jnp.int32, (A, D), 1)
    return (feature == order(core, chip)).astype(F32).astype(BF)


def pick(hot, source):
    halves = [dot(hot[k : k + STRIP], source, 1, 1).astype(BF) for k in (0, STRIP)]
    return jnp.concatenate(halves, axis=0)


def local_rows(k):
    return pl.ds(pl.multiple_of((lax.axis_index("seq") ^ PEERS[k]) * LOCAL, LOCAL), LOCAL)


def forward_spatial(*refs):
    sources, refs = refs[:7], refs[7:]
    latents, cot, mod, gains, w_qkv, w_out_t, w_out = refs[:7]
    chunks, (both_mid, qkv_t, probs_t, normed, att, scaled_t, flat, tall, both, sems) = refs[7:15], refs[15:]
    loads = {
        k: pltpu.make_async_copy(sources[k], refs[k], sems.at[k]) for k in (0, 1, 2, 3, 5, 6)
    }
    pieces = [
        pltpu.make_async_copy(
            sources[4].at[pl.ds(STRIP * k, STRIP)], w_qkv.at[pl.ds(STRIP * k, STRIP)], sems.at[7 + k]
        )
        for k in range(Q // STRIP)
    ]
    for load in (loads[0], loads[2], loads[3], *pieces, loads[1], loads[5], loads[6]):
        load.start()
    for load in (loads[0], loads[2], loads[3]):
        load.wait()
    unit, _ = normalized(latents[...].astype(F32))
    norm = (unit * (1.0 + mod[1, 0:1, :]) + mod[0, 0:1, :]).astype(BF)
    normed[...] = norm
    for k, load in enumerate(pieces):
        load.wait()
        rows = slice(STRIP * k, STRIP * k + STRIP)
        qkv_t[rows, :] = dot(w_qkv[rows, :], norm, 1, 1).astype(BF).astype(F32)
    tall[A:, :] = jnp.zeros((A_PAD - A, T), F32)
    pair = gain_columns(gains, 0)
    heads_forward(qkv_t, pair, None, probs_t, tall)
    flip_back(tall, flat, A_PAD // 128)
    att[...] = flat[...].astype(BF)
    loads[1].wait()
    scaled = (mod[2, 1:2, :] * cot[...].astype(F32)).astype(BF)
    scaled_t[...] = scaled
    loads[5].wait()
    both[:, D:] = dot(scaled, w_out_t[...], 1, 1).astype(BF)
    loads[6].wait()
    result = dot(att[:, :A], w_out[...], 1, 0)
    mid = (latents[...].astype(F32) + mod[2, 0:1, :] * result).astype(BF)
    both_mid[...] = mid
    both[:, :D] = mid
    for k in range(8):
        chunks[k][...] = both[local_rows(k), :]


def temporal(*refs):
    mod, gains, w_qkv = refs[8:11]
    normed, qkv_grad, tall_qkv, tall_grad, wide, flat, tall, tall_att, both, probs_t, work = refs[19:]
    for k in range(8):
        both[LOCAL * k : LOCAL * k + LOCAL, :] = refs[k][...]
    unit, _ = normalized(both[:, :D].astype(F32))
    norm = (unit * (1.0 + mod[1, 1:2, :]) + mod[0, 1:2, :]).astype(BF)
    normed[...] = norm
    for k in range(Q // STRIP):
        rows = slice(STRIP * k, STRIP * k + STRIP)
        tall_qkv[rows, :] = dot(w_qkv[rows, :], norm, 1, 1).astype(BF).astype(F32)
    flat[:, A:] = jnp.zeros((T, A_PAD - A), F32)
    flat[:, :A] = both[:, D:].astype(F32)
    flip(flat, tall, A_PAD // 128)
    tall_att[A:, :] = jnp.zeros((A_PAD - A, T), F32)
    tall_grad[Q:, :] = jnp.zeros((Q_PAD - Q, T), F32)
    pair = gain_columns(gains, 1)
    heads_forward(tall_qkv, pair, same_patch(), probs_t, tall_att)
    heads_back(tall_qkv, pair, probs_t, tall, tall_grad, work)
    flip_back(tall_att, flat, A_PAD // 128)
    both[:, D:] = flat[:, :A].astype(BF)
    flip_back(tall_grad, wide, Q_PAD // 128)
    qkv_grad[...] = wide[...].astype(BF)
    both[:, :D] = dot(qkv_grad[:, :Q], w_qkv[...], 1, 0).astype(BF)
    for k in range(8):
        refs[11 + k][...] = both[LOCAL * k : LOCAL * k + LOCAL, :]


def pick_early(normed, scaled, w_far, own, other, mine, theirs, w_qkv, sem):
    load = pltpu.make_async_copy(w_far, w_qkv, sem)
    load.start()
    core, chip = position()
    own[...] = picker(core, chip)
    other[...] = picker(1 - core, chip)
    for k, source in enumerate((normed, scaled)):
        rows = slice(k * A, k * A + A)
        theirs[rows, :] = pick(other[...], source[...])
        mine[rows, :] = pick(own[...], source[...])
    load.wait()


def pick_later(source, own, other, mine, theirs):
    theirs[...] = pick(other[...], source[...])
    mine[...] = pick(own[...], source[...])


def enter_spatial_back(*refs):
    mid, cot, mod, w_out, mid_grad, scaled_s, att_grad, att_t, back = refs[8:]
    for k in range(8):
        back[local_rows(k), :] = refs[k][...]
    unit, spread = normalized(mid[...].astype(F32))
    grad = normalized_back(unit, spread, mod[1, 1:2, :], back[:, :D].astype(F32))
    total = (cot[...].astype(F32) + grad).astype(BF)
    mid_grad[...] = total
    scaled = (mod[2, 0:1, :] * total.astype(F32)).astype(BF)
    scaled_s[...] = scaled
    att_grad[:, A:] = jnp.zeros((T, A_PAD - A), F32)
    att_grad[:, :A] = dot(scaled, w_out[...], 1, 1).astype(BF).astype(F32)
    att_t[:, A:] = jnp.zeros((T, A_PAD - A), BF)
    att_t[:, :A] = back[:, D:]


def spatial_attention_back(att_grad, qkv_t, probs_t, gains, qkv_grad, tall_grad, wide, tall, work):
    flip(att_grad, tall, A_PAD // 128)
    tall_grad[Q:, :] = jnp.zeros((Q_PAD - Q, T), F32)
    heads_back(qkv_t, gain_columns(gains, 0), probs_t, tall, tall_grad, work)
    flip_back(tall_grad, wide, Q_PAD // 128)
    qkv_grad[...] = wide[...].astype(BF)


def leave_spatial_back(mid_grad, qkv_grad, latents, mod, w_qkv, latents_grad):
    norm_grad = dot(qkv_grad[:, :Q], w_qkv[...], 1, 0).astype(BF).astype(F32)
    unit, spread = normalized(latents[...].astype(F32))
    grad = normalized_back(unit, spread, mod[1, 0:1, :], norm_grad)
    latents_grad[...] = (mid_grad[...].astype(F32) + grad).astype(BF)


def project_output(mid, att_t, mod, w_out, output):
    result = dot(att_t[:, :A], w_out[...], 1, 0)
    output[...] = (mid[...].astype(F32) + mod[2, 1:2, :] * result).astype(BF)


def weight_rows(groups, start):
    def body(*refs):
        keep, sends = refs[-4], refs[-3:]
        fill(refs, keep, sends, start)

    def fill(refs, keep, sends, start):
        for (left, left_in, row), (right, right_in, column), width in groups:
            lefts = [refs[k][row : row + A, :] for k in (left, left_in)]
            rights = [refs[k][:, column : column + width] for k in (right, right_in)]
            tall_left = jnp.concatenate(lefts, axis=1)
            tall_right = jnp.concatenate(rights, axis=0)
            padded = -(-width // 128) * 128
            for at in range(0, width, 576):
                size = min(576, width - at)
                total = dot(tall_left, tall_right[:, at : at + size], 1, 0)
                for p in range(3):
                    rows = total[192 * p : 192 * p + 192]
                    columns = slice(start + at, start + at + size)
                    keep[p, :, columns] = rows[:96]
                    sends[p][:, columns] = rows[96:].astype(BF)
            if padded > width:
                gap = slice(start + width, start + padded)
                for p in range(3):
                    keep[p, :, gap] = jnp.zeros((96, padded - width), F32)
                    sends[p][:, gap] = jnp.zeros((96, padded - width), BF)
            start += padded

    return body


def first_halve(p):
    def body(keep, got, kept, send):
        total = keep[p] + got[...].astype(F32)
        half = kept.shape[0]
        kept[...] = total[:half]
        send[...] = total[half:].astype(BF)

    return body


def add_halve(keep, got, kept, send):
    half = kept.shape[0]
    total = keep[...] + got[...].astype(F32)
    kept[...] = total[:half]
    send[...] = total[half:].astype(BF)


def cut_pieces(*refs):
    own, sends = refs[6], refs[7:]
    width = refs[0].shape[1]
    for p in range(3):
        total = refs[p][...] + refs[3 + p][...].astype(F32)
        columns = slice(p * width, p * width + width)
        own[:, columns] = total[:3]
        for t in range(1, 8):
            sends[t - 1][:, columns] = total[3 * t : 3 * t + 3].astype(BF)


def last_add(*refs):
    width = refs[0].shape[1] // 3
    start = 0
    for out in refs[8:]:
        size = out.shape[1]
        for p in range(3):
            columns = slice(p * width + start, p * width + start + size)
            rows = refs[0][:, columns]
            for k in range(1, 8):
                rows = rows + refs[k][:, columns].astype(F32)
            out[3 * p : 3 * p + 3, :] = rows
        start += -(-size // 128) * 128


def pairs(change):
    found = []
    for device in range(128):
        dp, seq = divmod(device, 8)
        x, y, z, core = dp >> 2, ((dp >> 1) & 1) * 2 + (seq >> 2), seq & 3, dp & 1
        x, y, z, core = change(x, y, z, core)
        found.append((device, (x * 4 + (y >> 1) * 2 + core) * 8 + (y & 1) * 4 + z))
    return found


def to_other_core(value):
    return lax.ppermute(value, MESH, pairs(lambda x, y, z, c: (x, y, z, 1 - c)))


def along(value, axis):
    def change(x, y, z, core):
        place = [x, y, z]
        place[axis] ^= 1 if core == 1 else 3
        return (*place, core)

    return lax.ppermute(value, MESH, pairs(change))


def to_frame_holders(chunks):
    def step(k):
        return lax.ppermute(chunks[k], MESH, [(d, d ^ PEERS[k]) for d in range(128)])

    return [chunks[0]] + [step(k) for k in range(1, 8)]


def to_owners(pieces):
    def step(t):
        def change(x, y, z, core):
            flip_by = 3 if core == 1 else 1
            return x ^ flip_by * (t >> 2), y ^ flip_by * (t >> 1 & 1), z ^ flip_by * (t & 1), core

        return lax.ppermute(pieces[t - 1], MESH, pairs(change))

    return [step(t) for t in (1, 7, 6, 5, 3, 4, 2)]


def weight_partials(groups, args, before=()):
    cost = sum(group[-1] for group in groups) / 1000
    outs = [((3, 96, COLUMNS), F32)] + [((96, COLUMNS), BF)] * 3
    start = Q_PAD if before else 0
    aliases = {len(args) + k: k for k in range(len(before))}
    return call(weight_rows(groups, start), outs, (*args, *before), cost, aliases=aliases)


def shards(
    latents, cotangent, modulation, qk_gains, spatial_qkv, spatial_out, temporal_qkv, temporal_out
):
    wide, tall_grad = pltpu.VMEM((T, Q_PAD), F32), pltpu.VMEM((Q_PAD, T), F32)
    flat, tall = pltpu.VMEM((T, A_PAD), F32), pltpu.VMEM((A_PAD, T), F32)
    stage, work = pltpu.VMEM((T, D + A), BF), pltpu.VMEM((HEADS, T, T), BF)
    one_block, chunk = ((A, T), BF), ((LOCAL, D + A), BF)

    x, cot, mod, gains, w_qkv_s, w_out_t, w_out_s, *rest = call(
        forward_spatial,
        [
            ((T, D), BF), ((T, D), BF), ((3, 2, D), F32), ((2, 2, HEAD_DIM), F32),
            ((Q, D), BF), ((A, D), BF), ((A, D), BF), *[chunk] * 8,
            ((T, D), BF), ((Q, T), F32), ((HEADS, T, T), F32),
            ((T, D), BF), ((T, A_PAD), BF), ((T, D), BF),
        ],
        (
            latents.reshape(T, D), cotangent.reshape(T, D), modulation[0].transpose(1, 0, 2), qk_gains,
            spatial_qkv.T, temporal_out, spatial_out,
        ),
        10,
        (flat, tall, stage, pltpu.SemaphoreType.DMA((13,))),
        limit=18,
        apart=range(7),
    )
    mid, qkv_t, probs_t, normed_s, att_s, scaled_t = rest[8:]
    patch = to_frame_holders(rest[:8])
    att_s_in = to_other_core(att_s)
    own, other, early_mine, early_theirs, w_qkv_t = call(
        pick_early,
        [((A, D), BF), ((A, D), BF), ((2 * A, T), BF), ((2 * A, T), BF), ((Q, D), BF)],
        (normed_s, scaled_t, temporal_qkv.T),
        2.8,
        (pltpu.SemaphoreType.DMA(()),),
        apart=(2,),
    )
    *patch, early_mine, early_theirs, att_s_in = in_order(
        *patch, early_mine, early_theirs, att_s_in
    )
    early_in = to_other_core(early_theirs)

    *back, normed_t, qkv_grad_t = call(
        temporal,
        [*[chunk] * 8, ((T, D), BF), ((T, Q_PAD), BF)],
        (*patch, mod, gains, w_qkv_t),
        10,
        (
            pltpu.VMEM((Q, T), F32), tall_grad, wide, flat, tall, tall, stage,
            pltpu.VMEM((HEADS, T, T), F32), work,
        ),
        limit=24,
    )
    back = to_frame_holders(back)
    t_mine, t_theirs = call(pick_later, [one_block] * 2, (normed_t, own, other), 1)
    *back, t_theirs, early_theirs, qkv_grad_t = in_order(
        *back, t_theirs, early_theirs, qkv_grad_t
    )
    early_in = to_other_core(early_theirs)
    t_in, qkv_grad_t_in = to_other_core(t_theirs), to_other_core(qkv_grad_t)

    mid_grad, scaled_s, att_grad_s, att_t = call(
        enter_spatial_back,
        [((T, D), BF), ((T, D), BF), ((T, A_PAD), F32), ((T, A_PAD), BF)],
        (*back, mid, cot, mod, w_out_s),
        1.5,
        (stage,),
    )
    att_t_in = to_other_core(att_t)
    (qkv_grad_s,) = call(
        spatial_attention_back,
        [((T, Q_PAD), BF)],
        (att_grad_s, qkv_t, probs_t, gains),
        2.9,
        (tall_grad, wide, tall, work),
    )
    qkv_grad_s, scaled_s, t_in, qkv_grad_t_in, att_t_in = in_order(
        qkv_grad_s, scaled_s, t_in, qkv_grad_t_in, att_t_in
    )
    qkv_grad_s_in = to_other_core(qkv_grad_s)
    late_mine, late_theirs = call(pick_later, [one_block] * 2, (scaled_s, own, other), 1)
    late_in = to_other_core(late_theirs)
    partials = weight_partials(
        (((0, 1, 0), (2, 3, 0), Q),), (t_mine, t_in, qkv_grad_t, qkv_grad_t_in)
    )
    *partials, qkv_grad_s_in, late_in = in_order(*partials, qkv_grad_s_in, late_in)
    keep, *sends = weight_partials(
        (
            ((0, 1, 0), (2, 3, 0), Q), ((0, 1, A), (4, 5, 0), A), ((6, 7, 0), (8, 9, 0), A),
        ),
        (
            early_mine, early_in, qkv_grad_s, qkv_grad_s_in, att_t, att_t_in, late_mine, late_in,
            att_s, att_s_in,
        ),
        partials,
    )
    keep, att_t, mid_grad, *sends = in_order(keep, att_t, mid_grad, *sends)
    got = [along(sends[p], p) for p in range(3)]
    (output,) = call(project_output, [((T, D), BF, "any")], (mid, att_t, mod, w_out_t), 1.5)
    (latents_grad,) = call(
        leave_spatial_back, [((T, D), BF, "any")], (mid_grad, qkv_grad_s, x, mod, w_qkv_s), 2.7
    )
    keep, output, latents_grad = in_order(keep, output, latents_grad)

    kept = []
    for p in range(3):
        mine, send = call(
            first_halve(p), [((48, COLUMNS), F32), ((48, COLUMNS), BF)], (keep, got[p]), 0.2
        )
        kept.append(mine)
        got[p] = along(send, (p + 1) % 3)
    for p in range(3):
        kept[p], send = call(
            add_halve, [((24, COLUMNS), F32), ((24, COLUMNS), BF)], (kept[p], got[p]), 0.2
        )
        got[p] = along(send, (p + 2) % 3)
    own_piece, *pieces = call(
        cut_pieces, [((3, 3 * COLUMNS), F32)] + [((3, 3 * COLUMNS), BF)] * 7, (*kept, *got), 0.5
    )
    tq, sq, to, so = call(
        last_add,
        [((9, Q), F32, "any"), ((9, Q), F32, "any"), ((9, A), F32, "any"), ((9, A), F32, "any")],
        (own_piece, *to_owners(pieces)),
        1,
    )
    shape = (1, 1, T, D)
    return output.reshape(shape), latents_grad.reshape(shape), sq, so.T, tq, to.T


def solution(mesh):
    tokens = P("dp", "seq", None, None)
    rows, cols = P(("dp", "seq"), None), P(None, ("dp", "seq"))
    return jax.shard_map(
        shards,
        mesh=mesh,
        in_specs=(tokens, tokens, P("dp", None, None, None), P(), P(), P(), P(), P()),
        out_specs=(tokens, tokens, rows, cols, rows, cols),
        check_vma=False,
    )
```

```python
import math

import jax
import jax.numpy as jnp
from jax import lax
from jax.experimental import pallas as pl
from jax.experimental.pallas import tpu as pltpu
from jax.sharding import PartitionSpec as P

T = 256
D = 1152
HEADS = 8
HEAD_DIM = 72
A = HEADS * HEAD_DIM
Q = 3 * A
A_PAD = 640
Q_PAD = 1792
COLUMNS = 2 * Q + 2 * A
LOCAL = 32
STRIP = 288
EPS = 1e-06
BF = jnp.bfloat16
F32 = jnp.float32
MESH = ("dp", "seq")
MIB = 1024 * 1024
PEERS = (0, 6, 5, 7, 4, 2, 1, 3)


def dot(left, right, over_left, over_right):
    return lax.dot_general(
        left, right, (((over_left,), (over_right,)), ((), ())), preferred_element_type=F32
    )


def call(body, outs, args, cost, scratch=(), limit=16, apart=(), aliases={}):
    shapes, specs = [], []
    for k, (shape, kind, *place) in enumerate(outs):
        if not place:
            shapes.append(pltpu.VMEM(shape, kind))
        elif place[0] == "hbm":
            shapes.append(pltpu.HBM(shape, kind))
        else:
            shapes.append(jax.ShapeDtypeStruct(shape, kind))
        specs.append(pl.BlockSpec(memory_space=pltpu.HBM if place == ["hbm"] else pltpu.VMEM))
    size = sum(x.size * x.dtype.itemsize for x in args)
    size += sum(math.prod(out[0]) * jnp.dtype(out[1]).itemsize for out in outs)
    args = [
        pltpu.with_memory_space_constraint(x, pltpu.HBM) if k in apart else x
        for k, x in enumerate(args)
    ]
    spaces = [pltpu.HBM if k in apart else pltpu.VMEM for k in range(len(args))]
    return pl.pallas_call(
        body,
        out_shape=tuple(shapes),
        in_specs=[pl.BlockSpec(memory_space=space) for space in spaces],
        out_specs=tuple(specs),
        scratch_shapes=list(scratch),
        input_output_aliases=aliases,
        cost_estimate=pl.CostEstimate(
            flops=int(cost * 1.1e9), bytes_accessed=size, transcendentals=0
        ),
        compiler_params=pltpu.CompilerParams(vmem_limit_bytes=limit * MIB),
    )(*args)


def in_order(*values):
    return lax.optimization_barrier(values)


def normalized(x32):
    mean = jnp.mean(x32, axis=-1, keepdims=True)
    centered = x32 - mean
    spread = lax.rsqrt(jnp.mean(centered * centered, axis=-1, keepdims=True) + EPS)
    return centered * spread, spread


def normalized_back(unit, spread, scale, grad):
    grad = grad * (1.0 + scale)
    inner = jnp.mean(grad * unit, axis=-1, keepdims=True)
    return spread * (grad - jnp.mean(grad, axis=-1, keepdims=True) - unit * inner)


def flip(source, target, blocks):
    for b in range(blocks):
        target[128 * b : 128 * b + 128, :] = source[:, 128 * b : 128 * b + 128].T


def flip_back(source, target, blocks):
    for b in range(blocks):
        target[:, 128 * b : 128 * b + 128] = source[128 * b : 128 * b + 128, :].T


def gain_columns(gains, block):
    row = lax.broadcasted_iota(jnp.int32, (HEAD_DIM, HEAD_DIM), 0)
    column = lax.broadcasted_iota(jnp.int32, (HEAD_DIM, HEAD_DIM), 1)
    return tuple(
        jnp.sum(jnp.where(row == column, gains[block, k : k + 1, :], 0.0), axis=1, keepdims=True)
        for k in range(2)
    )


def head_rows(which, h):
    start = which * A + h * HEAD_DIM
    return slice(start, start + HEAD_DIM)


def head_norm(rows, gain):
    root = lax.rsqrt(jnp.mean(rows * rows, axis=0, keepdims=True) + EPS)
    return root, (rows * root * gain).astype(BF)


def head_norm_back(rows, root, gain, grad):
    grad = grad.astype(BF).astype(F32) * gain
    inner = jnp.mean(rows * grad, axis=0, keepdims=True)
    return (root * grad - rows * (root * root * root * inner)).astype(BF).astype(F32)


def same_patch():
    key = lax.broadcasted_iota(jnp.int32, (T, T), 0)
    query = lax.broadcasted_iota(jnp.int32, (T, T), 1)
    return ((key ^ query) & (LOCAL - 1)) == 0


def heads_forward(qkv, pair, mask, probs, result):
    for h in range(HEADS):
        queries = head_norm(qkv[head_rows(0, h), :], pair[0])[1]
        keys = head_norm(qkv[head_rows(1, h), :], pair[1])[1]
        probs[h] = dot(keys, queries, 0, 0)
    for h in range(HEADS):
        scores = probs[h] * HEAD_DIM ** (-0.5)
        if mask is not None:
            scores = jnp.where(mask, scores, -1e30)
        expo = jnp.exp(scores - jnp.max(scores, axis=0, keepdims=True))
        probs[h] = expo * (1.0 / jnp.sum(expo, axis=0, keepdims=True))
    for h in range(HEADS):
        values = qkv[head_rows(2, h), :].astype(BF)
        result[head_rows(0, h), :] = dot(values, probs[h].astype(BF), 1, 0)


def heads_back(qkv, pair, probs, grads, out, work):
    for h in range(HEADS):
        grad = grads[head_rows(0, h), :].astype(BF)
        work[h] = dot(qkv[head_rows(2, h), :].astype(BF), grad, 0, 0).astype(BF)
        out[head_rows(2, h), :] = dot(grad, probs[h].astype(BF), 1, 1).astype(BF).astype(F32)
    for h in range(HEADS):
        prob, p_grad = probs[h], work[h].astype(F32)
        inner = jnp.sum(p_grad * prob, axis=0, keepdims=True)
        work[h] = (prob * (p_grad - inner) * HEAD_DIM ** (-0.5)).astype(BF)
    for h in range(HEADS):
        queries = head_norm(qkv[head_rows(0, h), :], pair[0])[1]
        keys = head_norm(qkv[head_rows(1, h), :], pair[1])[1]
        out[head_rows(0, h), :] = dot(keys, work[h], 1, 0)
        out[head_rows(1, h), :] = dot(queries, work[h], 1, 1)
    for h in range(HEADS):
        for which in range(2):
            rows = head_rows(which, h)
            root = head_norm(qkv[rows, :], pair[which])[0]
            out[rows, :] = head_norm_back(qkv[rows, :], root, pair[which], out[rows, :])


def order(core, chip):
    row = lax.broadcasted_iota(jnp.int32, (A, 1), 0)
    part = (row >= 192).astype(jnp.int32) + (row >= 384).astype(jnp.int32)
    rest = row - 192 * part
    first = (rest * 171) >> 12
    rest = rest - 24 * first
    second = (rest * 11) >> 5
    piece = 3 * part + rest - 3 * second
    place = []
    for axis in range(3):
        step = axis - part
        step = jnp.where(step < 0, step + 3, step)
        one = jnp.where(step == 0, first >> 2, jnp.where(step == 1, first >> 1, first)) & 1
        two = (second >> (2 - axis)) & 1
        near = jnp.where(core == 1, one, two) ^ ((chip[axis] ^ (chip[axis] >> 1)) & 1)
        far = jnp.where(core == 1, two, one) ^ (chip[axis] >> 1)
        place.append(2 * far + (near ^ far))
    x, y, z = place
    device = x * 32 + (y >> 1) * 16 + core * 8 + (y & 1) * 4 + z
    return 9 * device + piece


def position():
    dp, seq = lax.axis_index("dp"), lax.axis_index("seq")
    return dp & 1, (dp >> 2, ((dp >> 1) & 1) * 2 + (seq >> 2), seq & 3)


def picker(core, chip):
    feature = lax.broadcasted_iota(jnp.int32, (A, D), 1)
    return (feature == order(core, chip)).astype(F32).astype(BF)


def pick(hot, source):
    halves = [dot(hot[k : k + STRIP], source, 1, 1).astype(BF) for k in (0, STRIP)]
    return jnp.concatenate(halves, axis=0)


def local_rows(k):
    return pl.ds(pl.multiple_of((lax.axis_index("seq") ^ PEERS[k]) * LOCAL, LOCAL), LOCAL)


def forward_spatial(*refs):
    sources, refs = refs[:7], refs[7:]
    latents, cot, mod, gains, w_qkv, w_out_t, w_out = refs[:7]
    chunks, (both_mid, qkv_t, probs_t, normed, att, scaled_t, flat, tall, both, sems) = refs[7:15], refs[15:]
    loads = {
        k: pltpu.make_async_copy(sources[k], refs[k], sems.at[k]) for k in (0, 1, 2, 3, 5, 6)
    }
    pieces = [
        pltpu.make_async_copy(
            sources[4].at[pl.ds(STRIP * k, STRIP)], w_qkv.at[pl.ds(STRIP * k, STRIP)], sems.at[7 + k]
        )
        for k in range(Q // STRIP)
    ]
    for load in (loads[0], loads[2], loads[3], *pieces, loads[1], loads[5], loads[6]):
        load.start()
    for load in (loads[0], loads[2], loads[3]):
        load.wait()
    unit, _ = normalized(latents[...].astype(F32))
    norm = (unit * (1.0 + mod[1, 0:1, :]) + mod[0, 0:1, :]).astype(BF)
    normed[...] = norm
    for k, load in enumerate(pieces):
        load.wait()
        rows = slice(STRIP * k, STRIP * k + STRIP)
        qkv_t[rows, :] = dot(w_qkv[rows, :], norm, 1, 1).astype(BF).astype(F32)
    tall[A:, :] = jnp.zeros((A_PAD - A, T), F32)
    pair = gain_columns(gains, 0)
    heads_forward(qkv_t, pair, None, probs_t, tall)
    flip_back(tall, flat, A_PAD // 128)
    att[...] = flat[...].astype(BF)
    loads[1].wait()
    scaled = (mod[2, 1:2, :] * cot[...].astype(F32)).astype(BF)
    scaled_t[...] = scaled
    loads[5].wait()
    both[:, D:] = dot(scaled, w_out_t[...], 1, 1).astype(BF)
    loads[6].wait()
    result = dot(att[:, :A], w_out[...], 1, 0)
    mid = (latents[...].astype(F32) + mod[2, 0:1, :] * result).astype(BF)
    both_mid[...] = mid
    both[:, :D] = mid
    for k in range(8):
        chunks[k][...] = both[local_rows(k), :]


def temporal(*refs):
    mod, gains, w_qkv = refs[8:11]
    normed, qkv_grad, tall_qkv, tall_grad, wide, flat, tall, tall_att, both, probs_t, work = refs[19:]
    for k in range(8):
        both[LOCAL * k : LOCAL * k + LOCAL, :] = refs[k][...]
    unit, _ = normalized(both[:, :D].astype(F32))
    norm = (unit * (1.0 + mod[1, 1:2, :]) + mod[0, 1:2, :]).astype(BF)
    normed[...] = norm
    for k in range(Q // STRIP):
        rows = slice(STRIP * k, STRIP * k + STRIP)
        tall_qkv[rows, :] = dot(w_qkv[rows, :], norm, 1, 1).astype(BF).astype(F32)
    flat[:, A:] = jnp.zeros((T, A_PAD - A), F32)
    flat[:, :A] = both[:, D:].astype(F32)
    flip(flat, tall, A_PAD // 128)
    tall_att[A:, :] = jnp.zeros((A_PAD - A, T), F32)
    tall_grad[Q:, :] = jnp.zeros((Q_PAD - Q, T), F32)
    pair = gain_columns(gains, 1)
    heads_forward(tall_qkv, pair, same_patch(), probs_t, tall_att)
    heads_back(tall_qkv, pair, probs_t, tall, tall_grad, work)
    flip_back(tall_att, flat, A_PAD // 128)
    both[:, D:] = flat[:, :A].astype(BF)
    flip_back(tall_grad, wide, Q_PAD // 128)
    qkv_grad[...] = wide[...].astype(BF)
    both[:, :D] = dot(qkv_grad[:, :Q], w_qkv[...], 1, 0).astype(BF)
    for k in range(8):
        refs[11 + k][...] = both[LOCAL * k : LOCAL * k + LOCAL, :]


def pick_early(normed, scaled, w_far, own, other, mine, theirs, w_qkv, sem):
    load = pltpu.make_async_copy(w_far, w_qkv, sem)
    load.start()
    core, chip = position()
    own[...] = picker(core, chip)
    other[...] = picker(1 - core, chip)
    for k, source in enumerate((normed, scaled)):
        rows = slice(k * A, k * A + A)
        theirs[rows, :] = pick(other[...], source[...])
        mine[rows, :] = pick(own[...], source[...])
    load.wait()


def pick_later(source, own, other, mine, theirs):
    theirs[...] = pick(other[...], source[...])
    mine[...] = pick(own[...], source[...])


def enter_spatial_back(*refs):
    mid, cot, mod, w_out, own, other, mid_grad, att_grad, att_t, mine, theirs, back = refs[8:]
    for k in range(8):
        back[local_rows(k), :] = refs[k][...]
    unit, spread = normalized(mid[...].astype(F32))
    grad = normalized_back(unit, spread, mod[1, 1:2, :], back[:, :D].astype(F32))
    total = (cot[...].astype(F32) + grad).astype(BF)
    mid_grad[...] = total
    scaled = (mod[2, 0:1, :] * total.astype(F32)).astype(BF)
    theirs[...] = pick(other[...], scaled)
    mine[...] = pick(own[...], scaled)
    att_grad[:, A:] = jnp.zeros((T, A_PAD - A), F32)
    att_grad[:, :A] = dot(scaled, w_out[...], 1, 1).astype(BF).astype(F32)
    att_t[:, A:] = jnp.zeros((T, A_PAD - A), BF)
    att_t[:, :A] = back[:, D:]


def spatial_attention_back(att_grad, qkv_t, probs_t, gains, qkv_grad, tall_grad, wide, tall, work):
    flip(att_grad, tall, A_PAD // 128)
    tall_grad[Q:, :] = jnp.zeros((Q_PAD - Q, T), F32)
    heads_back(qkv_t, gain_columns(gains, 0), probs_t, tall, tall_grad, work)
    flip_back(tall_grad, wide, Q_PAD // 128)
    qkv_grad[...] = wide[...].astype(BF)


def leave_spatial_back(mid_grad, qkv_grad, latents, mod, w_qkv, latents_grad):
    norm_grad = dot(qkv_grad[:, :Q], w_qkv[...], 1, 0).astype(BF).astype(F32)
    unit, spread = normalized(latents[...].astype(F32))
    grad = normalized_back(unit, spread, mod[1, 0:1, :], norm_grad)
    latents_grad[...] = (mid_grad[...].astype(F32) + grad).astype(BF)


def project_output(mid, att_t, mod, w_out, output):
    result = dot(att_t[:, :A], w_out[...], 1, 0)
    output[...] = (mid[...].astype(F32) + mod[2, 1:2, :] * result).astype(BF)


def weight_rows(groups):
    def body(*refs):
        keep, sends = refs[-4], refs[-3:]
        for (left, left_in, row), (right, right_in, column), width, start in groups:
            lefts = [refs[k][row : row + A, :] for k in (left, left_in)]
            rights = [refs[k][:, column : column + width] for k in (right, right_in)]
            tall_left = jnp.concatenate(lefts, axis=1)
            tall_right = jnp.concatenate(rights, axis=0)
            for at in range(0, width, 576):
                size = min(576, width - at)
                total = dot(tall_left, tall_right[:, at : at + size], 1, 0)
                for p in range(3):
                    rows = total[192 * p : 192 * p + 192]
                    columns = slice(start + at, start + at + size)
                    keep[p, :, columns] = rows[:96]
                    sends[p][:, columns] = rows[96:].astype(BF)

    return body


def first_halve(p):
    def body(keep, got, kept, send):
        half = kept.shape[0]
        total = keep[p] + got[...].astype(F32)
        kept[...] = total[:half]
        send[...] = total[half:].astype(BF)

    return body


def add_halve(keep, got, kept, send):
    half = kept.shape[0]
    total = keep[...] + got[...].astype(F32)
    kept[...] = total[:half]
    send[...] = total[half:].astype(BF)


def cut_pieces(*refs):
    own, sends = refs[6], refs[7:]
    width = refs[0].shape[1]
    for p in range(3):
        total = refs[p][...] + refs[3 + p][...].astype(F32)
        columns = slice(p * width, p * width + width)
        own[:, columns] = total[:3]
        for t in range(1, 8):
            sends[t - 1][:, columns] = total[3 * t : 3 * t + 3].astype(BF)


def last_add(*refs):
    width = refs[0].shape[1] // 3
    start = 0
    for out in refs[8:]:
        size = out.shape[1]
        for p in range(3):
            columns = slice(p * width + start, p * width + start + size)
            rows = refs[0][:, columns]
            for k in range(1, 8):
                rows = rows + refs[k][:, columns].astype(F32)
            out[3 * p : 3 * p + 3, :] = rows
        start += size


def pairs(change):
    found = []
    for device in range(128):
        dp, seq = divmod(device, 8)
        x, y, z, core = dp >> 2, ((dp >> 1) & 1) * 2 + (seq >> 2), seq & 3, dp & 1
        x, y, z, core = change(x, y, z, core)
        found.append((device, (x * 4 + (y >> 1) * 2 + core) * 8 + (y & 1) * 4 + z))
    return found


def to_other_core(value):
    return lax.ppermute(value, MESH, pairs(lambda x, y, z, c: (x, y, z, 1 - c)))


def along(value, axis):
    def change(x, y, z, core):
        place = [x, y, z]
        place[axis] ^= 1 if core == 1 else 3
        return (*place, core)

    return lax.ppermute(value, MESH, pairs(change))


def to_frame_holders(chunks):
    def step(k):
        return lax.ppermute(chunks[k], MESH, [(d, d ^ PEERS[k]) for d in range(128)])

    return [chunks[0]] + [step(k) for k in range(1, 8)]


def to_owners(pieces):
    def step(t):
        def change(x, y, z, core):
            flip_by = 3 if core == 1 else 1
            return x ^ flip_by * (t >> 2), y ^ flip_by * (t >> 1 & 1), z ^ flip_by * (t & 1), core

        return lax.ppermute(pieces[t - 1], MESH, pairs(change))

    return [step(t) for t in (1, 7, 6, 5, 3, 4, 2)]


def weight_partials(groups, args, before=()):
    cost = sum(group[2] for group in groups) / 1100
    outs = [((3, 96, COLUMNS), F32)] + [((96, COLUMNS), BF)] * 3
    aliases = {len(args) + k: k for k in range(len(before))}
    return call(weight_rows(groups), outs, (*args, *before), cost, aliases=aliases)


def shards(
    latents, cotangent, modulation, qk_gains, spatial_qkv, spatial_out, temporal_qkv, temporal_out
):
    wide, tall_grad = pltpu.VMEM((T, Q_PAD), F32), pltpu.VMEM((Q_PAD, T), F32)
    flat, tall = pltpu.VMEM((T, A_PAD), F32), pltpu.VMEM((A_PAD, T), F32)
    stage, work = pltpu.VMEM((T, D + A), BF), pltpu.VMEM((HEADS, T, T), BF)
    one_block, chunk = ((A, T), BF), ((LOCAL, D + A), BF)

    x, cot, mod, gains, w_qkv_s, w_out_t, w_out_s, *rest = call(
        forward_spatial,
        [
            ((T, D), BF), ((T, D), BF), ((3, 2, D), F32), ((2, 2, HEAD_DIM), F32),
            ((Q, D), BF), ((A, D), BF), ((A, D), BF), *[chunk] * 8,
            ((T, D), BF), ((Q, T), F32), ((HEADS, T, T), F32),
            ((T, D), BF), ((T, A_PAD), BF), ((T, D), BF),
        ],
        (
            latents.reshape(T, D), cotangent.reshape(T, D), modulation[0].transpose(1, 0, 2), qk_gains,
            spatial_qkv.T, temporal_out, spatial_out,
        ),
        10,
        (flat, tall, stage, pltpu.SemaphoreType.DMA((13,))),
        limit=18,
        apart=range(7),
    )
    mid, qkv_t, probs_t, normed_s, att_s, scaled_t = rest[8:]
    patch = to_frame_holders(rest[:8])
    att_s_in = to_other_core(att_s)
    own, other, early_mine, early_theirs, w_qkv_t = call(
        pick_early,
        [((A, D), BF), ((A, D), BF), ((2 * A, T), BF), ((2 * A, T), BF), ((Q, D), BF)],
        (normed_s, scaled_t, temporal_qkv.T),
        2.8,
        (pltpu.SemaphoreType.DMA(()),),
        apart=(2,),
    )
    *patch, early_mine, early_theirs, att_s_in = in_order(
        *patch, early_mine, early_theirs, att_s_in
    )
    early_in = to_other_core(early_theirs)

    *back, normed_t, qkv_grad_t = call(
        temporal,
        [*[chunk] * 8, ((T, D), BF), ((T, Q_PAD), BF)],
        (*patch, mod, gains, w_qkv_t),
        10,
        (
            pltpu.VMEM((Q, T), F32), tall_grad, wide, flat, tall, tall, stage,
            pltpu.VMEM((HEADS, T, T), F32), work,
        ),
        limit=24,
    )
    back = to_frame_holders(back)
    t_mine, t_theirs = call(pick_later, [one_block] * 2, (normed_t, own, other), 1)
    *back, t_theirs, early_theirs, qkv_grad_t = in_order(
        *back, t_theirs, early_theirs, qkv_grad_t
    )
    early_in = to_other_core(early_theirs)
    t_in, qkv_grad_t_in = to_other_core(t_theirs), to_other_core(qkv_grad_t)

    mid_grad, att_grad_s, att_t, late_mine, late_theirs = call(
        enter_spatial_back,
        [((T, D), BF), ((T, A_PAD), F32), ((T, A_PAD), BF), one_block, one_block],
        (*back, mid, cot, mod, w_out_s, own, other),
        2.4,
        (stage,),
    )
    att_t_in, late_in = to_other_core(att_t), to_other_core(late_theirs)
    (qkv_grad_s,) = call(
        spatial_attention_back,
        [((T, Q_PAD), BF)],
        (att_grad_s, qkv_t, probs_t, gains),
        2,
        (tall_grad, wide, tall, work),
    )
    qkv_grad_s, late_in, t_in, qkv_grad_t_in, att_t_in, early_in = in_order(
        qkv_grad_s, late_in, t_in, qkv_grad_t_in, att_t_in, early_in
    )
    qkv_grad_s_in = to_other_core(qkv_grad_s)
    partials = weight_partials(
        (
            ((0, 1, 0), (2, 3, 0), Q, 0), ((4, 5, A), (6, 7, 0), A, Q),
            ((8, 9, 0), (10, 11, 0), A, 2 * Q + A),
        ),
        (
            t_mine, t_in, qkv_grad_t, qkv_grad_t_in, early_mine, early_in, att_t, att_t_in,
            late_mine, late_in, att_s, att_s_in,
        ),
    )
    *partials, qkv_grad_s_in = in_order(*partials, qkv_grad_s_in)
    keep, *sends = weight_partials(
        (((0, 1, 0), (2, 3, 0), Q, Q + A),),
        (early_mine, early_in, qkv_grad_s, qkv_grad_s_in),
        partials,
    )
    keep, att_t, mid_grad, *sends = in_order(keep, att_t, mid_grad, *sends)
    got = [along(sends[p], p) for p in range(3)]
    (output,) = call(project_output, [((T, D), BF, "any")], (mid, att_t, mod, w_out_t), 1.5)
    (latents_grad,) = call(
        leave_spatial_back, [((T, D), BF, "any")], (mid_grad, qkv_grad_s, x, mod, w_qkv_s), 2.7
    )
    keep, output, latents_grad = in_order(keep, output, latents_grad)
    kept = []
    for p in range(3):
        mine, send = call(
            first_halve(p), [((48, COLUMNS), F32), ((48, COLUMNS), BF)], (keep, got[p]), 0.2
        )
        kept.append(mine)
        got[p] = along(send, (p + 1) % 3)
    for p in range(3):
        kept[p], send = call(
            add_halve, [((24, COLUMNS), F32), ((24, COLUMNS), BF)], (kept[p], got[p]), 0.2
        )
        got[p] = along(send, (p + 2) % 3)
    own_piece, *pieces = call(
        cut_pieces, [((3, 3 * COLUMNS), F32)] + [((3, 3 * COLUMNS), BF)] * 7, (*kept, *got), 0.5
    )
    tq, to, sq, so = call(
        last_add,
        [((9, Q), F32, "any"), ((9, A), F32, "any"), ((9, Q), F32, "any"), ((9, A), F32, "any")],
        (own_piece, *to_owners(pieces)),
        1,
    )
    shape = (1, 1, T, D)
    return output.reshape(shape), latents_grad.reshape(shape), sq, so.T, tq, to.T


def solution(mesh):
    tokens = P("dp", "seq", None, None)
    rows, cols = P(("dp", "seq"), None), P(None, ("dp", "seq"))
    return jax.shard_map(
        shards,
        mesh=mesh,
        in_specs=(tokens, tokens, P("dp", None, None, None), P(), P(), P(), P(), P()),
        out_specs=(tokens, tokens, rows, cols, rows, cols),
        check_vma=False,
    )
```

```python
import math

import jax
import jax.numpy as jnp
from jax import lax
from jax.experimental import pallas as pl
from jax.experimental.pallas import tpu as pltpu
from jax.sharding import PartitionSpec as P

T = 256
D = 1152
HEADS = 8
HEAD_DIM = 72
A = HEADS * HEAD_DIM
Q = 3 * A
A_PAD = 640
Q_PAD = 1792
COLUMNS = 2 * Q + 2 * A
LOCAL = 32
STRIP = 288
EPS = 1e-06
BF = jnp.bfloat16
F32 = jnp.float32
MESH = ("dp", "seq")
MIB = 1024 * 1024
PEERS = (0, 6, 5, 7, 4, 2, 1, 3)


def dot(left, right, over_left, over_right):
    return lax.dot_general(
        left, right, (((over_left,), (over_right,)), ((), ())), preferred_element_type=F32
    )


def call(body, outs, args, cost, scratch=(), limit=16, apart=(), aliases={}):
    shapes, specs = [], []
    for k, (shape, kind, *place) in enumerate(outs):
        if not place:
            shapes.append(pltpu.VMEM(shape, kind))
        elif place[0] == "hbm":
            shapes.append(pltpu.HBM(shape, kind))
        else:
            shapes.append(jax.ShapeDtypeStruct(shape, kind))
        specs.append(pl.BlockSpec(memory_space=pltpu.HBM if place == ["hbm"] else pltpu.VMEM))
    size = sum(x.size * x.dtype.itemsize for x in args)
    size += sum(math.prod(out[0]) * jnp.dtype(out[1]).itemsize for out in outs)
    args = [
        pltpu.with_memory_space_constraint(x, pltpu.HBM) if k in apart else x
        for k, x in enumerate(args)
    ]
    spaces = [pltpu.HBM if k in apart else pltpu.VMEM for k in range(len(args))]
    return pl.pallas_call(
        body,
        out_shape=tuple(shapes),
        in_specs=[pl.BlockSpec(memory_space=space) for space in spaces],
        out_specs=tuple(specs),
        scratch_shapes=list(scratch),
        input_output_aliases=aliases,
        cost_estimate=pl.CostEstimate(
            flops=int(cost * 1.1e9), bytes_accessed=size, transcendentals=0
        ),
        compiler_params=pltpu.CompilerParams(vmem_limit_bytes=limit * MIB),
    )(*args)


def in_order(*values):
    return lax.optimization_barrier(values)


def normalized(x32):
    mean = jnp.mean(x32, axis=-1, keepdims=True)
    centered = x32 - mean
    spread = lax.rsqrt(jnp.mean(centered * centered, axis=-1, keepdims=True) + EPS)
    return centered * spread, spread


def normalized_back(unit, spread, scale, grad):
    grad = grad * (1.0 + scale)
    inner = jnp.mean(grad * unit, axis=-1, keepdims=True)
    return spread * (grad - jnp.mean(grad, axis=-1, keepdims=True) - unit * inner)


def flip(source, target, blocks):
    for b in range(blocks):
        target[128 * b : 128 * b + 128, :] = source[:, 128 * b : 128 * b + 128].T


def flip_back(source, target, blocks):
    for b in range(blocks):
        target[:, 128 * b : 128 * b + 128] = source[128 * b : 128 * b + 128, :].T


def gain_columns(gains, block):
    row = lax.broadcasted_iota(jnp.int32, (HEAD_DIM, HEAD_DIM), 0)
    column = lax.broadcasted_iota(jnp.int32, (HEAD_DIM, HEAD_DIM), 1)
    return tuple(
        jnp.sum(jnp.where(row == column, gains[block, k : k + 1, :], 0.0), axis=1, keepdims=True)
        for k in range(2)
    )


def head_rows(which, h):
    start = which * A + h * HEAD_DIM
    return slice(start, start + HEAD_DIM)


def head_norm(rows, gain):
    root = lax.rsqrt(jnp.mean(rows * rows, axis=0, keepdims=True) + EPS)
    return root, (rows * root * gain).astype(BF)


def head_norm_back(rows, root, gain, grad):
    grad = grad.astype(BF).astype(F32) * gain
    inner = jnp.mean(rows * grad, axis=0, keepdims=True)
    return (root * grad - rows * (root * root * root * inner)).astype(BF).astype(F32)


def same_patch():
    key = lax.broadcasted_iota(jnp.int32, (T, T), 0)
    query = lax.broadcasted_iota(jnp.int32, (T, T), 1)
    return ((key ^ query) & (LOCAL - 1)) == 0


def heads_forward(qkv, pair, mask, probs, result):
    for h in range(HEADS):
        queries = head_norm(qkv[head_rows(0, h), :], pair[0])[1]
        keys = head_norm(qkv[head_rows(1, h), :], pair[1])[1]
        probs[h] = dot(keys, queries, 0, 0)
    for h in range(HEADS):
        scores = probs[h] * HEAD_DIM ** (-0.5)
        if mask is not None:
            scores = jnp.where(mask, scores, -1e30)
        expo = jnp.exp(scores - jnp.max(scores, axis=0, keepdims=True))
        probs[h] = expo * (1.0 / jnp.sum(expo, axis=0, keepdims=True))
    for h in range(HEADS):
        values = qkv[head_rows(2, h), :].astype(BF)
        result[head_rows(0, h), :] = dot(values, probs[h].astype(BF), 1, 0)


def heads_back(qkv, pair, probs, grads, out, work):
    for h in range(HEADS):
        grad = grads[head_rows(0, h), :].astype(BF)
        work[h] = dot(qkv[head_rows(2, h), :].astype(BF), grad, 0, 0).astype(BF)
        out[head_rows(2, h), :] = dot(grad, probs[h].astype(BF), 1, 1).astype(BF).astype(F32)
    for h in range(HEADS):
        prob, p_grad = probs[h], work[h].astype(F32)
        inner = jnp.sum(p_grad * prob, axis=0, keepdims=True)
        work[h] = (prob * (p_grad - inner) * HEAD_DIM ** (-0.5)).astype(BF)
    for h in range(HEADS):
        queries = head_norm(qkv[head_rows(0, h), :], pair[0])[1]
        keys = head_norm(qkv[head_rows(1, h), :], pair[1])[1]
        out[head_rows(0, h), :] = dot(keys, work[h], 1, 0)
        out[head_rows(1, h), :] = dot(queries, work[h], 1, 1)
    for h in range(HEADS):
        for which in range(2):
            rows = head_rows(which, h)
            root = head_norm(qkv[rows, :], pair[which])[0]
            out[rows, :] = head_norm_back(qkv[rows, :], root, pair[which], out[rows, :])


def order(core, chip):
    row = lax.broadcasted_iota(jnp.int32, (A, 1), 0)
    part = (row >= 192).astype(jnp.int32) + (row >= 384).astype(jnp.int32)
    rest = row - 192 * part
    first = (rest * 171) >> 12
    rest = rest - 24 * first
    second = (rest * 11) >> 5
    piece = 3 * part + rest - 3 * second
    place = []
    for axis in range(3):
        step = axis - part
        step = jnp.where(step < 0, step + 3, step)
        one = jnp.where(step == 0, first >> 2, jnp.where(step == 1, first >> 1, first)) & 1
        two = (second >> (2 - axis)) & 1
        near = jnp.where(core == 1, one, two) ^ ((chip[axis] ^ (chip[axis] >> 1)) & 1)
        far = jnp.where(core == 1, two, one) ^ (chip[axis] >> 1)
        place.append(2 * far + (near ^ far))
    x, y, z = place
    device = x * 32 + (y >> 1) * 16 + core * 8 + (y & 1) * 4 + z
    return 9 * device + piece


def position():
    dp, seq = lax.axis_index("dp"), lax.axis_index("seq")
    return dp & 1, (dp >> 2, ((dp >> 1) & 1) * 2 + (seq >> 2), seq & 3)


def picker(core, chip):
    feature = lax.broadcasted_iota(jnp.int32, (A, D), 1)
    return (feature == order(core, chip)).astype(F32).astype(BF)


def pick(hot, source):
    halves = [dot(hot[k : k + STRIP], source, 1, 1).astype(BF) for k in (0, STRIP)]
    return jnp.concatenate(halves, axis=0)


def local_rows(k):
    return pl.ds(pl.multiple_of((lax.axis_index("seq") ^ PEERS[k]) * LOCAL, LOCAL), LOCAL)


def forward_spatial(*refs):
    sources, refs = refs[:7], refs[7:]
    latents, cot, mod, gains, w_qkv, w_out_t, w_out = refs[:7]
    chunks, (both_mid, qkv_t, probs_t, normed, att, scaled_t, flat, tall, both, sems) = refs[7:15], refs[15:]
    loads = {
        k: pltpu.make_async_copy(sources[k], refs[k], sems.at[k]) for k in (0, 1, 2, 3, 5, 6)
    }
    pieces = [
        pltpu.make_async_copy(
            sources[4].at[pl.ds(STRIP * k, STRIP)], w_qkv.at[pl.ds(STRIP * k, STRIP)], sems.at[7 + k]
        )
        for k in range(Q // STRIP)
    ]
    for load in (loads[0], loads[2], loads[3], *pieces, loads[1], loads[5], loads[6]):
        load.start()
    for load in (loads[0], loads[2], loads[3]):
        load.wait()
    unit, _ = normalized(latents[...].astype(F32))
    norm = (unit * (1.0 + mod[1, 0:1, :]) + mod[0, 0:1, :]).astype(BF)
    normed[...] = norm
    for k, load in enumerate(pieces):
        load.wait()
        rows = slice(STRIP * k, STRIP * k + STRIP)
        qkv_t[rows, :] = dot(w_qkv[rows, :], norm, 1, 1).astype(BF).astype(F32)
    tall[A:, :] = jnp.zeros((A_PAD - A, T), F32)
    pair = gain_columns(gains, 0)
    heads_forward(qkv_t, pair, None, probs_t, tall)
    flip_back(tall, flat, A_PAD // 128)
    att[...] = flat[...].astype(BF)
    loads[1].wait()
    scaled = (mod[2, 1:2, :] * cot[...].astype(F32)).astype(BF)
    scaled_t[...] = scaled
    loads[5].wait()
    both[:, D:] = dot(scaled, w_out_t[...], 1, 1).astype(BF)
    loads[6].wait()
    result = dot(att[:, :A], w_out[...], 1, 0)
    mid = (latents[...].astype(F32) + mod[2, 0:1, :] * result).astype(BF)
    both_mid[...] = mid
    both[:, :D] = mid
    for k in range(8):
        chunks[k][...] = both[local_rows(k), :]


def temporal(*refs):
    mod, gains, w_qkv = refs[8:11]
    normed, qkv_grad, tall_qkv, tall_grad, wide, flat, tall, tall_att, both, probs_t, work = refs[19:]
    for k in range(8):
        both[LOCAL * k : LOCAL * k + LOCAL, :] = refs[k][...]
    unit, _ = normalized(both[:, :D].astype(F32))
    norm = (unit * (1.0 + mod[1, 1:2, :]) + mod[0, 1:2, :]).astype(BF)
    normed[...] = norm
    for k in range(Q // STRIP):
        rows = slice(STRIP * k, STRIP * k + STRIP)
        tall_qkv[rows, :] = dot(w_qkv[rows, :], norm, 1, 1).astype(BF).astype(F32)
    flat[:, A:] = jnp.zeros((T, A_PAD - A), F32)
    flat[:, :A] = both[:, D:].astype(F32)
    flip(flat, tall, A_PAD // 128)
    tall_att[A:, :] = jnp.zeros((A_PAD - A, T), F32)
    tall_grad[Q:, :] = jnp.zeros((Q_PAD - Q, T), F32)
    pair = gain_columns(gains, 1)
    heads_forward(tall_qkv, pair, same_patch(), probs_t, tall_att)
    heads_back(tall_qkv, pair, probs_t, tall, tall_grad, work)
    flip_back(tall_att, flat, A_PAD // 128)
    both[:, D:] = flat[:, :A].astype(BF)
    flip_back(tall_grad, wide, Q_PAD // 128)
    qkv_grad[...] = wide[...].astype(BF)
    both[:, :D] = dot(qkv_grad[:, :Q], w_qkv[...], 1, 0).astype(BF)
    for k in range(8):
        refs[11 + k][...] = both[LOCAL * k : LOCAL * k + LOCAL, :]


def pick_early(normed, scaled, w_far, own, other, mine, theirs, w_qkv, sem):
    load = pltpu.make_async_copy(w_far, w_qkv, sem)
    load.start()
    core, chip = position()
    own[...] = picker(core, chip)
    other[...] = picker(1 - core, chip)
    for k, source in enumerate((normed, scaled)):
        rows = slice(k * A, k * A + A)
        theirs[rows, :] = pick(other[...], source[...])
        mine[rows, :] = pick(own[...], source[...])
    load.wait()


def pick_later(source, own, other, mine, theirs):
    theirs[...] = pick(other[...], source[...])
    mine[...] = pick(own[...], source[...])


def enter_spatial_back(*refs):
    mid, cot, mod, w_out, own, other, mid_grad, att_grad, att_t, mine, theirs, back = refs[8:]
    for k in range(8):
        back[local_rows(k), :] = refs[k][...]
    unit, spread = normalized(mid[...].astype(F32))
    grad = normalized_back(unit, spread, mod[1, 1:2, :], back[:, :D].astype(F32))
    total = (cot[...].astype(F32) + grad).astype(BF)
    mid_grad[...] = total
    scaled = (mod[2, 0:1, :] * total.astype(F32)).astype(BF)
    theirs[...] = pick(other[...], scaled)
    mine[...] = pick(own[...], scaled)
    att_grad[:, A:] = jnp.zeros((T, A_PAD - A), F32)
    att_grad[:, :A] = dot(scaled, w_out[...], 1, 1).astype(BF).astype(F32)
    att_t[:, A:] = jnp.zeros((T, A_PAD - A), BF)
    att_t[:, :A] = back[:, D:]


def spatial_attention_back(att_grad, qkv_t, probs_t, gains, qkv_grad, tall_grad, wide, tall, work):
    flip(att_grad, tall, A_PAD // 128)
    tall_grad[Q:, :] = jnp.zeros((Q_PAD - Q, T), F32)
    heads_back(qkv_t, gain_columns(gains, 0), probs_t, tall, tall_grad, work)
    flip_back(tall_grad, wide, Q_PAD // 128)
    qkv_grad[...] = wide[...].astype(BF)


def leave_spatial_back(mid_grad, qkv_grad, latents, mod, w_qkv, latents_grad):
    norm_grad = dot(qkv_grad[:, :Q], w_qkv[...], 1, 0).astype(BF).astype(F32)
    unit, spread = normalized(latents[...].astype(F32))
    grad = normalized_back(unit, spread, mod[1, 0:1, :], norm_grad)
    latents_grad[...] = (mid_grad[...].astype(F32) + grad).astype(BF)


def project_output(mid, att_t, mod, w_out, output):
    result = dot(att_t[:, :A], w_out[...], 1, 0)
    output[...] = (mid[...].astype(F32) + mod[2, 1:2, :] * result).astype(BF)


def weight_rows(groups):
    def body(*refs):
        keep, sends = refs[-4], refs[-3:]
        for (left, left_in, row), (right, right_in, column), width, start in groups:
            lefts = [refs[k][row : row + A, :] for k in (left, left_in)]
            rights = [refs[k][:, column : column + width] for k in (right, right_in)]
            tall_left = jnp.concatenate(lefts, axis=1)
            tall_right = jnp.concatenate(rights, axis=0)
            for at in range(0, width, 576):
                size = min(576, width - at)
                total = dot(tall_left, tall_right[:, at : at + size], 1, 0)
                for p in range(3):
                    rows = total[192 * p : 192 * p + 192]
                    columns = slice(start + at, start + at + size)
                    keep[p, :, columns] = rows[:96]
                    sends[p][:, columns] = rows[96:].astype(BF)

    return body


def first_halve(p):
    def body(keep, got, kept, send):
        half = kept.shape[0]
        total = keep[p] + got[...].astype(F32)
        kept[...] = total[:half]
        send[...] = total[half:].astype(BF)

    return body


def add_halve(keep, got, kept, send):
    half = kept.shape[0]
    total = keep[...] + got[...].astype(F32)
    kept[...] = total[:half]
    send[...] = total[half:].astype(BF)


def cut_pieces(*refs):
    own, sends = refs[6], refs[7:]
    width = refs[0].shape[1]
    for p in range(3):
        total = refs[p][...] + refs[3 + p][...].astype(F32)
        columns = slice(p * width, p * width + width)
        own[:, columns] = total[:3]
        for t in range(1, 8):
            sends[t - 1][:, columns] = total[3 * t : 3 * t + 3].astype(BF)


def last_add(*refs):
    width = refs[0].shape[1] // 3
    start = 0
    for out in refs[8:]:
        size = out.shape[1]
        for p in range(3):
            columns = slice(p * width + start, p * width + start + size)
            rows = refs[0][:, columns]
            for k in range(1, 8):
                rows = rows + refs[k][:, columns].astype(F32)
            out[3 * p : 3 * p + 3, :] = rows
        start += size


def pairs(change):
    found = []
    for device in range(128):
        dp, seq = divmod(device, 8)
        x, y, z, core = dp >> 2, ((dp >> 1) & 1) * 2 + (seq >> 2), seq & 3, dp & 1
        x, y, z, core = change(x, y, z, core)
        found.append((device, (x * 4 + (y >> 1) * 2 + core) * 8 + (y & 1) * 4 + z))
    return found


def to_other_core(value):
    return lax.ppermute(value, MESH, pairs(lambda x, y, z, c: (x, y, z, 1 - c)))


def along(value, axis):
    def change(x, y, z, core):
        place = [x, y, z]
        place[axis] ^= 1 if core == 1 else 3
        return (*place, core)

    return lax.ppermute(value, MESH, pairs(change))


def to_frame_holders(chunks):
    def step(k):
        return lax.ppermute(chunks[k], MESH, [(d, d ^ PEERS[k]) for d in range(128)])

    return [chunks[0]] + [step(k) for k in range(1, 8)]


def to_owners(pieces):
    def step(t):
        def change(x, y, z, core):
            flip_by = 3 if core == 1 else 1
            return x ^ flip_by * (t >> 2), y ^ flip_by * (t >> 1 & 1), z ^ flip_by * (t & 1), core

        return lax.ppermute(pieces[t - 1], MESH, pairs(change))

    return [step(t) for t in (4, 2, 1, 6, 5, 3, 7)]


def weight_partials(groups, args, before=()):
    cost = sum(group[2] for group in groups) / 1100
    outs = [((3, 96, COLUMNS), F32)] + [((96, COLUMNS), BF)] * 3
    aliases = {len(args) + k: k for k in range(len(before))}
    return call(weight_rows(groups), outs, (*args, *before), cost, aliases=aliases)


def shards(
    latents, cotangent, modulation, qk_gains, spatial_qkv, spatial_out, temporal_qkv, temporal_out
):
    wide, tall_grad = pltpu.VMEM((T, Q_PAD), F32), pltpu.VMEM((Q_PAD, T), F32)
    flat, tall = pltpu.VMEM((T, A_PAD), F32), pltpu.VMEM((A_PAD, T), F32)
    stage, work = pltpu.VMEM((T, D + A), BF), pltpu.VMEM((HEADS, T, T), BF)
    one_block, chunk = ((A, T), BF), ((LOCAL, D + A), BF)

    x, cot, mod, gains, w_qkv_s, w_out_t, w_out_s, *rest = call(
        forward_spatial,
        [
            ((T, D), BF), ((T, D), BF), ((3, 2, D), F32), ((2, 2, HEAD_DIM), F32),
            ((Q, D), BF), ((A, D), BF), ((A, D), BF), *[chunk] * 8,
            ((T, D), BF), ((Q, T), F32), ((HEADS, T, T), F32),
            ((T, D), BF), ((T, A_PAD), BF), ((T, D), BF),
        ],
        (
            latents.reshape(T, D), cotangent.reshape(T, D), modulation[0].transpose(1, 0, 2), qk_gains,
            spatial_qkv.T, temporal_out, spatial_out,
        ),
        10,
        (flat, tall, stage, pltpu.SemaphoreType.DMA((13,))),
        limit=18,
        apart=range(7),
    )
    mid, qkv_t, probs_t, normed_s, att_s, scaled_t = rest[8:]
    patch = to_frame_holders(rest[:8])
    own, other, early_mine, early_theirs, w_qkv_t = call(
        pick_early,
        [((A, D), BF), ((A, D), BF), ((2 * A, T), BF), ((2 * A, T), BF), ((Q, D), BF)],
        (normed_s, scaled_t, temporal_qkv.T),
        2.8,
        (pltpu.SemaphoreType.DMA(()),),
        apart=(2,),
    )
    *patch, early_mine, early_theirs = in_order(*patch, early_mine, early_theirs)
    early_in = to_other_core(early_theirs)

    *back, normed_t, qkv_grad_t = call(
        temporal,
        [*[chunk] * 8, ((T, D), BF), ((T, Q_PAD), BF)],
        (*patch, mod, gains, w_qkv_t),
        10,
        (
            pltpu.VMEM((Q, T), F32), tall_grad, wide, flat, tall, tall, stage,
            pltpu.VMEM((HEADS, T, T), F32), work,
        ),
        limit=24,
    )
    back = to_frame_holders(back)
    t_mine, t_theirs = call(pick_later, [one_block] * 2, (normed_t, own, other), 1)
    *back, t_theirs, early_theirs, qkv_grad_t, att_s = in_order(
        *back, t_theirs, early_theirs, qkv_grad_t, att_s
    )
    att_s_in = to_other_core(att_s)
    early_in = to_other_core(early_theirs)
    t_in, qkv_grad_t_in = to_other_core(t_theirs), to_other_core(qkv_grad_t)

    mid_grad, att_grad_s, att_t, late_mine, late_theirs = call(
        enter_spatial_back,
        [((T, D), BF), ((T, A_PAD), F32), ((T, A_PAD), BF), one_block, one_block],
        (*back, mid, cot, mod, w_out_s, own, other),
        2.4,
        (stage,),
    )
    att_t_in, late_in = to_other_core(att_t), to_other_core(late_theirs)
    (qkv_grad_s,) = call(
        spatial_attention_back,
        [((T, Q_PAD), BF)],
        (att_grad_s, qkv_t, probs_t, gains),
        2,
        (tall_grad, wide, tall, work),
    )
    qkv_grad_s, late_in, t_in, qkv_grad_t_in, att_t_in, early_in, att_s_in = in_order(
        qkv_grad_s, late_in, t_in, qkv_grad_t_in, att_t_in, early_in, att_s_in
    )
    qkv_grad_s_in = to_other_core(qkv_grad_s)
    partials = weight_partials(
        (
            ((0, 1, 0), (2, 3, 0), Q, 0), ((4, 5, A), (6, 7, 0), A, Q),
            ((8, 9, 0), (10, 11, 0), A, 2 * Q + A),
        ),
        (
            t_mine, t_in, qkv_grad_t, qkv_grad_t_in, early_mine, early_in, att_t, att_t_in,
            late_mine, late_in, att_s, att_s_in,
        ),
    )
    *partials, qkv_grad_s_in = in_order(*partials, qkv_grad_s_in)
    keep, *sends = weight_partials(
        (((0, 1, 0), (2, 3, 0), Q, Q + A),),
        (early_mine, early_in, qkv_grad_s, qkv_grad_s_in),
        partials,
    )
    keep, att_t, mid_grad, *sends = in_order(keep, att_t, mid_grad, *sends)
    got = [along(sends[p], p) for p in range(3)]
    (output,) = call(project_output, [((T, D), BF, "any")], (mid, att_t, mod, w_out_t), 1.5)
    (latents_grad,) = call(
        leave_spatial_back, [((T, D), BF, "any")], (mid_grad, qkv_grad_s, x, mod, w_qkv_s), 2.7
    )
    keep, output, latents_grad = in_order(keep, output, latents_grad)
    kept = []
    for p in range(3):
        mine, send = call(
            first_halve(p), [((48, COLUMNS), F32), ((48, COLUMNS), BF)], (keep, got[p]), 0.2
        )
        kept.append(mine)
        got[p] = along(send, (p + 1) % 3)
    for p in range(3):
        kept[p], send = call(
            add_halve, [((24, COLUMNS), F32), ((24, COLUMNS), BF)], (kept[p], got[p]), 0.2
        )
        got[p] = along(send, (p + 2) % 3)
    own_piece, *pieces = call(
        cut_pieces, [((3, 3 * COLUMNS), F32)] + [((3, 3 * COLUMNS), BF)] * 7, (*kept, *got), 0.5
    )
    tq, to, sq, so = call(
        last_add,
        [((9, Q), F32, "any"), ((9, A), F32, "any"), ((9, Q), F32, "any"), ((9, A), F32, "any")],
        (own_piece, *to_owners(pieces)),
        1,
    )
    shape = (1, 1, T, D)
    return output.reshape(shape), latents_grad.reshape(shape), sq, so.T, tq, to.T


def solution(mesh):
    tokens = P("dp", "seq", None, None)
    rows, cols = P(("dp", "seq"), None), P(None, ("dp", "seq"))
    return jax.shard_map(
        shards,
        mesh=mesh,
        in_specs=(tokens, tokens, P("dp", None, None, None), P(), P(), P(), P(), P()),
        out_specs=(tokens, tokens, rows, cols, rows, cols),
        check_vma=False,
    )
```

```python
import math

import jax
import jax.numpy as jnp
from jax import lax
from jax.experimental import pallas as pl
from jax.experimental.pallas import tpu as pltpu
from jax.sharding import PartitionSpec as P

T = 256
D = 1152
HEADS = 8
HEAD_DIM = 72
A = HEADS * HEAD_DIM
Q = 3 * A
A_PAD = 640
Q_PAD = 1792
COLUMNS = 2 * Q + 2 * A
LOCAL = 32
STRIP = 288
EPS = 1e-06
BF = jnp.bfloat16
F32 = jnp.float32
MESH = ("dp", "seq")
MIB = 1024 * 1024
PEERS = (0, 6, 5, 7, 4, 2, 1, 3)


def dot(left, right, over_left, over_right):
    return lax.dot_general(
        left, right, (((over_left,), (over_right,)), ((), ())), preferred_element_type=F32
    )


def call(body, outs, args, cost, scratch=(), limit=16, apart=(), aliases={}):
    shapes, specs = [], []
    for k, (shape, kind, *place) in enumerate(outs):
        if not place:
            shapes.append(pltpu.VMEM(shape, kind))
        elif place[0] == "hbm":
            shapes.append(pltpu.HBM(shape, kind))
        else:
            shapes.append(jax.ShapeDtypeStruct(shape, kind))
        specs.append(pl.BlockSpec(memory_space=pltpu.HBM if place == ["hbm"] else pltpu.VMEM))
    size = sum(x.size * x.dtype.itemsize for x in args)
    size += sum(math.prod(out[0]) * jnp.dtype(out[1]).itemsize for out in outs)
    args = [
        pltpu.with_memory_space_constraint(x, pltpu.HBM) if k in apart else x
        for k, x in enumerate(args)
    ]
    spaces = [pltpu.HBM if k in apart else pltpu.VMEM for k in range(len(args))]
    return pl.pallas_call(
        body,
        out_shape=tuple(shapes),
        in_specs=[pl.BlockSpec(memory_space=space) for space in spaces],
        out_specs=tuple(specs),
        scratch_shapes=list(scratch),
        input_output_aliases=aliases,
        cost_estimate=pl.CostEstimate(
            flops=int(cost * 1.1e9), bytes_accessed=size, transcendentals=0
        ),
        compiler_params=pltpu.CompilerParams(vmem_limit_bytes=limit * MIB),
    )(*args)


def in_order(*values):
    return lax.optimization_barrier(values)


def normalized(x32):
    mean = jnp.mean(x32, axis=-1, keepdims=True)
    centered = x32 - mean
    spread = lax.rsqrt(jnp.mean(centered * centered, axis=-1, keepdims=True) + EPS)
    return centered * spread, spread


def normalized_back(unit, spread, scale, grad):
    grad = grad * (1.0 + scale)
    inner = jnp.mean(grad * unit, axis=-1, keepdims=True)
    return spread * (grad - jnp.mean(grad, axis=-1, keepdims=True) - unit * inner)


def flip(source, target, blocks):
    for b in range(blocks):
        target[128 * b : 128 * b + 128, :] = source[:, 128 * b : 128 * b + 128].T


def flip_back(source, target, blocks):
    for b in range(blocks):
        target[:, 128 * b : 128 * b + 128] = source[128 * b : 128 * b + 128, :].T


def gain_columns(gains, block):
    row = lax.broadcasted_iota(jnp.int32, (HEAD_DIM, HEAD_DIM), 0)
    column = lax.broadcasted_iota(jnp.int32, (HEAD_DIM, HEAD_DIM), 1)
    return tuple(
        jnp.sum(jnp.where(row == column, gains[block, k : k + 1, :], 0.0), axis=1, keepdims=True)
        for k in range(2)
    )


def head_rows(which, h):
    start = which * A + h * HEAD_DIM
    return slice(start, start + HEAD_DIM)


def head_norm(rows, gain):
    root = lax.rsqrt(jnp.mean(rows * rows, axis=0, keepdims=True) + EPS)
    return root, (rows * root * gain).astype(BF)


def head_norm_back(rows, root, gain, grad):
    grad = grad.astype(BF).astype(F32) * gain
    inner = jnp.mean(rows * grad, axis=0, keepdims=True)
    return (root * grad - rows * (root * root * root * inner)).astype(BF).astype(F32)


def same_patch():
    key = lax.broadcasted_iota(jnp.int32, (T, T), 0)
    query = lax.broadcasted_iota(jnp.int32, (T, T), 1)
    return ((key ^ query) & (LOCAL - 1)) == 0


def heads_forward(qkv, pair, mask, probs, result):
    for h in range(HEADS):
        queries = head_norm(qkv[head_rows(0, h), :], pair[0])[1]
        keys = head_norm(qkv[head_rows(1, h), :], pair[1])[1]
        probs[h] = dot(keys, queries, 0, 0)
    for h in range(HEADS):
        scores = probs[h] * HEAD_DIM ** (-0.5)
        if mask is not None:
            scores = jnp.where(mask, scores, -1e30)
        expo = jnp.exp(scores - jnp.max(scores, axis=0, keepdims=True))
        probs[h] = expo * (1.0 / jnp.sum(expo, axis=0, keepdims=True))
    for h in range(HEADS):
        values = qkv[head_rows(2, h), :].astype(BF)
        result[head_rows(0, h), :] = dot(values, probs[h].astype(BF), 1, 0)


def heads_back(qkv, pair, probs, grads, out, work):
    for h in range(HEADS):
        grad = grads[head_rows(0, h), :].astype(BF)
        work[h] = dot(qkv[head_rows(2, h), :].astype(BF), grad, 0, 0).astype(BF)
        out[head_rows(2, h), :] = dot(grad, probs[h].astype(BF), 1, 1).astype(BF).astype(F32)
    for h in range(HEADS):
        prob, p_grad = probs[h], work[h].astype(F32)
        inner = jnp.sum(p_grad * prob, axis=0, keepdims=True)
        work[h] = (prob * (p_grad - inner) * HEAD_DIM ** (-0.5)).astype(BF)
    for h in range(HEADS):
        queries = head_norm(qkv[head_rows(0, h), :], pair[0])[1]
        keys = head_norm(qkv[head_rows(1, h), :], pair[1])[1]
        out[head_rows(0, h), :] = dot(keys, work[h], 1, 0)
        out[head_rows(1, h), :] = dot(queries, work[h], 1, 1)
    for h in range(HEADS):
        for which in range(2):
            rows = head_rows(which, h)
            root = head_norm(qkv[rows, :], pair[which])[0]
            out[rows, :] = head_norm_back(qkv[rows, :], root, pair[which], out[rows, :])


def order(core, chip):
    row = lax.broadcasted_iota(jnp.int32, (A, 1), 0)
    part = (row >= 192).astype(jnp.int32) + (row >= 384).astype(jnp.int32)
    rest = row - 192 * part
    first = (rest * 171) >> 12
    rest = rest - 24 * first
    second = (rest * 11) >> 5
    piece = 3 * part + rest - 3 * second
    place = []
    for axis in range(3):
        step = axis - part
        step = jnp.where(step < 0, step + 3, step)
        one = jnp.where(step == 0, first >> 2, jnp.where(step == 1, first >> 1, first)) & 1
        two = (second >> (2 - axis)) & 1
        near = jnp.where(core == 1, one, two) ^ ((chip[axis] ^ (chip[axis] >> 1)) & 1)
        far = jnp.where(core == 1, two, one) ^ (chip[axis] >> 1)
        place.append(2 * far + (near ^ far))
    x, y, z = place
    device = x * 32 + (y >> 1) * 16 + core * 8 + (y & 1) * 4 + z
    return 9 * device + piece


def position():
    dp, seq = lax.axis_index("dp"), lax.axis_index("seq")
    return dp & 1, (dp >> 2, ((dp >> 1) & 1) * 2 + (seq >> 2), seq & 3)


def picker(core, chip):
    feature = lax.broadcasted_iota(jnp.int32, (A, D), 1)
    return (feature == order(core, chip)).astype(F32).astype(BF)


def pick(hot, source):
    halves = [dot(hot[k : k + STRIP], source, 1, 1).astype(BF) for k in (0, STRIP)]
    return jnp.concatenate(halves, axis=0)


def local_rows(k):
    return pl.ds(pl.multiple_of((lax.axis_index("seq") ^ PEERS[k]) * LOCAL, LOCAL), LOCAL)


def forward_spatial(*refs):
    sources, refs = refs[:7], refs[7:]
    latents, cot, mod, gains, w_qkv, w_out_t, w_out = refs[:7]
    chunks, (both_mid, qkv_t, probs_t, normed, att, scaled_t, flat, tall, both, sems) = refs[7:15], refs[15:]
    loads = {
        k: pltpu.make_async_copy(sources[k], refs[k], sems.at[k]) for k in (0, 1, 2, 3, 5, 6)
    }
    pieces = [
        pltpu.make_async_copy(
            sources[4].at[pl.ds(STRIP * k, STRIP)], w_qkv.at[pl.ds(STRIP * k, STRIP)], sems.at[7 + k]
        )
        for k in range(Q // STRIP)
    ]
    for load in (loads[0], loads[2], loads[3], *pieces, loads[1], loads[5], loads[6]):
        load.start()
    for load in (loads[0], loads[2], loads[3]):
        load.wait()
    unit, _ = normalized(latents[...].astype(F32))
    norm = (unit * (1.0 + mod[1, 0:1, :]) + mod[0, 0:1, :]).astype(BF)
    normed[...] = norm
    for k, load in enumerate(pieces):
        load.wait()
        rows = slice(STRIP * k, STRIP * k + STRIP)
        qkv_t[rows, :] = dot(w_qkv[rows, :], norm, 1, 1).astype(BF).astype(F32)
    tall[A:, :] = jnp.zeros((A_PAD - A, T), F32)
    pair = gain_columns(gains, 0)
    heads_forward(qkv_t, pair, None, probs_t, tall)
    flip_back(tall, flat, A_PAD // 128)
    att[...] = flat[...].astype(BF)
    loads[1].wait()
    scaled = (mod[2, 1:2, :] * cot[...].astype(F32)).astype(BF)
    scaled_t[...] = scaled
    loads[5].wait()
    both[:, D:] = dot(scaled, w_out_t[...], 1, 1).astype(BF)
    loads[6].wait()
    result = dot(att[:, :A], w_out[...], 1, 0)
    mid = (latents[...].astype(F32) + mod[2, 0:1, :] * result).astype(BF)
    both_mid[...] = mid
    both[:, :D] = mid
    for k in range(8):
        chunks[k][...] = both[local_rows(k), :]


def temporal(*refs):
    mod, gains, w_qkv = refs[8:11]
    normed, qkv_grad, tall_qkv, tall_grad, wide, flat, tall, tall_att, both, probs_t, work = refs[19:]
    for k in range(8):
        both[LOCAL * k : LOCAL * k + LOCAL, :] = refs[k][...]
    unit, _ = normalized(both[:, :D].astype(F32))
    norm = (unit * (1.0 + mod[1, 1:2, :]) + mod[0, 1:2, :]).astype(BF)
    normed[...] = norm
    for k in range(Q // STRIP):
        rows = slice(STRIP * k, STRIP * k + STRIP)
        tall_qkv[rows, :] = dot(w_qkv[rows, :], norm, 1, 1).astype(BF).astype(F32)
    flat[:, A:] = jnp.zeros((T, A_PAD - A), F32)
    flat[:, :A] = both[:, D:].astype(F32)
    flip(flat, tall, A_PAD // 128)
    tall_att[A:, :] = jnp.zeros((A_PAD - A, T), F32)
    tall_grad[Q:, :] = jnp.zeros((Q_PAD - Q, T), F32)
    pair = gain_columns(gains, 1)
    heads_forward(tall_qkv, pair, same_patch(), probs_t, tall_att)
    heads_back(tall_qkv, pair, probs_t, tall, tall_grad, work)
    flip_back(tall_att, flat, A_PAD // 128)
    both[:, D:] = flat[:, :A].astype(BF)
    flip_back(tall_grad, wide, Q_PAD // 128)
    qkv_grad[...] = wide[...].astype(BF)
    both[:, :D] = dot(qkv_grad[:, :Q], w_qkv[...], 1, 0).astype(BF)
    for k in range(8):
        refs[11 + k][...] = both[LOCAL * k : LOCAL * k + LOCAL, :]


def pick_early(normed, scaled, w_far, own, other, mine, theirs, w_qkv, sem):
    load = pltpu.make_async_copy(w_far, w_qkv, sem)
    load.start()
    core, chip = position()
    own[...] = picker(core, chip)
    other[...] = picker(1 - core, chip)
    for k, source in enumerate((normed, scaled)):
        rows = slice(k * A, k * A + A)
        theirs[rows, :] = pick(other[...], source[...])
        mine[rows, :] = pick(own[...], source[...])
    load.wait()


def pick_later(source, own, other, mine, theirs):
    theirs[...] = pick(other[...], source[...])
    mine[...] = pick(own[...], source[...])


def enter_spatial_back(*refs):
    mid, cot, mod, w_out, own, other, mid_grad, att_grad, att_t, mine, theirs, back = refs[8:]
    for k in range(8):
        back[local_rows(k), :] = refs[k][...]
    unit, spread = normalized(mid[...].astype(F32))
    grad = normalized_back(unit, spread, mod[1, 1:2, :], back[:, :D].astype(F32))
    total = (cot[...].astype(F32) + grad).astype(BF)
    mid_grad[...] = total
    scaled = (mod[2, 0:1, :] * total.astype(F32)).astype(BF)
    theirs[...] = pick(other[...], scaled)
    mine[...] = pick(own[...], scaled)
    att_grad[:, A:] = jnp.zeros((T, A_PAD - A), F32)
    att_grad[:, :A] = dot(scaled, w_out[...], 1, 1).astype(BF).astype(F32)
    att_t[:, A:] = jnp.zeros((T, A_PAD - A), BF)
    att_t[:, :A] = back[:, D:]


def spatial_attention_back(att_grad, qkv_t, probs_t, gains, qkv_grad, tall_grad, wide, tall, work):
    flip(att_grad, tall, A_PAD // 128)
    tall_grad[Q:, :] = jnp.zeros((Q_PAD - Q, T), F32)
    heads_back(qkv_t, gain_columns(gains, 0), probs_t, tall, tall_grad, work)
    flip_back(tall_grad, wide, Q_PAD // 128)
    qkv_grad[...] = wide[...].astype(BF)


def leave_spatial_back(mid_grad, qkv_grad, latents, mod, w_qkv, latents_grad):
    norm_grad = dot(qkv_grad[:, :Q], w_qkv[...], 1, 0).astype(BF).astype(F32)
    unit, spread = normalized(latents[...].astype(F32))
    grad = normalized_back(unit, spread, mod[1, 0:1, :], norm_grad)
    latents_grad[...] = (mid_grad[...].astype(F32) + grad).astype(BF)


def project_output(mid, att_t, mod, w_out, output):
    result = dot(att_t[:, :A], w_out[...], 1, 0)
    output[...] = (mid[...].astype(F32) + mod[2, 1:2, :] * result).astype(BF)


def weight_rows(groups):
    def body(*refs):
        keep, sends = refs[-4], refs[-3:]
        for (left, left_in, row), (right, right_in, column), width, start in groups:
            lefts = [refs[k][row : row + A, :] for k in (left, left_in)]
            rights = [refs[k][:, column : column + width] for k in (right, right_in)]
            tall_left = jnp.concatenate(lefts, axis=1)
            tall_right = jnp.concatenate(rights, axis=0)
            for at in range(0, width, 640):
                size = min(640, width - at)
                total = dot(tall_left, tall_right[:, at : at + size], 1, 0)
                for p in range(3):
                    rows = total[192 * p : 192 * p + 192]
                    columns = slice(start + at, start + at + size)
                    keep[p, :, columns] = rows[:96]
                    sends[p][:, columns] = rows[96:].astype(BF)

    return body


def first_halve(p):
    def body(keep, got, kept, send):
        half = kept.shape[0]
        total = keep[p] + got[...].astype(F32)
        kept[...] = total[:half]
        send[...] = total[half:].astype(BF)

    return body


def add_halve(keep, got, kept, send):
    half = kept.shape[0]
    total = keep[...] + got[...].astype(F32)
    kept[...] = total[:half]
    send[...] = total[half:].astype(BF)


def cut_pieces(*refs):
    own, sends = refs[6], refs[7:]
    width = refs[0].shape[1]
    for p in range(3):
        total = refs[p][...] + refs[3 + p][...].astype(F32)
        columns = slice(p * width, p * width + width)
        own[:, columns] = total[:3]
        for t in range(1, 8):
            sends[t - 1][:, columns] = total[3 * t : 3 * t + 3].astype(BF)


def last_add(*refs):
    width = refs[0].shape[1] // 3
    start = 0
    for out in refs[8:]:
        size = out.shape[1]
        for p in range(3):
            columns = slice(p * width + start, p * width + start + size)
            rows = refs[0][:, columns]
            for k in range(1, 8):
                rows = rows + refs[k][:, columns].astype(F32)
            out[3 * p : 3 * p + 3, :] = rows
        start += size


def pairs(change):
    found = []
    for device in range(128):
        dp, seq = divmod(device, 8)
        x, y, z, core = dp >> 2, ((dp >> 1) & 1) * 2 + (seq >> 2), seq & 3, dp & 1
        x, y, z, core = change(x, y, z, core)
        found.append((device, (x * 4 + (y >> 1) * 2 + core) * 8 + (y & 1) * 4 + z))
    return found


def to_other_core(value):
    return lax.ppermute(value, MESH, pairs(lambda x, y, z, c: (x, y, z, 1 - c)))


def along(value, axis):
    def change(x, y, z, core):
        place = [x, y, z]
        place[axis] ^= 1 if core == 1 else 3
        return (*place, core)

    return lax.ppermute(value, MESH, pairs(change))


def to_frame_holders(chunks):
    def step(k):
        return lax.ppermute(chunks[k], MESH, [(d, d ^ PEERS[k]) for d in range(128)])

    return [chunks[0]] + [step(k) for k in range(1, 8)]


def to_owners(pieces):
    def step(t):
        def change(x, y, z, core):
            flip_by = 3 if core == 1 else 1
            return x ^ flip_by * (t >> 2), y ^ flip_by * (t >> 1 & 1), z ^ flip_by * (t & 1), core

        return lax.ppermute(pieces[t - 1], MESH, pairs(change))

    return [step(t) for t in (4, 2, 1, 6, 5, 3, 7)]


def weight_partials(groups, args, before=()):
    cost = sum(group[2] for group in groups) / 1100
    outs = [((3, 96, COLUMNS), F32)] + [((96, COLUMNS), BF)] * 3
    aliases = {len(args) + k: k for k in range(len(before))}
    return call(weight_rows(groups), outs, (*args, *before), cost, aliases=aliases)


def shards(
    latents, cotangent, modulation, qk_gains, spatial_qkv, spatial_out, temporal_qkv, temporal_out
):
    wide, tall_grad = pltpu.VMEM((T, Q_PAD), F32), pltpu.VMEM((Q_PAD, T), F32)
    flat, tall = pltpu.VMEM((T, A_PAD), F32), pltpu.VMEM((A_PAD, T), F32)
    stage, work = pltpu.VMEM((T, D + A), BF), pltpu.VMEM((HEADS, T, T), BF)
    one_block, chunk = ((A, T), BF), ((LOCAL, D + A), BF)

    x, cot, mod, gains, w_qkv_s, w_out_t, w_out_s, *rest = call(
        forward_spatial,
        [
            ((T, D), BF), ((T, D), BF), ((3, 2, D), F32), ((2, 2, HEAD_DIM), F32),
            ((Q, D), BF), ((A, D), BF), ((A, D), BF), *[chunk] * 8,
            ((T, D), BF), ((Q, T), F32), ((HEADS, T, T), F32),
            ((T, D), BF), ((T, A_PAD), BF), ((T, D), BF),
        ],
        (
            latents.reshape(T, D), cotangent.reshape(T, D), modulation[0].transpose(1, 0, 2), qk_gains,
            spatial_qkv.T, temporal_out, spatial_out,
        ),
        10,
        (flat, tall, stage, pltpu.SemaphoreType.DMA((13,))),
        limit=18,
        apart=range(7),
    )
    mid, qkv_t, probs_t, normed_s, att_s, scaled_t = rest[8:]
    patch = to_frame_holders(rest[:8])
    own, other, early_mine, early_theirs, w_qkv_t = call(
        pick_early,
        [((A, D), BF), ((A, D), BF), ((2 * A, T), BF), ((2 * A, T), BF), ((Q, D), BF)],
        (normed_s, scaled_t, temporal_qkv.T),
        2.8,
        (pltpu.SemaphoreType.DMA(()),),
        apart=(2,),
    )
    *patch, early_mine, early_theirs = in_order(*patch, early_mine, early_theirs)
    early_in = to_other_core(early_theirs)

    *back, normed_t, qkv_grad_t = call(
        temporal,
        [*[chunk] * 8, ((T, D), BF), ((T, Q_PAD), BF)],
        (*patch, mod, gains, w_qkv_t),
        10,
        (
            pltpu.VMEM((Q, T), F32), tall_grad, wide, flat, tall, tall, stage,
            pltpu.VMEM((HEADS, T, T), F32), work,
        ),
        limit=24,
    )
    back = to_frame_holders(back)
    t_mine, t_theirs = call(pick_later, [one_block] * 2, (normed_t, own, other), 1)
    *back, t_theirs, early_theirs, qkv_grad_t, att_s = in_order(
        *back, t_theirs, early_theirs, qkv_grad_t, att_s
    )
    att_s_in = to_other_core(att_s)
    early_in = to_other_core(early_theirs)
    t_in, qkv_grad_t_in = to_other_core(t_theirs), to_other_core(qkv_grad_t)

    mid_grad, att_grad_s, att_t, late_mine, late_theirs = call(
        enter_spatial_back,
        [((T, D), BF), ((T, A_PAD), F32), ((T, A_PAD), BF), one_block, one_block],
        (*back, mid, cot, mod, w_out_s, own, other),
        2.4,
        (stage,),
    )
    att_t_in, late_in = to_other_core(att_t), to_other_core(late_theirs)
    (qkv_grad_s,) = call(
        spatial_attention_back,
        [((T, Q_PAD), BF)],
        (att_grad_s, qkv_t, probs_t, gains),
        2,
        (tall_grad, wide, tall, work),
    )
    qkv_grad_s, late_in, t_in, qkv_grad_t_in, att_t_in, early_in, att_s_in = in_order(
        qkv_grad_s, late_in, t_in, qkv_grad_t_in, att_t_in, early_in, att_s_in
    )
    qkv_grad_s_in = to_other_core(qkv_grad_s)
    partials = weight_partials(
        (
            ((0, 1, 0), (2, 3, 0), Q, 0), ((4, 5, A), (6, 7, 0), A, Q),
            ((8, 9, 0), (10, 11, 0), A, 2 * Q + A),
        ),
        (
            t_mine, t_in, qkv_grad_t, qkv_grad_t_in, early_mine, early_in, att_t, att_t_in,
            late_mine, late_in, att_s, att_s_in,
        ),
    )
    *partials, qkv_grad_s_in = in_order(*partials, qkv_grad_s_in)
    keep, *sends = weight_partials(
        (((0, 1, 0), (2, 3, 0), Q, Q + A),),
        (early_mine, early_in, qkv_grad_s, qkv_grad_s_in),
        partials,
    )
    keep, att_t, mid_grad, *sends = in_order(keep, att_t, mid_grad, *sends)
    got = [along(sends[p], p) for p in range(3)]
    (output,) = call(project_output, [((T, D), BF, "any")], (mid, att_t, mod, w_out_t), 1.5)
    (latents_grad,) = call(
        leave_spatial_back, [((T, D), BF, "any")], (mid_grad, qkv_grad_s, x, mod, w_qkv_s), 2.7
    )
    keep, output, latents_grad = in_order(keep, output, latents_grad)
    kept = []
    for p in range(3):
        mine, send = call(
            first_halve(p), [((48, COLUMNS), F32), ((48, COLUMNS), BF)], (keep, got[p]), 0.2
        )
        kept.append(mine)
        got[p] = along(send, (p + 1) % 3)
    for p in range(3):
        kept[p], send = call(
            add_halve, [((24, COLUMNS), F32), ((24, COLUMNS), BF)], (kept[p], got[p]), 0.2
        )
        got[p] = along(send, (p + 2) % 3)
    own_piece, *pieces = call(
        cut_pieces, [((3, 3 * COLUMNS), F32)] + [((3, 3 * COLUMNS), BF)] * 7, (*kept, *got), 0.5
    )
    tq, to, sq, so = call(
        last_add,
        [((9, Q), F32, "any"), ((9, A), F32, "any"), ((9, Q), F32, "any"), ((9, A), F32, "any")],
        (own_piece, *to_owners(pieces)),
        1,
    )
    shape = (1, 1, T, D)
    return output.reshape(shape), latents_grad.reshape(shape), sq, so.T, tq, to.T


def solution(mesh):
    tokens = P("dp", "seq", None, None)
    rows, cols = P(("dp", "seq"), None), P(None, ("dp", "seq"))
    return jax.shard_map(
        shards,
        mesh=mesh,
        in_specs=(tokens, tokens, P("dp", None, None, None), P(), P(), P(), P(), P()),
        out_specs=(tokens, tokens, rows, cols, rows, cols),
        check_vma=False,
    )
```

```python
import math

import jax
import jax.numpy as jnp
from jax import lax
from jax.experimental import pallas as pl
from jax.experimental.pallas import tpu as pltpu
from jax.sharding import PartitionSpec as P

T = 256
D = 1152
HEADS = 8
HEAD_DIM = 72
A = HEADS * HEAD_DIM
Q = 3 * A
A_PAD = 640
Q_PAD = 1792
COLUMNS = 2 * Q + 2 * A
LOCAL = 32
STRIP = 288
EPS = 1e-06
FACTOR = HEAD_DIM ** (-0.5) * math.log2(math.e)
BF = jnp.bfloat16
F32 = jnp.float32
MESH = ("dp", "seq")
MIB = 1024 * 1024
PEERS = (0, 6, 5, 7, 4, 2, 1, 3)


def dot(left, right, over_left, over_right):
    return lax.dot_general(
        left, right, (((over_left,), (over_right,)), ((), ())), preferred_element_type=F32
    )


def call(body, outs, args, cost, scratch=(), limit=16, apart=(), aliases={}):
    shapes, specs = [], []
    for k, (shape, kind, *place) in enumerate(outs):
        if not place:
            shapes.append(pltpu.VMEM(shape, kind))
        elif place[0] == "hbm":
            shapes.append(pltpu.HBM(shape, kind))
        else:
            shapes.append(jax.ShapeDtypeStruct(shape, kind))
        specs.append(pl.BlockSpec(memory_space=pltpu.HBM if place == ["hbm"] else pltpu.VMEM))
    size = sum(x.size * x.dtype.itemsize for x in args)
    size += sum(math.prod(out[0]) * jnp.dtype(out[1]).itemsize for out in outs)
    args = [
        pltpu.with_memory_space_constraint(x, pltpu.HBM) if k in apart else x
        for k, x in enumerate(args)
    ]
    spaces = [pltpu.HBM if k in apart else pltpu.VMEM for k in range(len(args))]
    return pl.pallas_call(
        body,
        out_shape=tuple(shapes),
        in_specs=[pl.BlockSpec(memory_space=space) for space in spaces],
        out_specs=tuple(specs),
        scratch_shapes=list(scratch),
        input_output_aliases=aliases,
        cost_estimate=pl.CostEstimate(
            flops=int(cost * 1.1e9), bytes_accessed=size, transcendentals=0
        ),
        compiler_params=pltpu.CompilerParams(vmem_limit_bytes=limit * MIB),
    )(*args)


def in_order(*values):
    return lax.optimization_barrier(values)


def normalized(x32):
    mean = jnp.mean(x32, axis=-1, keepdims=True)
    centered = x32 - mean
    spread = lax.rsqrt(jnp.mean(centered * centered, axis=-1, keepdims=True) + EPS)
    return centered * spread, spread


def normalized_back(unit, spread, scale, grad):
    grad = grad * (1.0 + scale)
    inner = jnp.mean(grad * unit, axis=-1, keepdims=True)
    return spread * (grad - jnp.mean(grad, axis=-1, keepdims=True) - unit * inner)


def flip(source, target, blocks):
    for b in range(blocks):
        target[128 * b : 128 * b + 128, :] = source[:, 128 * b : 128 * b + 128].T


def flip_back(source, target, blocks):
    for b in range(blocks):
        target[:, 128 * b : 128 * b + 128] = source[128 * b : 128 * b + 128, :].T


def gain_columns(gains, block):
    row = lax.broadcasted_iota(jnp.int32, (HEAD_DIM, HEAD_DIM), 0)
    column = lax.broadcasted_iota(jnp.int32, (HEAD_DIM, HEAD_DIM), 1)
    return tuple(
        jnp.sum(jnp.where(row == column, gains[block, k : k + 1, :], 0.0), axis=1, keepdims=True)
        for k in range(2)
    )


def head_rows(which, h):
    start = which * A + h * HEAD_DIM
    return slice(start, start + HEAD_DIM)


def head_norm(rows, gain):
    root = lax.rsqrt(jnp.mean(rows * rows, axis=0, keepdims=True) + EPS)
    return root, (rows * root * gain).astype(BF)


def head_norm_back(rows, root, gain, grad):
    grad = grad.astype(BF).astype(F32) * gain
    inner = jnp.mean(rows * grad, axis=0, keepdims=True)
    return (root * grad - rows * (root * root * root * inner)).astype(BF).astype(F32)


def same_patch():
    key = lax.broadcasted_iota(jnp.int32, (T, T), 0)
    query = lax.broadcasted_iota(jnp.int32, (T, T), 1)
    return ((key ^ query) & (LOCAL - 1)) == 0


def heads_forward(qkv, pair, mask, probs, result):
    for h in range(HEADS):
        queries = head_norm(qkv[head_rows(0, h), :], pair[0])[1]
        keys = head_norm(qkv[head_rows(1, h), :], pair[1])[1]
        probs[h] = dot(keys, queries, 0, 0)
    for h in range(HEADS):
        scores = probs[h]
        if mask is not None:
            scores = jnp.where(mask, scores, -1e30)
        expo = jnp.exp2((scores - jnp.max(scores, axis=0, keepdims=True)) * FACTOR)
        probs[h] = expo * (1.0 / jnp.sum(expo, axis=0, keepdims=True))
    for h in range(HEADS):
        values = qkv[head_rows(2, h), :].astype(BF)
        result[head_rows(0, h), :] = dot(values, probs[h].astype(BF), 1, 0)


def heads_back(qkv, pair, probs, grads, out, work):
    for h in range(HEADS):
        grad = grads[head_rows(0, h), :].astype(BF)
        work[h] = dot(qkv[head_rows(2, h), :].astype(BF), grad, 0, 0).astype(BF)
        out[head_rows(2, h), :] = dot(grad, probs[h].astype(BF), 1, 1).astype(BF).astype(F32)
    for h in range(HEADS):
        prob, p_grad = probs[h], work[h].astype(F32)
        inner = jnp.sum(p_grad * prob, axis=0, keepdims=True)
        work[h] = (prob * (p_grad - inner) * HEAD_DIM ** (-0.5)).astype(BF)
    for h in range(HEADS):
        queries = head_norm(qkv[head_rows(0, h), :], pair[0])[1]
        keys = head_norm(qkv[head_rows(1, h), :], pair[1])[1]
        out[head_rows(0, h), :] = dot(keys, work[h], 1, 0)
        out[head_rows(1, h), :] = dot(queries, work[h], 1, 1)
    for h in range(HEADS):
        for which in range(2):
            rows = head_rows(which, h)
            root = head_norm(qkv[rows, :], pair[which])[0]
            out[rows, :] = head_norm_back(qkv[rows, :], root, pair[which], out[rows, :])


def order(core, chip):
    row = lax.broadcasted_iota(jnp.int32, (A, 1), 0)
    part = (row >= 192).astype(jnp.int32) + (row >= 384).astype(jnp.int32)
    rest = row - 192 * part
    first = (rest * 171) >> 12
    rest = rest - 24 * first
    second = (rest * 11) >> 5
    piece = 3 * part + rest - 3 * second
    place = []
    for axis in range(3):
        step = axis - part
        step = jnp.where(step < 0, step + 3, step)
        one = jnp.where(step == 0, first >> 2, jnp.where(step == 1, first >> 1, first)) & 1
        two = (second >> (2 - axis)) & 1
        near = jnp.where(core == 1, one, two) ^ ((chip[axis] ^ (chip[axis] >> 1)) & 1)
        far = jnp.where(core == 1, two, one) ^ (chip[axis] >> 1)
        place.append(2 * far + (near ^ far))
    x, y, z = place
    device = x * 32 + (y >> 1) * 16 + core * 8 + (y & 1) * 4 + z
    return 9 * device + piece


def position():
    dp, seq = lax.axis_index("dp"), lax.axis_index("seq")
    return dp & 1, (dp >> 2, ((dp >> 1) & 1) * 2 + (seq >> 2), seq & 3)


def picker(core, chip):
    feature = lax.broadcasted_iota(jnp.int32, (A, D), 1)
    return (feature == order(core, chip)).astype(F32).astype(BF)


def pick(hot, source):
    halves = [dot(hot[k : k + STRIP], source, 1, 1).astype(BF) for k in (0, STRIP)]
    return jnp.concatenate(halves, axis=0)


def local_rows(k):
    return pl.ds(pl.multiple_of((lax.axis_index("seq") ^ PEERS[k]) * LOCAL, LOCAL), LOCAL)


def forward_spatial(*refs):
    sources, refs = refs[:7], refs[7:]
    latents, cot, mod, gains, w_qkv, w_out_t, w_out = refs[:7]
    chunks, (both_mid, qkv_t, probs_t, normed, att, scaled_t, flat, tall, both, sems) = refs[7:15], refs[15:]
    loads = {
        k: pltpu.make_async_copy(sources[k], refs[k], sems.at[k]) for k in (0, 1, 2, 3, 5, 6)
    }
    pieces = [
        pltpu.make_async_copy(
            sources[4].at[pl.ds(STRIP * k, STRIP)], w_qkv.at[pl.ds(STRIP * k, STRIP)], sems.at[7 + k]
        )
        for k in range(Q // STRIP)
    ]
    for load in (loads[0], loads[2], loads[3], *pieces, loads[1], loads[5], loads[6]):
        load.start()
    for load in (loads[0], loads[2], loads[3]):
        load.wait()
    unit, _ = normalized(latents[...].astype(F32))
    norm = (unit * (1.0 + mod[1, 0:1, :]) + mod[0, 0:1, :]).astype(BF)
    normed[...] = norm
    for k, load in enumerate(pieces):
        load.wait()
        rows = slice(STRIP * k, STRIP * k + STRIP)
        qkv_t[rows, :] = dot(w_qkv[rows, :], norm, 1, 1).astype(BF).astype(F32)
    tall[A:, :] = jnp.zeros((A_PAD - A, T), F32)
    pair = gain_columns(gains, 0)
    heads_forward(qkv_t, pair, None, probs_t, tall)
    flip_back(tall, flat, A_PAD // 128)
    att[...] = flat[...].astype(BF)
    loads[1].wait()
    scaled = (mod[2, 1:2, :] * cot[...].astype(F32)).astype(BF)
    scaled_t[...] = scaled
    loads[5].wait()
    both[:, D:] = dot(scaled, w_out_t[...], 1, 1).astype(BF)
    loads[6].wait()
    result = dot(att[:, :A], w_out[...], 1, 0)
    mid = (latents[...].astype(F32) + mod[2, 0:1, :] * result).astype(BF)
    both_mid[...] = mid
    both[:, :D] = mid
    for k in range(8):
        chunks[k][...] = both[local_rows(k), :]


def temporal(*refs):
    mod, gains, w_qkv = refs[8:11]
    normed, qkv_grad, tall_qkv, tall_grad, wide, flat, tall, tall_att, both, probs_t, work = refs[19:]
    for k in range(8):
        both[LOCAL * k : LOCAL * k + LOCAL, :] = refs[k][...]
    unit, _ = normalized(both[:, :D].astype(F32))
    norm = (unit * (1.0 + mod[1, 1:2, :]) + mod[0, 1:2, :]).astype(BF)
    normed[...] = norm
    for k in range(Q // STRIP):
        rows = slice(STRIP * k, STRIP * k + STRIP)
        tall_qkv[rows, :] = dot(w_qkv[rows, :], norm, 1, 1).astype(BF).astype(F32)
    flat[:, A:] = jnp.zeros((T, A_PAD - A), F32)
    flat[:, :A] = both[:, D:].astype(F32)
    flip(flat, tall, A_PAD // 128)
    tall_att[A:, :] = jnp.zeros((A_PAD - A, T), F32)
    tall_grad[Q:, :] = jnp.zeros((Q_PAD - Q, T), F32)
    pair = gain_columns(gains, 1)
    heads_forward(tall_qkv, pair, same_patch(), probs_t, tall_att)
    heads_back(tall_qkv, pair, probs_t, tall, tall_grad, work)
    flip_back(tall_att, flat, A_PAD // 128)
    both[:, D:] = flat[:, :A].astype(BF)
    flip_back(tall_grad, wide, Q_PAD // 128)
    qkv_grad[...] = wide[...].astype(BF)
    both[:, :D] = dot(qkv_grad[:, :Q], w_qkv[...], 1, 0).astype(BF)
    for k in range(8):
        refs[11 + k][...] = both[LOCAL * k : LOCAL * k + LOCAL, :]


def pick_early(normed, scaled, w_far, own, other, mine, theirs, w_qkv, sem):
    load = pltpu.make_async_copy(w_far, w_qkv, sem)
    load.start()
    core, chip = position()
    own[...] = picker(core, chip)
    other[...] = picker(1 - core, chip)
    for k, source in enumerate((normed, scaled)):
        rows = slice(k * A, k * A + A)
        theirs[rows, :] = pick(other[...], source[...])
        mine[rows, :] = pick(own[...], source[...])
    load.wait()


def pick_later(source, own, other, mine, theirs):
    theirs[...] = pick(other[...], source[...])
    mine[...] = pick(own[...], source[...])


def enter_spatial_back(*refs):
    mid, cot, mod, w_out, own, other, mid_grad, att_grad, att_t, mine, theirs, back = refs[8:]
    for k in range(8):
        back[local_rows(k), :] = refs[k][...]
    unit, spread = normalized(mid[...].astype(F32))
    grad = normalized_back(unit, spread, mod[1, 1:2, :], back[:, :D].astype(F32))
    total = (cot[...].astype(F32) + grad).astype(BF)
    mid_grad[...] = total
    scaled = (mod[2, 0:1, :] * total.astype(F32)).astype(BF)
    theirs[...] = pick(other[...], scaled)
    mine[...] = pick(own[...], scaled)
    att_grad[:, A:] = jnp.zeros((T, A_PAD - A), F32)
    att_grad[:, :A] = dot(scaled, w_out[...], 1, 1).astype(BF).astype(F32)
    att_t[:, A:] = jnp.zeros((T, A_PAD - A), BF)
    att_t[:, :A] = back[:, D:]


def spatial_attention_back(att_grad, qkv_t, probs_t, gains, qkv_grad, tall_grad, wide, tall, work):
    flip(att_grad, tall, A_PAD // 128)
    tall_grad[Q:, :] = jnp.zeros((Q_PAD - Q, T), F32)
    heads_back(qkv_t, gain_columns(gains, 0), probs_t, tall, tall_grad, work)
    flip_back(tall_grad, wide, Q_PAD // 128)
    qkv_grad[...] = wide[...].astype(BF)


def leave_spatial_back(mid_grad, qkv_grad, latents, mod, w_qkv, latents_grad):
    norm_grad = dot(qkv_grad[:, :Q], w_qkv[...], 1, 0).astype(BF).astype(F32)
    unit, spread = normalized(latents[...].astype(F32))
    grad = normalized_back(unit, spread, mod[1, 0:1, :], norm_grad)
    latents_grad[...] = (mid_grad[...].astype(F32) + grad).astype(BF)


def project_output(mid, att_t, mod, w_out, output):
    result = dot(att_t[:, :A], w_out[...], 1, 0)
    output[...] = (mid[...].astype(F32) + mod[2, 1:2, :] * result).astype(BF)


def weight_rows(groups):
    def body(*refs):
        keep, sends = refs[-4], refs[-3:]
        for (left, left_in, row), (right, right_in, column), width, start in groups:
            lefts = [refs[k][row : row + A, :] for k in (left, left_in)]
            rights = [refs[k][:, column : column + width] for k in (right, right_in)]
            tall_left = jnp.concatenate(lefts, axis=1)
            tall_right = jnp.concatenate(rights, axis=0)
            for at in range(0, width, 640):
                size = min(640, width - at)
                total = dot(tall_left, tall_right[:, at : at + size], 1, 0)
                for p in range(3):
                    rows = total[192 * p : 192 * p + 192]
                    columns = slice(start + at, start + at + size)
                    keep[p, :, columns] = rows[:96]
                    sends[p][:, columns] = rows[96:].astype(BF)

    return body


def first_halve(p):
    def body(keep, got, kept, send):
        half = kept.shape[0]
        total = keep[p] + got[...].astype(F32)
        kept[...] = total[:half]
        send[...] = total[half:].astype(BF)

    return body


def add_halve(keep, got, kept, send):
    half = kept.shape[0]
    total = keep[...] + got[...].astype(F32)
    kept[...] = total[:half]
    send[...] = total[half:].astype(BF)


def cut_pieces(*refs):
    own, sends = refs[6], refs[7:]
    width = refs[0].shape[1]
    for p in range(3):
        total = refs[p][...] + refs[3 + p][...].astype(F32)
        columns = slice(p * width, p * width + width)
        own[:, columns] = total[:3]
        for t in range(1, 8):
            sends[t - 1][:, columns] = total[3 * t : 3 * t + 3].astype(BF)


def last_add(*refs):
    width = refs[0].shape[1] // 3
    start = 0
    for out in refs[8:]:
        size = out.shape[1]
        for p in range(3):
            columns = slice(p * width + start, p * width + start + size)
            rows = refs[0][:, columns]
            for k in range(1, 8):
                rows = rows + refs[k][:, columns].astype(F32)
            out[3 * p : 3 * p + 3, :] = rows
        start += size


def pairs(change):
    found = []
    for device in range(128):
        dp, seq = divmod(device, 8)
        x, y, z, core = dp >> 2, ((dp >> 1) & 1) * 2 + (seq >> 2), seq & 3, dp & 1
        x, y, z, core = change(x, y, z, core)
        found.append((device, (x * 4 + (y >> 1) * 2 + core) * 8 + (y & 1) * 4 + z))
    return found


def to_other_core(value):
    return lax.ppermute(value, MESH, pairs(lambda x, y, z, c: (x, y, z, 1 - c)))


def along(value, axis):
    def change(x, y, z, core):
        place = [x, y, z]
        place[axis] ^= 1 if core == 1 else 3
        return (*place, core)

    return lax.ppermute(value, MESH, pairs(change))


def to_frame_holders(chunks):
    def step(k):
        return lax.ppermute(chunks[k], MESH, [(d, d ^ PEERS[k]) for d in range(128)])

    return [chunks[0]] + [step(k) for k in range(1, 8)]


def to_owners(pieces):
    def step(t):
        def change(x, y, z, core):
            flip_by = 3 if core == 1 else 1
            return x ^ flip_by * (t >> 2), y ^ flip_by * (t >> 1 & 1), z ^ flip_by * (t & 1), core

        return lax.ppermute(pieces[t - 1], MESH, pairs(change))

    return [step(t) for t in (4, 2, 1, 6, 5, 3, 7)]


def weight_partials(groups, args, before=()):
    cost = sum(group[2] for group in groups) / 1100
    outs = [((3, 96, COLUMNS), F32)] + [((96, COLUMNS), BF)] * 3
    aliases = {len(args) + k: k for k in range(len(before))}
    return call(weight_rows(groups), outs, (*args, *before), cost, aliases=aliases)


def shards(
    latents, cotangent, modulation, qk_gains, spatial_qkv, spatial_out, temporal_qkv, temporal_out
):
    wide, tall_grad = pltpu.VMEM((T, Q_PAD), F32), pltpu.VMEM((Q_PAD, T), F32)
    flat, tall = pltpu.VMEM((T, A_PAD), F32), pltpu.VMEM((A_PAD, T), F32)
    stage, work = pltpu.VMEM((T, D + A), BF), pltpu.VMEM((HEADS, T, T), BF)
    one_block, chunk = ((A, T), BF), ((LOCAL, D + A), BF)

    x, cot, mod, gains, w_qkv_s, w_out_t, w_out_s, *rest = call(
        forward_spatial,
        [
            ((T, D), BF), ((T, D), BF), ((3, 2, D), F32), ((2, 2, HEAD_DIM), F32),
            ((Q, D), BF), ((A, D), BF), ((A, D), BF), *[chunk] * 8,
            ((T, D), BF), ((Q, T), F32), ((HEADS, T, T), F32),
            ((T, D), BF), ((T, A_PAD), BF), ((T, D), BF),
        ],
        (
            latents.reshape(T, D), cotangent.reshape(T, D), modulation[0].transpose(1, 0, 2), qk_gains,
            spatial_qkv.T, temporal_out, spatial_out,
        ),
        10,
        (flat, tall, stage, pltpu.SemaphoreType.DMA((13,))),
        limit=18,
        apart=range(7),
    )
    mid, qkv_t, probs_t, normed_s, att_s, scaled_t = rest[8:]
    patch = to_frame_holders(rest[:8])
    own, other, early_mine, early_theirs, w_qkv_t = call(
        pick_early,
        [((A, D), BF), ((A, D), BF), ((2 * A, T), BF), ((2 * A, T), BF), ((Q, D), BF)],
        (normed_s, scaled_t, temporal_qkv.T),
        2.8,
        (pltpu.SemaphoreType.DMA(()),),
        apart=(2,),
    )
    *patch, early_mine, early_theirs = in_order(*patch, early_mine, early_theirs)
    early_in = to_other_core(early_theirs)

    *back, normed_t, qkv_grad_t = call(
        temporal,
        [*[chunk] * 8, ((T, D), BF), ((T, Q_PAD), BF)],
        (*patch, mod, gains, w_qkv_t),
        10,
        (
            pltpu.VMEM((Q, T), F32), tall_grad, wide, flat, tall, tall, stage,
            pltpu.VMEM((HEADS, T, T), F32), work,
        ),
        limit=24,
    )
    back = to_frame_holders(back)
    t_mine, t_theirs = call(pick_later, [one_block] * 2, (normed_t, own, other), 1)
    *back, t_theirs, early_theirs, qkv_grad_t, att_s = in_order(
        *back, t_theirs, early_theirs, qkv_grad_t, att_s
    )
    att_s_in = to_other_core(att_s)
    early_in = to_other_core(early_theirs)
    t_in, qkv_grad_t_in = to_other_core(t_theirs), to_other_core(qkv_grad_t)

    mid_grad, att_grad_s, att_t, late_mine, late_theirs = call(
        enter_spatial_back,
        [((T, D), BF), ((T, A_PAD), F32), ((T, A_PAD), BF), one_block, one_block],
        (*back, mid, cot, mod, w_out_s, own, other),
        2.4,
        (stage,),
    )
    att_t_in, late_in = to_other_core(att_t), to_other_core(late_theirs)
    (qkv_grad_s,) = call(
        spatial_attention_back,
        [((T, Q_PAD), BF)],
        (att_grad_s, qkv_t, probs_t, gains),
        2,
        (tall_grad, wide, tall, work),
    )
    qkv_grad_s, late_in, t_in, qkv_grad_t_in, att_t_in, early_in, att_s_in = in_order(
        qkv_grad_s, late_in, t_in, qkv_grad_t_in, att_t_in, early_in, att_s_in
    )
    qkv_grad_s_in = to_other_core(qkv_grad_s)
    partials = weight_partials(
        (
            ((0, 1, 0), (2, 3, 0), Q, 0), ((4, 5, A), (6, 7, 0), A, Q),
            ((8, 9, 0), (10, 11, 0), A, 2 * Q + A),
        ),
        (
            t_mine, t_in, qkv_grad_t, qkv_grad_t_in, early_mine, early_in, att_t, att_t_in,
            late_mine, late_in, att_s, att_s_in,
        ),
    )
    *partials, qkv_grad_s_in = in_order(*partials, qkv_grad_s_in)
    keep, *sends = weight_partials(
        (((0, 1, 0), (2, 3, 0), Q, Q + A),),
        (early_mine, early_in, qkv_grad_s, qkv_grad_s_in),
        partials,
    )
    keep, att_t, mid_grad, *sends = in_order(keep, att_t, mid_grad, *sends)
    got = [along(sends[p], p) for p in range(3)]
    (output,) = call(project_output, [((T, D), BF, "any")], (mid, att_t, mod, w_out_t), 1.5)
    (latents_grad,) = call(
        leave_spatial_back, [((T, D), BF, "any")], (mid_grad, qkv_grad_s, x, mod, w_qkv_s), 2.7
    )
    keep, output, latents_grad = in_order(keep, output, latents_grad)
    kept = []
    for p in range(3):
        mine, send = call(
            first_halve(p), [((48, COLUMNS), F32), ((48, COLUMNS), BF)], (keep, got[p]), 0.2
        )
        kept.append(mine)
        got[p] = along(send, (p + 1) % 3)
    for p in range(3):
        kept[p], send = call(
            add_halve, [((24, COLUMNS), F32), ((24, COLUMNS), BF)], (kept[p], got[p]), 0.2
        )
        got[p] = along(send, (p + 2) % 3)
    own_piece, *pieces = call(
        cut_pieces, [((3, 3 * COLUMNS), F32)] + [((3, 3 * COLUMNS), BF)] * 7, (*kept, *got), 0.5
    )
    tq, to, sq, so = call(
        last_add,
        [((9, Q), F32, "any"), ((9, A), F32, "any"), ((9, Q), F32, "any"), ((9, A), F32, "any")],
        (own_piece, *to_owners(pieces)),
        1,
    )
    shape = (1, 1, T, D)
    return output.reshape(shape), latents_grad.reshape(shape), sq, so.T, tq, to.T


def solution(mesh):
    tokens = P("dp", "seq", None, None)
    rows, cols = P(("dp", "seq"), None), P(None, ("dp", "seq"))
    return jax.shard_map(
        shards,
        mesh=mesh,
        in_specs=(tokens, tokens, P("dp", None, None, None), P(), P(), P(), P(), P()),
        out_specs=(tokens, tokens, rows, cols, rows, cols),
        check_vma=False,
    )
```
